32 devices in a mesh: lat: 8 (over y, x, core), lon: 4 (over z).
Axes of the slice: x: 2, y: 2, z: 4, core: 2. Of those that a mesh axis runs over, the one named last changes fastest.
Arguments:
- state: bfloat16 [64, 64, 1080], P(None, 'lat', 'lon'), may hold values from -6 to 6
- land_sea: int32 [64, 1080], P('lat', 'lon'), may hold values 0 or 1
- cotangent: bfloat16 [64, 64, 1080], P(None, 'lat', 'lon'), may hold values from -6 to 6
- kernel: float32 [64, 7, 7], replicated, may hold values from -0.875 to 0.875
- conv_bias: float32 [64], replicated, may hold values from -4 to 4
- ln_gain: float32 [64], replicated, may hold values from 0.1 to 1.9
- ln_bias: float32 [64], replicated, may hold values from -3 to 3
- w_expand: bfloat16 [64, 256], replicated, may hold values from -0.75 to 0.75
- b_expand: float32 [256], replicated, may hold values from -3 to 3
- w_project: bfloat16 [256, 64], replicated, may hold values from -0.375 to 0.375
Outputs:
- state_grad: bfloat16 [64, 64, 1080], P(None, 'lat', 'lon')
- kernel_grad: float32 [64, 7, 7], replicated
- conv_bias_grad: float32 [64], replicated
- gain_grad: float32 [64], replicated
- ln_bias_grad: float32 [64], replicated
- expand_grad: float32 [64, 256], replicated
- b_expand_grad: float32 [256], replicated
- project_grad: float32 [256, 64], replicated
- b_project_grad: float32 [64], replicated
The draws below stay inside these ranges and needn't reach their ends.
Inputs may be any that keep to these rules, and one draw needn't show every extreme that they name: `land_sea`: 1 marks an ocean cell, 0 a land cell.
All inputs are finite; a program needn't handle non-finite values. No bound on the sum of `land_sea` on one device may be relied on, other than what follows from the above.
Results may differ from the reference program's by a relative error of at most 0.0064.
Values may be sent and summed in bfloat16 or wider, within the bound.
No kernel may reach another device: no remote copies, remote signals or barrier semaphores. Data moves between devices by JAX's collectives and lax.ppermute only.
A program may use at most 64 MiB of HBM per device.

```python
import math
import jax
import jax.numpy as jnp
from jax import lax

CHAN = 64
EXPAND = 256
TAPS = 7
ROWS_DEV = 8
NLAT = 64
NLON = 1080
N_LAT = 8


def plant(array, key, least, top_value):
    shape = array.shape
    index_at = [jax.random.randint(jax.random.fold_in(key, axis), (), 0, shape[axis]) for axis in range(len(shape))]
    array = array.at[tuple(index_at)].set(least)
    longest = shape.index(max(shape))
    index_at[longest] = (index_at[longest] + 1) % shape[longest]
    return array.at[tuple(index_at)].set(top_value)


def steps_of(key, dims, cuts, smallest, top_value):
    def one(dim, shards_of):
        steps = jax.random.uniform(jax.random.fold_in(jax.random.fold_in(key, 6), dim), (shards_of,), jnp.float32, smallest / len(cuts), top_value / len(cuts))
        return jnp.repeat(jnp.exp(steps), dims[dim] // shards_of).reshape((-1,) + (1,) * (len(dims) - dim - 1))

    gain = one(*cuts[0])
    for cut in cuts[1:]:
        gain = gain * one(*cut)
    return gain


def gaussian(own_key, shape, deviation, reach, cuts=(), kind=jnp.bfloat16):
    loudness = steps_of(own_key, shape, cuts, -0.22, 0.18) if cuts else 1.0
    result = jax.random.normal(own_key, shape, jnp.float32) * deviation * loudness
    return jnp.minimum(jnp.maximum(result, -reach), reach).astype(kind)


def setup_inputs(seed: int = 0) -> dict:
    splits = jax.random.split(jax.random.key(seed), 11)
    state = gaussian(splits[0], (CHAN, NLAT, NLON), 1.0, 6.0, ((1, 8), (2, 4)))
    land_sea = plant((jax.random.randint(splits[1], (NLAT, NLON), 0, 4) < 3).astype(jnp.int32), jax.random.fold_in(splits[1], 1), 0, 1)
    cotangent = gaussian(splits[2], (CHAN, NLAT, NLON), 1.0, 6.0, ((1, 8), (2, 4)))
    kernel = gaussian(splits[3], (CHAN, TAPS, TAPS), (TAPS * TAPS) ** -0.5, 0.875, (), jnp.float32)
    conv_bias = gaussian(splits[4], (CHAN,), 1.0, 4.0, (), jnp.float32)
    ln_gain = jnp.clip(1.0 + 0.18 * jax.random.normal(splits[5], (CHAN,), jnp.float32), 0.1, 1.9)
    ln_bias = gaussian(splits[6], (CHAN,), 0.5, 3.0, (), jnp.float32)
    w_expand = gaussian(splits[7], (CHAN, EXPAND), CHAN ** -0.5, 0.75)
    b_expand = gaussian(splits[8], (EXPAND,), 0.5, 3.0, (), jnp.float32)
    w_project = gaussian(splits[9], (EXPAND, CHAN), EXPAND ** -0.5, 0.375)
    return {"state": state, "land_sea": land_sea, "cotangent": cotangent, "kernel": kernel, "conv_bias": conv_bias, "ln_gain": ln_gain, "ln_bias": ln_bias, "w_expand": w_expand, "b_expand": b_expand, "w_project": w_project}


ln_eps = 1e-06
root_half = 0.7071067811865476
inv_root_tau = 0.3989422804014327
highest = lax.Precision.HIGHEST

def gelu_value(values):
    return 0.5 * values * (1.0 + lax.erf(values * root_half))

def gelu_slope(values):
    return 0.5 * (1.0 + lax.erf(values * root_half)) + values * jnp.exp(-0.5 * values * values) * inv_root_tau

def pad_field(field):
    padded = jnp.pad(field, ((0, 0), (3, 3), (0, 0)))
    return jnp.concatenate([padded[:, :, -3:], padded, padded[:, :, :3]], axis=2)

def depthwise(padded, kernel, n_rows, n_cols):
    total = jnp.zeros((padded.shape[0], n_rows, n_cols), jnp.float32)
    for row_tap in range(TAPS):
        for col_tap in range(TAPS):
            total = total + kernel[:, row_tap, col_tap][:, None, None] * padded[:, row_tap:row_tap + n_rows, col_tap:col_tap + n_cols]
    return total

def transpose_conv(padded, kernel, n_rows, n_cols):
    total = jnp.zeros((padded.shape[0], n_rows, n_cols), jnp.float32)
    for row_tap in range(TAPS):
        for col_tap in range(TAPS):
            total = total + kernel[:, row_tap, col_tap][:, None, None] * padded[:, 6 - row_tap:6 - row_tap + n_rows, 6 - col_tap:6 - col_tap + n_cols]
    return total

def kernel_sums(dconv, padded, n_rows, n_cols):
    taps = []
    for row_tap in range(TAPS):
        for col_tap in range(TAPS):
            taps.append(lax.optimization_barrier(jnp.sum(dconv * padded[:, row_tap:row_tap + n_rows, col_tap:col_tap + n_cols], axis=(1, 2))))
    return jnp.stack(taps, axis=1).reshape(dconv.shape[0], TAPS, TAPS)

def cell_terms(conv_out, wet_cot, ln_gain, ln_bias, w_expand, b_expand, w_project):
    center = conv_out - lax.optimization_barrier(jnp.mean(conv_out, axis=0, keepdims=True))
    rstd = lax.rsqrt(lax.optimization_barrier(jnp.mean(center * center, axis=0, keepdims=True)) + ln_eps)
    normed = center * rstd
    zed = (normed * ln_gain[:, None, None] + ln_bias[:, None, None]).astype(jnp.bfloat16)
    pre = jnp.einsum('chw,ce->ehw', zed.astype(jnp.float32), w_expand.astype(jnp.float32), precision=highest) + b_expand[:, None, None]
    act = gelu_value(pre).astype(jnp.bfloat16)
    dact = jnp.einsum('chw,ec->ehw', wet_cot.astype(jnp.float32), w_project.astype(jnp.float32), precision=highest)
    dhid = (dact * gelu_slope(pre)).astype(jnp.bfloat16)
    dzed = jnp.einsum('ehw,ce->chw', dhid.astype(jnp.float32), w_expand.astype(jnp.float32), precision=highest)
    dnorm = dzed * ln_gain[:, None, None]
    dconv = rstd * (dnorm - lax.optimization_barrier(jnp.mean(dnorm, axis=0, keepdims=True)) - normed * lax.optimization_barrier(jnp.mean(dnorm * normed, axis=0, keepdims=True)))
    return (zed, act, dhid, normed, dzed, dconv)

def pointwise_sums(zed, act, dhid, normed, dzed, wet_cot):
    expand_sum = jnp.einsum('chw,ehw->ce', zed.astype(jnp.float32), dhid.astype(jnp.float32), precision=highest)
    b_expand_sum = lax.optimization_barrier(jnp.sum(dhid.astype(jnp.float32), axis=(1, 2)))
    project_sum = jnp.einsum('ehw,chw->ec', act.astype(jnp.float32), wet_cot.astype(jnp.float32), precision=highest)
    b_project_sum = lax.optimization_barrier(jnp.sum(wet_cot.astype(jnp.float32), axis=(1, 2)))
    gain_sum = lax.optimization_barrier(jnp.sum(dzed * normed, axis=(1, 2)))
    bias_sum = lax.optimization_barrier(jnp.sum(dzed, axis=(1, 2)))
    return (expand_sum, b_expand_sum, project_sum, b_project_sum, gain_sum, bias_sum)

def reference(state, land_sea, cotangent, kernel, conv_bias, ln_gain, ln_bias, w_expand, b_expand, w_project):
    state_pad = pad_field(state.astype(jnp.float32))
    conv_out = depthwise(state_pad, kernel, NLAT, NLON) + conv_bias[:, None, None]
    wet_cot = cotangent * land_sea[None].astype(cotangent.dtype)
    conv_blocks = conv_out.reshape(CHAN, N_LAT, ROWS_DEV, NLON).transpose(1, 0, 2, 3)
    cot_blocks = wet_cot.reshape(CHAN, N_LAT, ROWS_DEV, NLON).transpose(1, 0, 2, 3)

    def step(carry, pieces):
        terms = cell_terms(pieces[0], pieces[1], ln_gain, ln_bias, w_expand, b_expand, w_project)
        sums = pointwise_sums(terms[0], terms[1], terms[2], terms[3], terms[4], pieces[1])
        return (tuple((old + new for old, new in zip(carry, sums))), terms[5])
    start = (jnp.zeros((CHAN, EXPAND), jnp.float32), jnp.zeros((EXPAND,), jnp.float32), jnp.zeros((EXPAND, CHAN), jnp.float32), jnp.zeros((CHAN,), jnp.float32), jnp.zeros((CHAN,), jnp.float32), jnp.zeros((CHAN,), jnp.float32))
    sums, dconv_blocks = lax.scan(step, start, (conv_blocks, cot_blocks))
    dconv = dconv_blocks.transpose(1, 0, 2, 3).reshape(CHAN, NLAT, NLON)
    scale = 1.0 / math.sqrt(NLAT * NLON)
    kernel_grad = kernel_sums(dconv, state_pad, NLAT, NLON) * scale
    conv_bias_grad = lax.optimization_barrier(jnp.sum(dconv, axis=(1, 2))) * scale
    state_grad = (cotangent.astype(jnp.float32) + transpose_conv(pad_field(dconv), kernel, NLAT, NLON)).astype(jnp.bfloat16)
    return (state_grad, kernel_grad, conv_bias_grad, sums[4] * scale, sums[5] * scale, sums[0] * scale, sums[1] * scale, sums[2] * scale, sums[3] * scale)
```

```python
import math

import jax
import jax.numpy as jnp
from jax import lax
from jax.sharding import PartitionSpec as P

TAPS = 7


ln_eps = 1e-06
root_half = 0.7071067811865476
inv_root_tau = 0.3989422804014327


def extended(shard, sides, width):
    for axis, dim in sides:
        size, length = (lax.axis_size(axis), shard.shape[dim])
        wraps = axis == "lon"
        up = [(i, (i + 1) % size) for i in range(size if wraps else size - 1)]
        down = [(j, i) for i, j in up]
        last = lax.slice_in_dim(shard, length - width, length, axis=dim)
        first = lax.slice_in_dim(shard, 0, width, axis=dim)
        if wraps:
            shape = (last.shape[1] * last.shape[2], last.shape[0])
            last = last.transpose(1, 2, 0).reshape(shape)
            first = first.transpose(1, 2, 0).reshape(shape)
        before = lax.ppermute(last, axis, up)
        after = lax.ppermute(first, axis, down)
        if wraps:
            back = (shard.shape[1], width, shard.shape[0])
            before = before.reshape(back).transpose(2, 0, 1)
            after = after.reshape(back).transpose(2, 0, 1)
        shard = jnp.concatenate([before, shard, after], axis=dim)
    return shard


def summed(values):
    flat = jnp.concatenate([v.reshape(-1) for v in values])
    count = flat.shape[0]
    rows = -(-count // 1024) * 8
    flat = jnp.pad(flat, (0, rows * 128 - count)).reshape(rows, 128)
    for axis in ("lat", "lon"):
        size = lax.axis_size(axis)
        if size & (size - 1):
            flat = lax.psum(flat, axis)
            continue
        bit = 1
        while bit < size:
            flat = flat + lax.ppermute(flat, axis, [(i, i ^ bit) for i in range(size)])
            bit *= 2
    flat, out, start = flat.reshape(-1), [], 0
    for v in values:
        out.append(flat[start : start + v.size].reshape(v.shape))
        start += v.size
    return out


def gelu_value(values):
    return 0.5 * values * (1.0 + lax.erf(values * root_half))


def gelu_slope(values):
    return (
        0.5 * (1.0 + lax.erf(values * root_half))
        + values * jnp.exp(-0.5 * values * values) * inv_root_tau
    )


def extend_in(field, rim_width):
    return extended(field, (("lon", 2), ("lat", 1)), rim_width)


def extend_back(field):
    return extended(field, (("lon", 2), ("lat", 1)), 3)


def depthwise(padded, kernel, n_rows, n_cols):
    total = jnp.zeros((padded.shape[0], n_rows, n_cols), jnp.float32)
    for row_tap in range(TAPS):
        for col_tap in range(TAPS):
            total = (
                total
                + kernel[:, row_tap, col_tap][:, None, None]
                * padded[:, row_tap : row_tap + n_rows, col_tap : col_tap + n_cols]
            )
    return total


def transpose_conv(padded, kernel, n_rows, n_cols):
    total = jnp.zeros((padded.shape[0], n_rows, n_cols), jnp.float32)
    for row_tap in range(TAPS):
        for col_tap in range(TAPS):
            total = (
                total
                + kernel[:, row_tap, col_tap][:, None, None]
                * padded[:, 6 - row_tap : 6 - row_tap + n_rows, 6 - col_tap : 6 - col_tap + n_cols]
            )
    return total


def kernel_sums(dconv, padded, n_rows, n_cols):
    taps = []
    for row_tap in range(TAPS):
        for col_tap in range(TAPS):
            taps.append(
                jnp.sum(
                    dconv * padded[:, row_tap : row_tap + n_rows, col_tap : col_tap + n_cols],
                    axis=(1, 2),
                )
            )
    return jnp.stack(taps, axis=1).reshape(dconv.shape[0], TAPS, TAPS)


def cell_terms(conv_out, wet_cot, ln_gain, ln_bias, w_expand, b_expand, w_project):
    center = conv_out - jnp.mean(conv_out, axis=0, keepdims=True)
    rstd = lax.rsqrt(jnp.mean(center * center, axis=0, keepdims=True) + ln_eps)
    normed = center * rstd
    zed = (normed * ln_gain[:, None, None] + ln_bias[:, None, None]).astype(jnp.bfloat16)
    pre = (
        jnp.einsum("chw,ce->ehw", zed, w_expand, preferred_element_type=jnp.float32)
        + b_expand[:, None, None]
    )
    act = gelu_value(pre).astype(jnp.bfloat16)
    dact = jnp.einsum("chw,ec->ehw", wet_cot, w_project, preferred_element_type=jnp.float32)
    dhid = (dact * gelu_slope(pre)).astype(jnp.bfloat16)
    dzed = jnp.einsum("ehw,ce->chw", dhid, w_expand, preferred_element_type=jnp.float32)
    dnorm = dzed * ln_gain[:, None, None]
    dconv = rstd * (
        dnorm
        - jnp.mean(dnorm, axis=0, keepdims=True)
        - normed * jnp.mean(dnorm * normed, axis=0, keepdims=True)
    )
    return (zed, act, dhid, normed, dzed, dconv)


def pointwise_sums(zed, act, dhid, normed, dzed, wet_cot):
    expand_sum = jnp.einsum("chw,ehw->ce", zed, dhid, preferred_element_type=jnp.float32)
    b_expand_sum = jnp.sum(dhid.astype(jnp.float32), axis=(1, 2))
    project_sum = jnp.einsum("ehw,chw->ec", act, wet_cot, preferred_element_type=jnp.float32)
    b_project_sum = jnp.sum(wet_cot.astype(jnp.float32), axis=(1, 2))
    gain_sum = jnp.sum(dzed * normed, axis=(1, 2))
    bias_sum = jnp.sum(dzed, axis=(1, 2))
    return (expand_sum, b_expand_sum, project_sum, b_project_sum, gain_sum, bias_sum)


def body(
    state, land_sea, cotangent, kernel, conv_bias, ln_gain, ln_bias, w_expand, b_expand, w_project
):
    n_chan, n_rows, n_cols = state.shape
    wet_cot = cotangent * land_sea[None].astype(jnp.bfloat16)
    state_ext = extend_in(state, 3).astype(jnp.float32)
    conv_out = depthwise(state_ext, kernel, n_rows, n_cols) + conv_bias[:, None, None]
    terms = cell_terms(conv_out, wet_cot, ln_gain, ln_bias, w_expand, b_expand, w_project)
    point = pointwise_sums(terms[0], terms[1], terms[2], terms[3], terms[4], wet_cot)
    dconv = terms[5]
    dconv_ext = extend_back(dconv)
    tap_sum = kernel_sums(dconv, state_ext, n_rows, n_cols)
    bias_conv_sum = jnp.sum(dconv, axis=(1, 2))
    totals = summed(
        (point[0], point[1], point[2], point[3], point[4], point[5], tap_sum, bias_conv_sum)
    )
    state_grad = (
        cotangent.astype(jnp.float32) + transpose_conv(dconv_ext, kernel, n_rows, n_cols)
    ).astype(jnp.bfloat16)
    scale = 1.0 / math.sqrt(n_rows * lax.axis_size("lat") * n_cols * lax.axis_size("lon"))
    return (
        state_grad,
        totals[6] * scale,
        totals[7] * scale,
        totals[4] * scale,
        totals[5] * scale,
        totals[0] * scale,
        totals[1] * scale,
        totals[2] * scale,
        totals[3] * scale,
    )


def solution(mesh):
    in_specs = (
        P(None, "lat", "lon"),
        P("lat", "lon"),
        P(None, "lat", "lon"),
        P(),
        P(),
        P(),
        P(),
        P(),
        P(),
        P(),
    )
    out_specs = (P(None, "lat", "lon"), P(), P(), P(), P(), P(), P(), P(), P())
    return jax.shard_map(body, mesh=mesh, in_specs=in_specs, out_specs=out_specs, check_vma=False)
```

```python
import functools
import math

import jax
import jax.numpy as jnp
from jax import lax
from jax.experimental import pallas as pl
from jax.experimental.pallas import tpu as pltpu
from jax.sharding import PartitionSpec as P

TAPS = 7
RIM = 3
STEP = 16

ln_eps = 1e-06
root_half = 0.7071067811865476
inv_root_tau = 0.3989422804014327
f32 = jnp.float32
bf16 = jnp.bfloat16


def neighbours(axis, wraps):
    size = lax.axis_size(axis)
    up = [(i, (i + 1) % size) for i in range(size if wraps else size - 1)]
    return up, [(j, i) for i, j in up]


def rim_columns(first, last):
    up, down = neighbours("lon", True)
    return lax.ppermute(last, "lon", up), lax.ppermute(first, "lon", down)


def rim_rows(first, last):
    up, down = neighbours("lat", False)
    return lax.ppermute(last, "lat", up), lax.ppermute(first, "lat", down)


def pack(field):
    half = field.shape[0] // 2
    return jnp.concatenate([field[:half], field[half:]], axis=2)


def unpack(field):
    chan = field.shape[2] // 2
    return jnp.concatenate([field[:, :, :chan], field[:, :, chan:]], axis=0)


def pack_extended(ext, half):
    return jnp.concatenate([ext[: half + 2 * RIM], ext[half:]], axis=2)


def summed(flat):
    for axis in ("lat", "lon"):
        size = lax.axis_size(axis)
        if size & (size - 1):
            flat = lax.psum(flat, axis)
            continue
        bit = 1
        while bit < size:
            flat = flat + lax.ppermute(flat, axis, [(i, i ^ bit) for i in range(size)])
            bit *= 2
    return flat


def fill_taps(taps_ref, wide_ref, flip):
    count, chan = taps_ref.shape
    for tap in range(count):
        row = taps_ref[count - 1 - tap if flip else tap, :].reshape(1, chan)
        wide_ref[tap] = jnp.broadcast_to(jnp.concatenate([row, row], axis=1), (8, 2 * chan))


def convolve(ext_ref, wide_ref, store, half, columns):
    def trip(t, carry):
        start = pl.multiple_of(t * STEP, STEP)
        tiles = STEP // 8
        total = [[None] * tiles for _ in range(half)]
        for row in range(half + 2 * RIM):
            for b in range(TAPS):
                piece = [ext_ref[row, pl.ds(start + b + 8 * s, 8), :] for s in range(tiles)]
                for i in range(half):
                    a = row - i
                    if 0 <= a < TAPS:
                        weight = wide_ref[a * TAPS + b]
                        for s in range(tiles):
                            term = weight * piece[s]
                            total[i][s] = term if total[i][s] is None else total[i][s] + term
        for i in range(half):
            store(i, start, jnp.concatenate(total[i], axis=0))
        return carry

    lax.fori_loop(0, columns // STEP, trip, 0)


def group_mean(values, ones):
    high = values.astype(bf16)
    low = (values - high.astype(f32)).astype(bf16)
    return jnp.dot(high, ones, preferred_element_type=f32) + jnp.dot(
        low, ones, preferred_element_type=f32
    )


def block_kernel(
    ext_ref, wet_ref, taps_ref, vec_ref, w1_ref, b1_ref, w2_ref,
    dconv_ref, sums_ref,
    ext32, wide, conv, w1, w2, expand, project, hidden, small,
):
    half, columns, lanes = wet_ref.shape
    chan = lanes // 2
    wide_e = w1_ref.shape[1]
    ext32[...] = ext_ref[...].astype(f32)
    fill_taps(taps_ref, wide, False)
    w1[...] = jnp.zeros_like(w1)
    w2[...] = jnp.zeros_like(w2)
    w1[:chan, :wide_e] = w1_ref[...]
    w1[chan:, wide_e:] = w1_ref[...]
    w2[:chan, :wide_e] = w2_ref[...]
    w2[chan:, wide_e:] = w2_ref[...]
    expand[...] = jnp.zeros_like(expand)
    project[...] = jnp.zeros_like(project)
    hidden[...] = jnp.zeros_like(hidden)
    small[...] = jnp.zeros_like(small)

    def put(i, start, value):
        conv[i, pl.ds(start, STEP), :] = value

    convolve(ext32, wide, put, half, columns)

    row_half = lax.broadcasted_iota(jnp.int32, (lanes, lanes), 0) >= chan
    col_half = lax.broadcasted_iota(jnp.int32, (lanes, lanes), 1) >= chan
    ones = jnp.where(row_half == col_half, 1.0 / chan, 0.0).astype(bf16)
    conv_bias, gain, bias = vec_ref[0:1, :], vec_ref[1:2, :], vec_ref[2:3, :]
    hidden_bias = b1_ref[...]

    def row_step(i, carry):
        out = conv[i] + conv_bias
        wet = wet_ref[i]
        center = out - group_mean(out, ones)
        rstd = lax.rsqrt(group_mean(center * center, ones) + ln_eps)
        normed = center * rstd
        zed = (normed * gain + bias).astype(bf16)
        pre = jnp.dot(zed, w1[...], preferred_element_type=f32) + hidden_bias
        dact = jnp.dot(wet, w2[...], preferred_element_type=f32)
        phi = 0.5 + 0.5 * lax.erf(pre * root_half)
        act = (pre * phi).astype(bf16)
        dhid = (dact * (phi + pre * (jnp.exp(-0.5 * pre * pre) * inv_root_tau))).astype(bf16)
        dzed = lax.dot_general(dhid, w1[...], (((1,), (1,)), ((), ())), preferred_element_type=f32)
        rows_first = (((0,), (0,)), ((), ()))
        expand[...] += lax.dot_general(zed, dhid, rows_first, preferred_element_type=f32)
        project[...] += lax.dot_general(wet, act, rows_first, preferred_element_type=f32)
        dnorm = dzed * gain
        mean1 = group_mean(dnorm, ones)
        mean2 = group_mean(dnorm * normed, ones)
        dconv = rstd * (dnorm - mean1 - normed * mean2)
        dconv_ref[i] = dconv
        hidden[...] += jnp.sum(dhid.astype(f32).reshape(columns // 8, 8, -1), axis=0)
        parts = (wet.astype(f32), dzed * normed, dzed, dconv)
        for k, part in enumerate(parts):
            small[k] += jnp.sum(part.reshape(columns // 8, 8, lanes), axis=0)
        return carry

    lax.fori_loop(0, half, row_step, 0)

    at = 0
    for block in (expand, project):
        total = block[:chan, :wide_e] + block[chan:, wide_e:]
        for k in range(wide_e // lanes):
            sums_ref[at : at + chan, :] = total[:, k * lanes : (k + 1) * lanes]
            at += chan
    total = jnp.sum(hidden[...], axis=0, keepdims=True)
    total = total[:, :wide_e] + total[:, wide_e:]
    rows = [total[:, k * lanes : (k + 1) * lanes] for k in range(wide_e // lanes)]
    rows += [jnp.sum(small[k], axis=0, keepdims=True) for k in range(4)]
    spare = sums_ref.shape[0] - at - len(rows)
    rows.append(jnp.zeros((spare, lanes), f32))
    sums_ref[at:, :] = jnp.concatenate(rows, axis=0)


def tap_kernel(ext_ref, dconv_ref, sums_ref, all_ref, ext32):
    half, columns, lanes = dconv_ref.shape
    ext32[...] = ext_ref[...].astype(f32)
    first = sums_ref.shape[0]
    all_ref[:first, :] = sums_ref[...]

    def trip(t, carry):
        start = pl.multiple_of(t * 8, 8)
        total = list(carry)
        grads = [dconv_ref[i, pl.ds(start, 8), :] for i in range(half)]
        for row in range(half + 2 * RIM):
            for b in range(TAPS):
                piece = ext32[row, pl.ds(start + b, 8), :]
                for i in range(half):
                    a = row - i
                    if 0 <= a < TAPS:
                        total[a * TAPS + b] = total[a * TAPS + b] + grads[i] * piece
        return tuple(total)

    zero = jnp.zeros((8, lanes), f32)
    total = lax.fori_loop(0, columns // 8, trip, (zero,) * (TAPS * TAPS))
    for a in range(TAPS):
        rows = [jnp.sum(total[a * TAPS + b], axis=0, keepdims=True) for b in range(TAPS)]
        rows.append(jnp.zeros((1, lanes), f32))
        all_ref[first + 8 * a : first + 8 * a + 8, :] = jnp.concatenate(rows, axis=0)


def back_kernel(ext_ref, cot_ref, taps_ref, out_ref, wide):
    half, columns, lanes = out_ref.shape
    fill_taps(taps_ref, wide, True)

    def put(i, start, value):
        cot = cot_ref[i, pl.ds(start, STEP), :].astype(f32)
        out_ref[i, pl.ds(start, STEP), :] = (cot + value).astype(bf16)

    convolve(ext_ref, wide, put, half, columns)


def call(kernel, out_shape, scratch, flops, *args):
    vmem = pl.BlockSpec(memory_space=pltpu.VMEM)
    many = isinstance(out_shape, (list, tuple))
    return pl.pallas_call(
        kernel,
        out_shape=out_shape,
        in_specs=[vmem] * len(args),
        out_specs=[vmem] * len(out_shape) if many else vmem,
        scratch_shapes=scratch,
        cost_estimate=pl.CostEstimate(flops=flops, bytes_accessed=1 << 20, transcendentals=0),
        compiler_params=pltpu.CompilerParams(vmem_limit_bytes=40 << 20),
    )(*args)


def body(
    state, land_sea, cotangent, kernel, conv_bias, ln_gain, ln_bias, w_expand, b_expand, w_project
):
    n_chan, n_rows, n_cols = state.shape
    n_wide = w_expand.shape[1]
    half = n_rows // 2
    lanes = 2 * n_chan
    columns = -(-n_cols // STEP) * STEP
    spare = columns - n_cols
    padded = -(-(columns + 2 * RIM) // 8) * 8
    taps = kernel.transpose(1, 2, 0).reshape(TAPS * TAPS, n_chan)
    twice = lambda v: jnp.concatenate([v, v])
    vectors = jnp.stack([twice(conv_bias), twice(ln_gain), twice(ln_bias)])

    field = state.transpose(1, 2, 0)
    flat = (n_rows * RIM, n_chan)
    left, right = rim_columns(field[:, :RIM].reshape(flat), field[:, -RIM:].reshape(flat))
    piece = (n_rows, RIM, n_chan)
    field = jnp.concatenate([left.reshape(piece), field, right.reshape(piece)], axis=1)
    top, bottom = rim_rows(field[:RIM], field[-RIM:])
    field = jnp.concatenate([top, field, bottom], axis=0)
    field = jnp.pad(field, ((0, 0), (0, padded - field.shape[1]), (0, 0)))
    ext = pack_extended(field, half)

    cot = pack(jnp.pad(cotangent.transpose(1, 2, 0), ((0, 0), (0, spare), (0, 0))))
    mask = jnp.pad(land_sea, ((0, 0), (0, spare))).astype(bf16)
    wet = cot * pack(jnp.broadcast_to(mask[:, :, None], (n_rows, columns, n_chan)))

    cells = n_rows * n_cols
    dconv, sums = call(
        block_kernel,
        [
            jax.ShapeDtypeStruct((half, columns, lanes), f32),
            jax.ShapeDtypeStruct((2 * n_chan * n_wide // lanes + 8, lanes), f32),
        ],
        [
            pltpu.VMEM(ext.shape, f32),
            pltpu.VMEM((TAPS * TAPS, 8, lanes), f32),
            pltpu.VMEM((half, columns, lanes), f32),
            pltpu.VMEM((lanes, 2 * n_wide), bf16),
            pltpu.VMEM((lanes, 2 * n_wide), bf16),
            pltpu.VMEM((lanes, 2 * n_wide), f32),
            pltpu.VMEM((lanes, 2 * n_wide), f32),
            pltpu.VMEM((8, 2 * n_wide), f32),
            pltpu.VMEM((4, 8, lanes), f32),
        ],
        cells * n_chan * n_wide * 10,
        ext, wet, taps, vectors, w_expand, twice(b_expand).reshape(1, -1), w_project.T,
    )

    first, last = rim_columns(dconv[:, :RIM], dconv[:, n_cols - RIM : n_cols])
    sums = call(
        tap_kernel,
        jax.ShapeDtypeStruct((sums.shape[0] + 8 * TAPS, lanes), f32),
        [pltpu.VMEM(ext.shape, f32)],
        cells * n_chan * TAPS * TAPS * 2,
        ext, dconv, sums,
    )
    grads = unpack(jnp.concatenate([first, dconv[:, :n_cols], last], axis=1))
    top, bottom = rim_rows(grads[:RIM], grads[-RIM:])
    grads = jnp.concatenate([top, grads, bottom], axis=0)
    grads = jnp.pad(grads, ((0, 0), (0, padded - grads.shape[1]), (0, 0)))
    state_grad = call(
        back_kernel,
        jax.ShapeDtypeStruct((half, columns, lanes), bf16),
        [pltpu.VMEM((TAPS * TAPS, 8, lanes), f32)],
        cells * n_chan * TAPS * TAPS * 2,
        pack_extended(grads, half), cot, taps,
    )
    state_grad = unpack(state_grad)[:, :n_cols].transpose(2, 0, 1)

    scale = 1.0 / math.sqrt(cells * lax.axis_size("lat") * lax.axis_size("lon"))
    sums = summed(sums) * scale
    wide_blocks = n_wide // lanes

    def wide(at):
        blocks = [sums[at + k * n_chan : at + (k + 1) * n_chan] for k in range(wide_blocks)]
        return jnp.concatenate(blocks, axis=1)

    at = 2 * wide_blocks * n_chan
    hidden = sums[at : at + wide_blocks].reshape(-1)
    narrow = sums[at + wide_blocks : at + wide_blocks + 4]
    narrow = narrow[:, :n_chan] + narrow[:, n_chan:]
    tap_sum = sums[-8 * TAPS :].reshape(TAPS, 8, lanes)[:, :TAPS]
    tap_sum = tap_sum[:, :, :n_chan] + tap_sum[:, :, n_chan:]
    return (
        state_grad,
        tap_sum.transpose(2, 0, 1),
        narrow[3],
        narrow[1],
        narrow[2],
        wide(0),
        hidden,
        wide(wide_blocks * n_chan).T,
        narrow[0],
    )


def solution(mesh):
    in_specs = (
        P(None, "lat", "lon"),
        P("lat", "lon"),
        P(None, "lat", "lon"),
        P(),
        P(),
        P(),
        P(),
        P(),
        P(),
        P(),
    )
    out_specs = (P(None, "lat", "lon"), P(), P(), P(), P(), P(), P(), P(), P())
    return jax.shard_map(body, mesh=mesh, in_specs=in_specs, out_specs=out_specs, check_vma=False)
```

```python
import functools
import math

import jax
import jax.numpy as jnp
from jax import lax
from jax.experimental import pallas as pl
from jax.experimental.pallas import tpu as pltpu
from jax.sharding import PartitionSpec as P

TAPS = 7
RIM = 3
STEP = 16

ln_eps = 1e-06
root_half = 0.7071067811865476
inv_root_tau = 0.3989422804014327
f32 = jnp.float32
bf16 = jnp.bfloat16


def neighbours(axis, wraps):
    size = lax.axis_size(axis)
    up = [(i, (i + 1) % size) for i in range(size if wraps else size - 1)]
    return up, [(j, i) for i, j in up]


def pairs(axis, bit):
    return [(i, i ^ bit) for i in range(lax.axis_size(axis))]


def ring_pairs(axis):
    size = lax.axis_size(axis)
    return [(i, (i + 1) % size if i % 2 else (i - 1) % size) for i in range(size)]


def higher_bits(axis):
    size, bit, bits = lax.axis_size(axis), 4, []
    while bit < size:
        bits.append(bit)
        bit *= 2
    return bits


def pack(field):
    half = field.shape[0] // 2
    return jnp.concatenate([field[:half], field[half:]], axis=2)


def unpack(field):
    chan = field.shape[2] // 2
    return jnp.concatenate([field[:, :, :chan], field[:, :, chan:]], axis=0)


def dense(rows):
    half = rows.shape[1] // 2
    return jnp.concatenate([rows[:, :half], rows[:, half:]], axis=2)


def swap(value):
    return pltpu.roll(value, value.shape[-1] // 2, value.ndim - 1)


def assemble(ext_ref, mid_ref, top, bottom):
    half, columns, lanes = mid_ref.shape
    first = lax.broadcasted_iota(jnp.int32, (columns, lanes), 1) < lanes // 2
    for k in range(RIM):
        above, below = top(k), bottom(k)
        above = jnp.concatenate([above, swap(above)], axis=0)
        below = jnp.concatenate([swap(below), below], axis=0)
        upper = swap(mid_ref[half - RIM + k].astype(f32))
        lower = swap(mid_ref[k].astype(f32))
        ext_ref[k] = jnp.where(first, above, upper)
        ext_ref[half + RIM + k] = jnp.where(first, lower, below)
    for i in range(half):
        ext_ref[RIM + i] = mid_ref[i].astype(f32)


def split(value):
    high = value.astype(bf16)
    return high, (value - high.astype(f32)).astype(bf16)


def added(mine_ref, other_ref, coarse, fine):
    at = coarse + fine
    big = mine_ref[:coarse].astype(f32) + other_ref[:coarse].astype(f32)
    one = mine_ref[coarse:at].astype(f32) + mine_ref[at : at + fine].astype(f32)
    two = other_ref[coarse:at].astype(f32) + other_ref[at : at + fine].astype(f32)
    return big, one + two


def put_sums(out_ref, big, small):
    coarse, fine = big.shape[0], small.shape[0]
    high, low = split(small)
    out_ref[:coarse] = big.astype(bf16)
    out_ref[coarse : coarse + fine] = high
    out_ref[coarse + fine : coarse + 2 * fine] = low


def fill_taps(taps_ref, wide_ref, flip):
    count, chan = taps_ref.shape
    for tap in range(count):
        row = taps_ref[count - 1 - tap if flip else tap, :].reshape(1, chan)
        wide_ref[tap] = jnp.broadcast_to(jnp.concatenate([row, row], axis=1), (8, 2 * chan))


def convolve(ext_ref, wide_ref, store, half, columns):
    def trip(t, carry):
        start = pl.multiple_of(t * STEP, STEP)
        tiles = STEP // 8
        total = [[None] * tiles for _ in range(half)]
        for row in range(half + 2 * RIM):
            for b in range(TAPS):
                piece = [ext_ref[row, pl.ds(start + b + 8 * s, 8), :] for s in range(tiles)]
                for i in range(half):
                    a = row - i
                    if 0 <= a < TAPS:
                        weight = wide_ref[a * TAPS + b]
                        for s in range(tiles):
                            term = weight * piece[s]
                            total[i][s] = term if total[i][s] is None else total[i][s] + term
        for i in range(half):
            store(i, start, jnp.concatenate(total[i], axis=0))
        return carry

    lax.fori_loop(0, columns // STEP, trip, 0)


def group_mean(values, ones):
    high = values.astype(bf16)
    low = (values - high.astype(f32)).astype(bf16)
    return jnp.dot(high, ones, preferred_element_type=f32) + jnp.dot(
        low, ones, preferred_element_type=f32
    )


def block_kernel(
    n_cols, odd_ref, mid_ref, top_ref, bottom_ref, wet_ref, taps_ref, vec_ref, w1_ref, b1_ref, w2_ref,
    dconv_ref, send_ref, later_ref,
    ext32, wide, conv, w1, w2, expand, project, hidden, small,
):
    half, columns, lanes = wet_ref.shape
    chan = lanes // 2
    wide_e = w1_ref.shape[1]
    cells = later_ref.shape[0] // half
    assemble(ext32, mid_ref, lambda k: top_ref[k].astype(f32), lambda k: bottom_ref[k].astype(f32))
    fill_taps(taps_ref, wide, False)
    w1[...] = jnp.zeros_like(w1)
    w2[...] = jnp.zeros_like(w2)
    w1[:chan, :wide_e] = w1_ref[...]
    w1[chan:, wide_e:] = w1_ref[...]
    w2[:chan, :wide_e] = w2_ref[...]
    w2[chan:, wide_e:] = w2_ref[...]
    expand[...] = jnp.zeros_like(expand)
    project[...] = jnp.zeros_like(project)
    hidden[...] = jnp.zeros_like(hidden)
    small[...] = jnp.zeros_like(small)
    dconv_ref[...] = jnp.zeros_like(dconv_ref)

    def put(i, start, value):
        conv[i, pl.ds(start, STEP), :] = value

    convolve(ext32, wide, put, half, columns)

    row_half = lax.broadcasted_iota(jnp.int32, (lanes, lanes), 0) >= chan
    col_half = lax.broadcasted_iota(jnp.int32, (lanes, lanes), 1) >= chan
    ones = jnp.where(row_half == col_half, 1.0 / chan, 0.0).astype(bf16)
    conv_bias, gain, bias = vec_ref[0:1, :], vec_ref[1:2, :], vec_ref[2:3, :]
    hidden_bias = b1_ref[...]

    def row_step(i, carry):
        out = conv[i] + conv_bias
        wet = wet_ref[i]
        center = out - group_mean(out, ones)
        rstd = lax.rsqrt(group_mean(center * center, ones) + ln_eps)
        normed = center * rstd
        zed = (normed * gain + bias).astype(bf16)
        pre = jnp.dot(zed, w1[...], preferred_element_type=f32) + hidden_bias
        dact = jnp.dot(wet, w2[...], preferred_element_type=f32)
        phi = 0.5 + 0.5 * lax.erf(pre * root_half)
        act = (pre * phi).astype(bf16)
        dhid = (dact * (phi + pre * (jnp.exp(-0.5 * pre * pre) * inv_root_tau))).astype(bf16)
        dzed = lax.dot_general(dhid, w1[...], (((1,), (1,)), ((), ())), preferred_element_type=f32)
        rows_first = (((0,), (0,)), ((), ()))
        expand[...] += lax.dot_general(zed, dhid, rows_first, preferred_element_type=f32)
        project[...] += lax.dot_general(wet, act, rows_first, preferred_element_type=f32)
        dnorm = dzed * gain
        mean1 = group_mean(dnorm, ones)
        mean2 = group_mean(dnorm * normed, ones)
        dconv = rstd * (dnorm - mean1 - normed * mean2)
        conv[i] = dconv
        dconv_ref[i, pl.ds(RIM, columns), :] = dconv
        hidden[...] += jnp.sum(dhid.astype(f32).reshape(columns // 8, 8, -1), axis=0)
        parts = (wet.astype(f32), dzed * normed, dzed, dconv)
        for k, part in enumerate(parts):
            small[k] += jnp.sum(part.reshape(columns // 8, 8, lanes), axis=0)
        return carry

    lax.fori_loop(0, half, row_step, 0)

    rows = []
    for block in (expand, project):
        total = block[:chan, :wide_e] + block[chan:, wide_e:]
        rows += [total[:, k * lanes : (k + 1) * lanes] for k in range(wide_e // lanes)]
    big = jnp.concatenate(rows, axis=0)
    total = jnp.sum(hidden[...], axis=0, keepdims=True)
    total = total[:, :wide_e] + total[:, wide_e:]
    rows = [total[:, k * lanes : (k + 1) * lanes] for k in range(wide_e // lanes)]
    rows += [jnp.sum(small[k], axis=0, keepdims=True) for k in range(4)]
    rows.append(jnp.zeros((-len(rows) % 8, lanes), f32))
    rows += tap_sums(ext32, conv)
    put_sums(send_ref, big, jnp.concatenate(rows, axis=0))

    pad = jnp.zeros((cells - RIM, lanes), f32)
    last_at = n_cols
    first = [x for i in range(half) for x in (conv[i, :RIM, :], pad)]
    last = [x for i in range(half) for x in (conv[i, last_at - RIM : last_at, :], pad)]
    first = jnp.concatenate(first, axis=0)
    last = jnp.concatenate(last, axis=0)
    odd = odd_ref[0] == 1
    base = send_ref.shape[0] - later_ref.shape[0]
    send_ref[base:] = jnp.where(odd, first, last).astype(bf16)
    later_ref[...] = jnp.where(odd, last, first).astype(bf16)


def tap_sums(ext32, grad_ref):
    half, columns, lanes = grad_ref.shape

    def trip(t, carry):
        start = pl.multiple_of(t * 8, 8)
        total = list(carry)
        grads = [grad_ref[i, pl.ds(start, 8), :] for i in range(half)]
        for row in range(half + 2 * RIM):
            for b in range(TAPS):
                piece = ext32[row, pl.ds(start + b, 8), :]
                for i in range(half):
                    a = row - i
                    if 0 <= a < TAPS:
                        total[a * TAPS + b] = total[a * TAPS + b] + grads[i] * piece
        return tuple(total)

    zero = jnp.zeros((8, lanes), f32)
    total = lax.fori_loop(0, columns // 8, trip, (zero,) * (TAPS * TAPS))
    rows = []
    for a in range(TAPS):
        rows += [jnp.sum(total[a * TAPS + b], axis=0, keepdims=True) for b in range(TAPS)]
        rows.append(jnp.zeros((1, lanes), f32))
    return rows


def add_kernel(coarse, fine, mine_ref, other_ref, later_ref, send_ref):
    put_sums(send_ref, *added(mine_ref, other_ref, coarse, fine))
    send_ref[coarse + 2 * fine :] = later_ref[...]


def plain_add_kernel(coarse, fine, mine_ref, other_ref, send_ref):
    put_sums(send_ref, *added(mine_ref, other_ref, coarse, fine))


def rows_kernel(
    coarse, fine, n_cols, odd_ref, mine_ref, other_ref, early_ref, dconv_ref, send_ref, later_ref, full_ref
):
    half, wide, lanes = dconv_ref.shape
    at = coarse + 2 * fine
    put_sums(send_ref, *added(mine_ref, other_ref, coarse, fine))
    odd_lon, odd_lat = odd_ref[0] == 1, odd_ref[1] == 1
    early = early_ref[at:].astype(f32)
    late = other_ref[at:].astype(f32)
    right = jnp.where(odd_lon, late, early)
    left = jnp.where(odd_lon, early, late)
    step = early.shape[0] // half
    for i in range(half):
        full_ref[i] = dconv_ref[i]
        full_ref[i, :RIM, :] = left[i * step : i * step + RIM]
        full_ref[i, RIM + n_cols : 2 * RIM + n_cols, :] = right[i * step : i * step + RIM]
    mid = wide // 2
    first = lax.broadcasted_iota(jnp.int32, (mid, lanes), 1) < lanes // 2
    for k in range(RIM):
        upper = full_ref[k]
        lower = full_ref[half - RIM + k]
        upper = jnp.where(first, upper[:mid], swap(upper[mid:]))
        lower = jnp.where(first, swap(lower[:mid]), lower[mid:])
        send_ref[at + k * mid : at + (k + 1) * mid, :] = jnp.where(odd_lat, upper, lower).astype(bf16)
        later_ref[k * mid : (k + 1) * mid, :] = jnp.where(odd_lat, lower, upper).astype(bf16)


def back_kernel(at, odd_ref, early_ref, late_ref, mid_ref, taps_ref, out_ref, ext32, wide):
    half, columns, lanes = out_ref.shape
    mid = mid_ref.shape[1] // 2
    odd_lat, edge = odd_ref[1] == 1, odd_ref[2] == 1

    def rows(k):
        early = early_ref[at + k * mid : at + (k + 1) * mid, :].astype(f32)
        late = late_ref[k * mid : (k + 1) * mid, :].astype(f32)
        return early, jnp.where(edge, 0.0, late)

    def top(k):
        early, late = rows(k)
        return jnp.where(odd_lat, early, late)

    def bottom(k):
        early, late = rows(k)
        return jnp.where(odd_lat, late, early)

    assemble(ext32, mid_ref, top, bottom)
    fill_taps(taps_ref, wide, True)

    def put(i, start, value):
        out_ref[i, pl.ds(start, STEP), :] = value

    convolve(ext32, wide, put, half, columns)


def finish_kernel(
    coarse, fine, scale, mine_ref, other_ref,
    taps_ref, conv_ref, gain_ref, bias_ref, expand_ref, hidden_ref, project_ref, wet_ref,
):
    lanes = mine_ref.shape[1]
    chan, wide_e = expand_ref.shape
    big, small = added(mine_ref, other_ref, coarse, fine)
    big, small = big * scale, small * scale
    blocks = wide_e // lanes
    for k in range(blocks):
        expand_ref[:, k * lanes : (k + 1) * lanes] = big[k * chan : (k + 1) * chan]
        at = (blocks + k) * chan
        project_ref[:, k * lanes : (k + 1) * lanes] = big[at : at + chan]
        hidden_ref[:, k * lanes : (k + 1) * lanes] = small[k : k + 1]
    narrow = small[:, :chan] + small[:, chan:]
    for k, ref in enumerate((wet_ref, gain_ref, bias_ref, conv_ref)):
        ref[...] = narrow[blocks + k : blocks + k + 1]
    at = fine - 8 * TAPS
    for a in range(TAPS):
        taps_ref[a] = narrow[at + 8 * a : at + 8 * a + TAPS]


def call(kernel, out_shape, scratch, flops, *args):
    vmem = pl.BlockSpec(memory_space=pltpu.VMEM)
    smem = pl.BlockSpec(memory_space=pltpu.SMEM)
    many = isinstance(out_shape, (list, tuple))
    return pl.pallas_call(
        kernel,
        out_shape=out_shape,
        in_specs=[smem if arg.dtype == jnp.int32 else vmem for arg in args],
        out_specs=[vmem] * len(out_shape) if many else vmem,
        scratch_shapes=scratch,
        cost_estimate=pl.CostEstimate(flops=flops, bytes_accessed=1 << 20, transcendentals=0),
        compiler_params=pltpu.CompilerParams(vmem_limit_bytes=40 << 20),
    )(*args)


def body(
    state, land_sea, cotangent, kernel, conv_bias, ln_gain, ln_bias, w_expand, b_expand, w_project
):
    n_chan, n_rows, n_cols = state.shape
    n_wide = w_expand.shape[1]
    half = n_rows // 2
    lanes = 2 * n_chan
    columns = -(-n_cols // STEP) * STEP
    padded = -(-(columns + 2 * RIM) // 32) * 32
    coarse = 2 * n_chan * n_wide // lanes
    fine = 8 * TAPS + -(-(n_wide // lanes + 4) // 8) * 8
    rim = half * 4
    at = coarse + 2 * fine
    rim_rows = RIM * padded // 2
    cells = n_rows * n_cols
    conv_flops = cells * n_chan * TAPS * TAPS * 2
    shaped = jax.ShapeDtypeStruct
    taps = kernel.transpose(1, 2, 0).reshape(TAPS * TAPS, n_chan)
    twice = lambda v: jnp.concatenate([v, v])
    vectors = jnp.stack([twice(conv_bias), twice(ln_gain), twice(ln_bias)])
    lat, lon = lax.axis_index("lat"), lax.axis_index("lon")
    lat_last = lax.axis_size("lat") - 1
    place = jnp.stack([lon % 2, lat % 2, ((lat == 0) | (lat == lat_last)).astype(jnp.int32)])

    field = state.transpose(1, 2, 0)
    flat = (n_rows * RIM, n_chan)
    up, down = neighbours("lon", True)
    left = lax.ppermute(field[:, -RIM:].reshape(flat), "lon", up)
    right = lax.ppermute(field[:, :RIM].reshape(flat), "lon", down)
    piece = (n_rows, RIM, n_chan)
    blank = jnp.zeros((n_rows, padded - n_cols - 2 * RIM, n_chan), bf16)
    field = jnp.concatenate([left.reshape(piece), field, right.reshape(piece), blank], axis=1)
    up, down = neighbours("lat", False)
    top = lax.ppermute(dense(field[-RIM:]), "lat", up)
    bottom = lax.ppermute(dense(field[:RIM]), "lat", down)

    wet = cotangent * land_sea[None].astype(bf16)
    wet = jnp.pad(wet.transpose(1, 2, 0), ((0, 0), (0, columns - n_cols), (0, 0)))

    dconv, mine, later = call(
        functools.partial(block_kernel, n_cols),
        [
            shaped((half, padded, lanes), f32),
            shaped((at + rim, lanes), bf16),
            shaped((rim, lanes), bf16),
        ],
        [
            pltpu.VMEM((half + 2 * RIM, padded, lanes), f32),
            pltpu.VMEM((TAPS * TAPS, 8, lanes), f32),
            pltpu.VMEM((half, columns, lanes), f32),
            pltpu.VMEM((lanes, 2 * n_wide), bf16),
            pltpu.VMEM((lanes, 2 * n_wide), bf16),
            pltpu.VMEM((lanes, 2 * n_wide), f32),
            pltpu.VMEM((lanes, 2 * n_wide), f32),
            pltpu.VMEM((8, 2 * n_wide), f32),
            pltpu.VMEM((4, 8, lanes), f32),
        ],
        cells * n_chan * n_wide * 10 + 2 * conv_flops,
        place, pack(field), top, bottom, pack(wet), taps, vectors, w_expand,
        twice(b_expand).reshape(1, -1), w_project.T,
    )

    def plain(mine, axis, bit):
        other = lax.ppermute(mine, axis, pairs(axis, bit))
        add = functools.partial(plain_add_kernel, coarse, fine)
        return call(add, shaped((at, lanes), bf16), [], at * lanes, mine, other)

    early = lax.ppermute(mine, "lon", pairs("lon", 1))
    bits = higher_bits("lon")
    if bits:
        add = functools.partial(plain_add_kernel, coarse, fine)
        mine = call(add, shaped((at, lanes), bf16), [], at * lanes, mine, early)
        for bit in bits:
            mine = plain(mine, "lon", bit)
        mine = jnp.concatenate([mine, later], axis=0)
    else:
        add = functools.partial(add_kernel, coarse, fine)
        mine = call(add, shaped((at + rim, lanes), bf16), [], at * lanes, mine, early, later)
    other = lax.ppermute(mine, "lon", ring_pairs("lon"))
    mine, later, full = call(
        functools.partial(rows_kernel, coarse, fine, n_cols),
        [
            shaped((at + rim_rows, lanes), bf16),
            shaped((rim_rows, lanes), bf16),
            shaped(dconv.shape, f32),
        ],
        [],
        at * lanes,
        place, mine, other, early, dconv,
    )
    early = lax.ppermute(mine, "lat", pairs("lat", 1))
    late = lax.ppermute(later, "lat", ring_pairs("lat"))
    add = functools.partial(plain_add_kernel, coarse, fine)
    mine = call(add, shaped((at, lanes), bf16), [], at * lanes, mine, early)
    bits = [2] + higher_bits("lat")
    for bit in bits[:-1]:
        mine = plain(mine, "lat", bit)
    other = lax.ppermute(mine, "lat", pairs("lat", bits[-1]))

    grad = call(
        functools.partial(back_kernel, at),
        shaped((half, columns, lanes), f32),
        [
            pltpu.VMEM((half + 2 * RIM, padded, lanes), f32),
            pltpu.VMEM((TAPS * TAPS, 8, lanes), f32),
        ],
        conv_flops,
        place, early, late, full, taps,
    )
    grad = unpack(grad)[:, :n_cols].transpose(2, 0, 1)
    state_grad = (cotangent.astype(f32) + grad).astype(bf16)

    scale = 1.0 / math.sqrt(cells * lax.axis_size("lat") * lax.axis_size("lon"))
    narrow = shaped((1, n_chan), f32)
    out = call(
        functools.partial(finish_kernel, coarse, fine, scale),
        [
            shaped((TAPS, TAPS, n_chan), f32),
            narrow,
            narrow,
            narrow,
            shaped((n_chan, n_wide), f32),
            shaped((1, n_wide), f32),
            shaped((n_chan, n_wide), f32),
            narrow,
        ],
        [],
        at * lanes,
        mine, other,
    )
    return (
        state_grad,
        out[0].transpose(2, 0, 1),
        out[1].reshape(-1),
        out[2].reshape(-1),
        out[3].reshape(-1),
        out[4],
        out[5].reshape(-1),
        out[6].T,
        out[7].reshape(-1),
    )


def solution(mesh):
    in_specs = (
        P(None, "lat", "lon"),
        P("lat", "lon"),
        P(None, "lat", "lon"),
        P(),
        P(),
        P(),
        P(),
        P(),
        P(),
        P(),
    )
    out_specs = (P(None, "lat", "lon"), P(), P(), P(), P(), P(), P(), P(), P())
    return jax.shard_map(body, mesh=mesh, in_specs=in_specs, out_specs=out_specs, check_vma=False)
```

```python
import functools
import math

import jax
import jax.numpy as jnp
from jax import lax
from jax.experimental import pallas as pl
from jax.experimental.pallas import tpu as pltpu
from jax.sharding import PartitionSpec as P

TAPS = 7
RIM = 3
STEP = 16

ln_eps = 1e-06
root_half = 0.7071067811865476
inv_root_tau = 0.3989422804014327
f32 = jnp.float32
bf16 = jnp.bfloat16


def pairs(axis, bit):
    return [(i, i ^ bit) for i in range(lax.axis_size(axis))]


def ring_pairs(axis, wraps):
    size = lax.axis_size(axis)
    swaps = [(i, i + 1 if i % 2 else i - 1) for i in range(size)]
    return [(i, j % size) for i, j in swaps if wraps or 0 <= j < size]


def bits(axis, first):
    size = lax.axis_size(axis)
    if size < 4 or size & (size - 1):
        raise ValueError("axis size")
    return [1 << k for k in range(first, size.bit_length() - 1)]


def split_rounds():
    steps = bits("lat", 1)
    turned = steps[1:] + steps[:1]
    size = lax.axis_size("lat")
    return [[(i, i ^ (b if i % 2 else a)) for i in range(size)] for a, b in zip(steps, turned)]


def pack(field):
    half = field.shape[0] // 2
    return jnp.concatenate([field[:half], field[half:]], axis=2)


def unpack(field):
    chan = field.shape[2] // 2
    return jnp.concatenate([field[:, :, :chan], field[:, :, chan:]], axis=0)


def dense(rows):
    half = rows.shape[1] // 2
    return jnp.concatenate([rows[:, :half], rows[:, half:]], axis=2)


def swap(value):
    return pltpu.roll(value, value.shape[-1] // 2, value.ndim - 1)


def assemble(ext_ref, mid_ref, top, bottom):
    half, columns, lanes = mid_ref.shape
    first = lax.broadcasted_iota(jnp.int32, (columns, lanes), 1) < lanes // 2
    for k in range(RIM):
        above, below = top(k), bottom(k)
        above = jnp.concatenate([above, swap(above)], axis=0)
        below = jnp.concatenate([swap(below), below], axis=0)
        upper = swap(mid_ref[half - RIM + k].astype(f32))
        lower = swap(mid_ref[k].astype(f32))
        ext_ref[k] = jnp.where(first, above, upper)
        ext_ref[half + RIM + k] = jnp.where(first, lower, below)
    for i in range(half):
        ext_ref[RIM + i] = mid_ref[i].astype(f32)


def split(value):
    high = value.astype(bf16)
    return high, (value - high.astype(f32)).astype(bf16)


def added(mine_ref, other_ref, total):
    return mine_ref[:total].astype(f32) + other_ref[:total].astype(f32)


def fill_taps(taps_ref, wide_ref, flip):
    count, chan = taps_ref.shape
    for tap in range(count):
        row = taps_ref[count - 1 - tap if flip else tap, :].reshape(1, chan)
        wide_ref[tap] = jnp.broadcast_to(jnp.concatenate([row, row], axis=1), (8, 2 * chan))


def convolve(ext_ref, wide_ref, store, half, columns, unroll):
    def trip(t, carry):
        start = pl.multiple_of(t * STEP, STEP)
        tiles = STEP // 8
        total = [[None] * tiles for _ in range(half)]
        for row in range(half + 2 * RIM):
            for b in range(TAPS):
                piece = [ext_ref[row, pl.ds(start + b + 8 * s, 8), :] for s in range(tiles)]
                for i in range(half):
                    a = row - i
                    if 0 <= a < TAPS:
                        weight = wide_ref[a * TAPS + b]
                        for s in range(tiles):
                            term = weight * piece[s]
                            total[i][s] = term if total[i][s] is None else total[i][s] + term
        for i in range(half):
            store(i, start, jnp.concatenate(total[i], axis=0))
        return carry

    lax.fori_loop(0, columns // STEP, trip, 0, unroll=unroll)


def group_mean(values, ones):
    high = values.astype(bf16)
    low = (values - high.astype(f32)).astype(bf16)
    return jnp.dot(jnp.concatenate([high, low], axis=1), ones, preferred_element_type=f32)


def block_kernel(
    n_cols, lon_ref, lat_ref, mid_ref, early_ref, late_ref, wet_ref, taps_ref, vec_ref, w1_ref, b1_ref, w2_ref,
    dconv_ref, send_ref, later_ref,
    ext32, wide, conv, w1, w2,
):
    half, columns, lanes = wet_ref.shape
    chan = lanes // 2
    wide_e = w1_ref.shape[1]
    cells = later_ref.shape[0] // half
    assemble(ext32, mid_ref, *rim_rows(lat_ref, early_ref, late_ref, 0))
    fill_taps(taps_ref, wide, False)
    w1[...] = jnp.zeros_like(w1)
    w2[...] = jnp.zeros_like(w2)
    w1[:chan, :wide_e] = w1_ref[...]
    w1[chan:, wide_e:] = w1_ref[...]
    w2[:chan, :wide_e] = w2_ref[...]
    w2[chan:, wide_e:] = w2_ref[...]
    dconv_ref[...] = jnp.zeros_like(dconv_ref)

    def put(i, start, value):
        conv[i, pl.ds(start, STEP), :] = value

    convolve(ext32, wide, put, half, columns, True)

    row_half = lax.broadcasted_iota(jnp.int32, (2 * lanes, lanes), 0) % lanes >= chan
    col_half = lax.broadcasted_iota(jnp.int32, (2 * lanes, lanes), 1) >= chan
    ones = jnp.where(row_half == col_half, 1.0 / chan, 0.0).astype(bf16)
    conv_bias, gain, bias = vec_ref[0:1, :], vec_ref[1:2, :], vec_ref[2:3, :]

    cells_all = half * columns
    out = conv[...].reshape(cells_all, lanes) + conv_bias
    wet = wet_ref[...].reshape(cells_all, lanes)
    center = out - group_mean(out, ones)
    rstd = lax.rsqrt(group_mean(center * center, ones) + ln_eps)
    normed = center * rstd
    zed = (normed * gain + bias).astype(bf16)
    pre = jnp.dot(zed, w1[...], preferred_element_type=f32) + b1_ref[...]
    dact = jnp.dot(wet, w2[...], preferred_element_type=f32)
    phi = 0.5 + 0.5 * lax.erf(pre * root_half)
    act = (pre * phi).astype(bf16)
    dhid = (dact * (phi + pre * (jnp.exp(-0.5 * pre * pre) * inv_root_tau))).astype(bf16)
    dzed = lax.dot_general(dhid, w1[...], (((1,), (1,)), ((), ())), preferred_element_type=f32)
    rows_first = (((0,), (0,)), ((), ()))
    expand = lax.dot_general(zed, dhid, rows_first, preferred_element_type=f32)
    project = lax.dot_general(wet, act, rows_first, preferred_element_type=f32)
    dnorm = dzed * gain
    mean1 = group_mean(dnorm, ones)
    mean2 = group_mean(dnorm * normed, ones)
    dconv = rstd * (dnorm - mean1 - normed * mean2)
    hidden = jnp.sum(dhid.astype(f32), axis=0, keepdims=True)
    parts = (wet.astype(f32), dzed * normed, dzed, dconv)
    small = [jnp.sum(part, axis=0, keepdims=True) for part in parts]
    dconv = dconv.reshape(half, columns, lanes)
    conv[...] = dconv
    dconv_ref[:, pl.ds(RIM, columns), :] = dconv

    rows = []
    for block in (expand, project):
        total = block[:chan, :wide_e] + block[chan:, wide_e:]
        rows += [total[:, k * lanes : (k + 1) * lanes] for k in range(wide_e // lanes)]
    total = hidden[:, :wide_e] + hidden[:, wide_e:]
    fine = [total[:, k * lanes : (k + 1) * lanes] for k in range(wide_e // lanes)] + small
    fine.append(jnp.zeros((-len(fine) % 8, lanes), f32))
    rows = jnp.concatenate(rows + fine + tap_sums(ext32, conv), axis=0)
    send_ref[: rows.shape[0]] = rows.astype(bf16)

    pad = jnp.zeros((cells - RIM, lanes), f32)
    first = [x for i in range(half) for x in (conv[i, :RIM, :], pad)]
    last = [x for i in range(half) for x in (conv[i, n_cols - RIM : n_cols, :], pad)]
    first = jnp.concatenate(first, axis=0)
    last = jnp.concatenate(last, axis=0)
    odd = lon_ref[0] == 1
    send_ref[rows.shape[0] :] = jnp.where(odd, first, last).astype(bf16)
    later_ref[...] = jnp.where(odd, last, first).astype(bf16)


def tap_sums(ext32, grad_ref):
    half, columns, lanes = grad_ref.shape

    def trip(t, carry):
        start = pl.multiple_of(t * 8, 8)
        total = list(carry)
        grads = [grad_ref[i, pl.ds(start, 8), :] for i in range(half)]
        for row in range(half + 2 * RIM):
            for b in range(TAPS):
                piece = ext32[row, pl.ds(start + b, 8), :]
                for i in range(half):
                    a = row - i
                    if 0 <= a < TAPS:
                        total[a * TAPS + b] = total[a * TAPS + b] + grads[i] * piece
        return tuple(total)

    zero = jnp.zeros((8, lanes), f32)
    total = lax.fori_loop(0, columns // 8, trip, (zero,) * (TAPS * TAPS))
    rows = []
    for a in range(TAPS):
        rows += [jnp.sum(total[a * TAPS + b], axis=0, keepdims=True) for b in range(TAPS)]
        rows.append(jnp.zeros((1, lanes), f32))
    return rows


def add_kernel(total, mine_ref, other_ref, later_ref, send_ref):
    send_ref[:total] = added(mine_ref, other_ref, total).astype(bf16)
    send_ref[total:] = later_ref[...]


def rows_kernel(
    n_total, n_cols, lon_ref, lat_ref, mine_ref, other_ref, early_ref, dconv_ref,
    keep_ref, send_ref, later_ref, full_ref,
):
    half, wide, lanes = dconv_ref.shape
    odd_lon, odd_lat = lon_ref[0] == 1, lat_ref[0] == 1
    total = added(mine_ref, other_ref, n_total)
    part = n_total // 2
    keep_ref[...] = jnp.where(odd_lat, total[part:], total[:part])
    high, low = split(jnp.where(odd_lat, total[:part], total[part:]))
    send_ref[:part] = high
    send_ref[part : 2 * part] = low
    early = early_ref[n_total:].astype(f32)
    late = other_ref[n_total:].astype(f32)
    right = jnp.where(odd_lon, late, early)
    left = jnp.where(odd_lon, early, late)
    step = early.shape[0] // half
    for i in range(half):
        full_ref[i] = dconv_ref[i]
        full_ref[i, :RIM, :] = left[i * step : i * step + RIM]
        full_ref[i, RIM + n_cols : 2 * RIM + n_cols, :] = right[i * step : i * step + RIM]
    mid = wide // 2
    first = lax.broadcasted_iota(jnp.int32, (mid, lanes), 1) < lanes // 2
    at = 2 * part
    for k in range(RIM):
        upper = full_ref[k]
        lower = full_ref[half - RIM + k]
        upper = jnp.where(first, upper[:mid], swap(upper[mid:]))
        lower = jnp.where(first, swap(lower[:mid]), lower[mid:])
        send_ref[at + k * mid : at + (k + 1) * mid, :] = jnp.where(odd_lat, upper, lower).astype(bf16)
        later_ref[k * mid : (k + 1) * mid, :] = jnp.where(odd_lat, lower, upper).astype(bf16)


def rim_rows(lat_ref, early_ref, late_ref, at):
    mid = late_ref.shape[0] // RIM
    odd = lat_ref[0] == 1

    def rows(k):
        early = early_ref[at + k * mid : at + (k + 1) * mid, :].astype(f32)
        return early, late_ref[k * mid : (k + 1) * mid, :].astype(f32)

    def top(k):
        early, late = rows(k)
        return jnp.where(odd, early, late)

    def bottom(k):
        early, late = rows(k)
        return jnp.where(odd, late, early)

    return top, bottom


def back_kernel(at, lat_ref, early_ref, late_ref, mid_ref, taps_ref, out_ref, ext32, wide):
    half, columns, lanes = out_ref.shape
    assemble(ext32, mid_ref, *rim_rows(lat_ref, early_ref, late_ref, at))
    fill_taps(taps_ref, wide, True)

    def put(i, start, value):
        out_ref[i, pl.ds(start, STEP), :] = value

    convolve(ext32, wide, put, half, columns, 1)


def finish_kernel(
    scale, lat_ref, mine_ref, other_ref,
    taps_ref, conv_ref, gain_ref, bias_ref, expand_ref, hidden_ref, project_ref, wet_ref,
):
    lanes = mine_ref.shape[1]
    chan, wide_e = expand_ref.shape
    odd = lat_ref[0] == 1
    mine, other = mine_ref[...] * scale, other_ref[...] * scale
    total = jnp.concatenate([jnp.where(odd, other, mine), jnp.where(odd, mine, other)], axis=0)
    blocks = wide_e // lanes
    small = total[2 * blocks * chan :]
    for k in range(blocks):
        expand_ref[:, k * lanes : (k + 1) * lanes] = total[k * chan : (k + 1) * chan]
        at = (blocks + k) * chan
        project_ref[:, k * lanes : (k + 1) * lanes] = total[at : at + chan]
        hidden_ref[:, k * lanes : (k + 1) * lanes] = small[k : k + 1]
    narrow = small[:, :chan] + small[:, chan:]
    for k, ref in enumerate((wet_ref, gain_ref, bias_ref, conv_ref)):
        ref[...] = narrow[blocks + k : blocks + k + 1]
    at = small.shape[0] - 8 * TAPS
    for a in range(TAPS):
        taps_ref[a] = narrow[at + 8 * a : at + 8 * a + TAPS]


def call(kernel, out_shape, scratch, flops, *args):
    vmem = pl.BlockSpec(memory_space=pltpu.VMEM)
    smem = pl.BlockSpec(memory_space=pltpu.SMEM)
    many = isinstance(out_shape, (list, tuple))
    return pl.pallas_call(
        kernel,
        out_shape=out_shape,
        in_specs=[smem if arg.dtype == jnp.int32 else vmem for arg in args],
        out_specs=[vmem] * len(out_shape) if many else vmem,
        scratch_shapes=scratch,
        cost_estimate=pl.CostEstimate(flops=flops, bytes_accessed=1 << 20, transcendentals=0),
        compiler_params=pltpu.CompilerParams(vmem_limit_bytes=40 << 20),
    )(*args)


def body(
    state, land_sea, cotangent, kernel, conv_bias, ln_gain, ln_bias, w_expand, b_expand, w_project
):
    n_chan, n_rows, n_cols = state.shape
    n_wide = w_expand.shape[1]
    half = n_rows // 2
    lanes = 2 * n_chan
    columns = -(-n_cols // STEP) * STEP
    padded = -(-(columns + 2 * RIM) // 32) * 32
    total = 2 * n_chan * n_wide // lanes + -(-(n_wide // lanes + 4) // 8) * 8 + 8 * TAPS
    part = total // 2
    rim = half * 4
    rows = RIM * padded // 2
    cells = n_rows * n_cols
    conv_flops = cells * n_chan * TAPS * TAPS * 2
    shaped = jax.ShapeDtypeStruct
    taps = kernel.transpose(1, 2, 0).reshape(TAPS * TAPS, n_chan)
    twice = lambda v: jnp.concatenate([v, v])
    vectors = jnp.stack([twice(conv_bias), twice(ln_gain), twice(ln_bias)])
    odd_lon, odd_lat = lax.axis_index("lon") % 2, lax.axis_index("lat") % 2
    scalars = (odd_lon.reshape(1), odd_lat.reshape(1))

    field = pack(state.transpose(1, 2, 0))
    first = pack(state[:, :, :RIM].transpose(1, 2, 0))
    last = pack(state[:, :, -RIM:].transpose(1, 2, 0))
    early = lax.ppermute(jnp.where(odd_lon == 1, first, last), "lon", pairs("lon", 1))
    late = lax.ppermute(jnp.where(odd_lon == 1, last, first), "lon", ring_pairs("lon", True))
    left, right = jnp.where(odd_lon == 1, early, late), jnp.where(odd_lon == 1, late, early)
    blank = jnp.zeros((half, padded - n_cols - 2 * RIM, lanes), bf16)
    field = jnp.concatenate([left, field, right, blank], axis=1)
    first, last = dense(field[:RIM, :, :n_chan]), dense(field[-RIM:, :, n_chan:])
    flat = (rows, lanes)
    early = lax.ppermute(
        jnp.where(odd_lat == 1, first, last).reshape(flat), "lat", pairs("lat", 1)
    )
    late = lax.ppermute(
        jnp.where(odd_lat == 1, last, first).reshape(flat), "lat", ring_pairs("lat", False)
    )

    wet = cotangent * land_sea[None].astype(bf16)
    wet = jnp.pad(wet.transpose(1, 2, 0), ((0, 0), (0, columns - n_cols), (0, 0)))

    dconv, mine, later = call(
        functools.partial(block_kernel, n_cols),
        [
            shaped((half, padded, lanes), f32),
            shaped((total + rim, lanes), bf16),
            shaped((rim, lanes), bf16),
        ],
        [
            pltpu.VMEM((half + 2 * RIM, padded, lanes), f32),
            pltpu.VMEM((TAPS * TAPS, 8, lanes), f32),
            pltpu.VMEM((half, columns, lanes), f32),
            pltpu.VMEM((lanes, 2 * n_wide), bf16),
            pltpu.VMEM((lanes, 2 * n_wide), bf16),
        ],
        cells * n_chan * n_wide * 10 + 2 * conv_flops,
        *scalars, field, early, late, pack(wet), taps, vectors, w_expand,
        twice(b_expand).reshape(1, -1), w_project.T,
    )

    early = lax.ppermute(mine, "lon", pairs("lon", 1))
    other = early
    for bit in bits("lon", 2) + [0]:
        add = functools.partial(add_kernel, total)
        sent = shaped((total + rim, lanes), bf16)
        mine = call(add, sent, [], total * lanes, mine, other, later)
        if bit:
            other = lax.ppermute(mine, "lon", pairs("lon", bit))
    other = lax.ppermute(mine, "lon", ring_pairs("lon", True))
    mine, send, later, full = call(
        functools.partial(rows_kernel, total, n_cols),
        [
            shaped((part, lanes), f32),
            shaped((2 * part + rows, lanes), bf16),
            shaped((rows, lanes), bf16),
            shaped(dconv.shape, f32),
        ],
        [],
        total * lanes,
        *scalars, mine, other, early, dconv,
    )
    early = lax.ppermute(send, "lat", pairs("lat", 1))
    late = lax.ppermute(later, "lat", ring_pairs("lat", False))
    mine = mine + early[:part].astype(f32) + early[part : 2 * part].astype(f32)
    for k, swaps in enumerate(split_rounds()):
        other = lax.ppermute(mine, "lat", swaps)
        if k == 0:
            other, late = lax.optimization_barrier((other, late))
        mine = mine + other
    other = lax.ppermute(mine, "lat", pairs("lat", 1))

    grad = call(
        functools.partial(back_kernel, 2 * part),
        shaped((half, columns, lanes), f32),
        [
            pltpu.VMEM((half + 2 * RIM, padded, lanes), f32),
            pltpu.VMEM((TAPS * TAPS, 8, lanes), f32),
        ],
        conv_flops,
        scalars[1], early, late, full, taps,
    )
    grad = unpack(grad)[:, :n_cols].transpose(2, 0, 1)
    state_grad = (cotangent.astype(f32) + grad).astype(bf16)

    scale = 1.0 / math.sqrt(cells * lax.axis_size("lat") * lax.axis_size("lon"))
    narrow = shaped((1, n_chan), f32)
    out = call(
        functools.partial(finish_kernel, scale),
        [
            shaped((TAPS, TAPS, n_chan), f32),
            narrow,
            narrow,
            narrow,
            shaped((n_chan, n_wide), f32),
            shaped((1, n_wide), f32),
            shaped((n_chan, n_wide), f32),
            narrow,
        ],
        [],
        total * lanes,
        scalars[1], mine, other,
    )
    return (
        state_grad,
        out[0].transpose(2, 0, 1),
        out[1].reshape(-1),
        out[2].reshape(-1),
        out[3].reshape(-1),
        out[4],
        out[5].reshape(-1),
        out[6].T,
        out[7].reshape(-1),
    )


def solution(mesh):
    in_specs = (
        P(None, "lat", "lon"),
        P("lat", "lon"),
        P(None, "lat", "lon"),
        P(),
        P(),
        P(),
        P(),
        P(),
        P(),
        P(),
    )
    out_specs = (P(None, "lat", "lon"), P(), P(), P(), P(), P(), P(), P(), P())
    return jax.shard_map(body, mesh=mesh, in_specs=in_specs, out_specs=out_specs, check_vma=False)
```

```python
import functools
import math

import jax
import jax.numpy as jnp
from jax import lax
from jax.experimental import pallas as pl
from jax.experimental.pallas import tpu as pltpu
from jax.sharding import PartitionSpec as P

TAPS = 7
RIM = 3
STEP = 16

ln_eps = 1e-06
root_half = 0.7071067811865476
inv_root_tau = 0.3989422804014327
f32 = jnp.float32
bf16 = jnp.bfloat16


def pairs(axis, bit):
    return [(i, i ^ bit) for i in range(lax.axis_size(axis))]


def ring_pairs(axis, wraps):
    size = lax.axis_size(axis)
    swaps = [(i, i + 1 if i % 2 else i - 1) for i in range(size)]
    return [(i, j % size) for i, j in swaps if wraps or 0 <= j < size]


def bits(axis, first):
    size = lax.axis_size(axis)
    if size < 4 or size & (size - 1):
        raise ValueError("axis size")
    return [1 << k for k in range(first, size.bit_length() - 1)]


def split_rounds():
    steps = bits("lat", 1)
    turned = steps[1:] + steps[:1]
    size = lax.axis_size("lat")
    return [[(i, i ^ (b if i % 2 else a)) for i in range(size)] for a, b in zip(steps, turned)]


def pack(field):
    half = field.shape[0] // 2
    return jnp.concatenate([field[:half], field[half:]], axis=2)


def unpack(field):
    chan = field.shape[2] // 2
    return jnp.concatenate([field[:, :, :chan], field[:, :, chan:]], axis=0)


def dense(rows):
    half = rows.shape[1] // 2
    return jnp.concatenate([rows[:, :half], rows[:, half:]], axis=2)


def swap(value):
    return pltpu.roll(value, value.shape[-1] // 2, value.ndim - 1)


def assemble(ext_ref, mid_ref, top, bottom):
    half, columns, lanes = mid_ref.shape
    first = lax.broadcasted_iota(jnp.int32, (columns, lanes), 1) < lanes // 2
    for k in range(RIM):
        above, below = top(k), bottom(k)
        above = jnp.concatenate([above, swap(above)], axis=0)
        below = jnp.concatenate([swap(below), below], axis=0)
        upper = swap(mid_ref[half - RIM + k].astype(f32))
        lower = swap(mid_ref[k].astype(f32))
        ext_ref[k] = jnp.where(first, above, upper)
        ext_ref[half + RIM + k] = jnp.where(first, lower, below)
    for i in range(half):
        ext_ref[RIM + i] = mid_ref[i].astype(f32)


def split(value):
    high = value.astype(bf16)
    return high, (value - high.astype(f32)).astype(bf16)


def added(mine_ref, other_ref, total):
    return mine_ref[:total].astype(f32) + other_ref[:total].astype(f32)


def fill_taps(taps_ref, wide_ref, flip):
    count, chan = taps_ref.shape
    for tap in range(count):
        row = taps_ref[count - 1 - tap if flip else tap, :].reshape(1, chan)
        wide_ref[tap] = jnp.broadcast_to(jnp.concatenate([row, row], axis=1), (8, 2 * chan))


def convolve_tile(ext_ref, wide_ref, store, half, start):
    tiles = STEP // 8
    total = [[None] * tiles for _ in range(half)]
    for row in range(half + 2 * RIM):
        for b in range(TAPS):
            piece = [ext_ref[row, pl.ds(start + b + 8 * s, 8), :] for s in range(tiles)]
            for i in range(half):
                a = row - i
                if 0 <= a < TAPS:
                    weight = wide_ref[a * TAPS + b]
                    for s in range(tiles):
                        term = weight * piece[s]
                        total[i][s] = term if total[i][s] is None else total[i][s] + term
    for i in range(half):
        store(i, start, jnp.concatenate(total[i], axis=0))


def convolve(ext_ref, wide_ref, store, half, columns, unroll):
    def trip(t, carry):
        convolve_tile(ext_ref, wide_ref, store, half, pl.multiple_of(t * STEP, STEP))
        return carry

    lax.fori_loop(0, columns // STEP, trip, 0, unroll=unroll)


def group_mean(values, ones):
    high = values.astype(bf16)
    low = (values - high.astype(f32)).astype(bf16)
    return jnp.dot(jnp.concatenate([high, low], axis=1), ones, preferred_element_type=f32)


def edge_kernel(n_cols, lon_ref, lat_ref, mid_ref, early_ref, late_ref, send_ref, later_ref):
    half, wide, lanes = mid_ref.shape
    mid = wide // 2
    odd_lat, odd_lon = lat_ref[0] == 1, lon_ref[0] == 1
    base = n_cols // 16 * 16
    skip = n_cols - base
    first = lax.broadcasted_iota(jnp.int32, (8, lanes), 1) < lanes // 2
    left, right = [], []
    for i in range(half):
        left.append(mid_ref[i, :16, :].astype(f32)[:8])
        right.append(mid_ref[i, base : base + 32, :].astype(f32)[skip : skip + 8])
    ends = [([], []), ([], [])]
    for k in range(RIM):
        at = k * mid
        one, two = [], []
        for ref in (early_ref, late_ref):
            one.append(ref[at : at + 16, :].astype(f32)[:8])
            two.append(ref[at + base - mid : at + mid, :].astype(f32)[skip : skip + 8])
        above = jnp.where(odd_lat, one[0], one[1]), jnp.where(odd_lat, two[0], two[1])
        below = jnp.where(odd_lat, one[1], one[0]), jnp.where(odd_lat, two[1], two[0])
        ends[0][0].append(jnp.where(first, above[0], swap(left[half - RIM + k])))
        ends[0][1].append(jnp.where(first, swap(above[1]), swap(right[half - RIM + k])))
        ends[1][0].append(jnp.where(first, swap(left[k]), swap(below[0])))
        ends[1][1].append(jnp.where(first, swap(right[k]), below[1]))
    left = ends[0][0] + left + ends[1][0]
    right = ends[0][1] + right + ends[1][1]
    left = jnp.concatenate([x[RIM : RIM + 4] for x in left], axis=0)
    right = jnp.concatenate([x[:4] for x in right], axis=0)
    send_ref[...] = jnp.where(odd_lon, left, right).astype(bf16)
    later_ref[...] = jnp.where(odd_lon, right, left).astype(bf16)


def inner_kernel(lat_ref, mid_ref, early_ref, late_ref, taps_ref, ext_ref, conv_ref, wide_ref):
    half, columns, lanes = conv_ref.shape
    assemble(ext_ref, mid_ref, *rim_rows(lat_ref, early_ref, late_ref, 0))
    fill_taps(taps_ref, wide_ref, False)

    def put(i, start, value):
        conv_ref[i, pl.ds(start, STEP), :] = value

    convolve(ext_ref, wide_ref, put, half, columns, 1)


def block_kernel(
    n_cols, lon_ref, lat_ref, early_ref, late_ref, wet_ref, wide, vec_ref, w1_ref, b1_ref, w2_ref,
    ext_in, conv_in, ext32, conv, dconv_ref, send_ref, later_ref, w1, w2,
):
    half, columns, lanes = wet_ref.shape
    chan = lanes // 2
    wide_e = w1_ref.shape[1]
    cells = later_ref.shape[0] // half
    odd = lon_ref[0] == 1
    one, two = early_ref[...].astype(f32), late_ref[...].astype(f32)
    left, right = jnp.where(odd, one, two), jnp.where(odd, two, one)
    for row in range(half + 2 * RIM):
        ext32[row, :RIM, :] = left[4 * row : 4 * row + RIM]
        ext32[row, RIM + n_cols : 2 * RIM + n_cols, :] = right[4 * row : 4 * row + RIM]

    def put(i, start, value):
        conv[i, pl.ds(start, STEP), :] = value

    for start in [0, *range((n_cols - RIM) // STEP * STEP, columns, STEP)]:
        convolve_tile(ext32, wide, put, half, start)
    w1[...] = jnp.zeros_like(w1)
    w2[...] = jnp.zeros_like(w2)
    w1[:chan, :wide_e] = w1_ref[...]
    w1[chan:, wide_e:] = w1_ref[...]
    w2[:chan, :wide_e] = w2_ref[...]
    w2[chan:, wide_e:] = w2_ref[...]
    dconv_ref[...] = jnp.zeros_like(dconv_ref)

    row_half = lax.broadcasted_iota(jnp.int32, (2 * lanes, lanes), 0) % lanes >= chan
    col_half = lax.broadcasted_iota(jnp.int32, (2 * lanes, lanes), 1) >= chan
    ones = jnp.where(row_half == col_half, 1.0 / chan, 0.0).astype(bf16)
    conv_bias, gain, bias = vec_ref[0:1, :], vec_ref[1:2, :], vec_ref[2:3, :]

    cells_all = half * columns
    out = conv[...].reshape(cells_all, lanes) + conv_bias
    wet = wet_ref[...].reshape(cells_all, lanes)
    center = out - group_mean(out, ones)
    rstd = lax.rsqrt(group_mean(center * center, ones) + ln_eps)
    normed = center * rstd
    zed = (normed * gain + bias).astype(bf16)
    pre = jnp.dot(zed, w1[...], preferred_element_type=f32) + b1_ref[...]
    dact = jnp.dot(wet, w2[...], preferred_element_type=f32)
    phi = 0.5 + 0.5 * lax.erf(pre * root_half)
    act = (pre * phi).astype(bf16)
    dhid = (dact * (phi + pre * (jnp.exp(-0.5 * pre * pre) * inv_root_tau))).astype(bf16)
    dzed = lax.dot_general(dhid, w1[...], (((1,), (1,)), ((), ())), preferred_element_type=f32)
    rows_first = (((0,), (0,)), ((), ()))
    expand = lax.dot_general(zed, dhid, rows_first, preferred_element_type=f32)
    project = lax.dot_general(wet, act, rows_first, preferred_element_type=f32)
    dnorm = dzed * gain
    mean1 = group_mean(dnorm, ones)
    mean2 = group_mean(dnorm * normed, ones)
    dconv = rstd * (dnorm - mean1 - normed * mean2)
    hidden = jnp.sum(dhid.astype(f32), axis=0, keepdims=True)
    parts = (wet.astype(f32), dzed * normed, dzed, dconv)
    small = [jnp.sum(part, axis=0, keepdims=True) for part in parts]
    dconv = dconv.reshape(half, columns, lanes)
    conv[...] = dconv
    dconv_ref[:, pl.ds(RIM, columns), :] = dconv

    rows = []
    for block in (expand, project):
        total = block[:chan, :wide_e] + block[chan:, wide_e:]
        rows += [total[:, k * lanes : (k + 1) * lanes] for k in range(wide_e // lanes)]
    total = hidden[:, :wide_e] + hidden[:, wide_e:]
    fine = [total[:, k * lanes : (k + 1) * lanes] for k in range(wide_e // lanes)] + small
    fine.append(jnp.zeros((-len(fine) % 8, lanes), f32))
    rows = jnp.concatenate(rows + fine + tap_sums(ext32, conv), axis=0)
    send_ref[: rows.shape[0]] = rows.astype(bf16)

    pad = jnp.zeros((cells - RIM, lanes), f32)
    first = [x for i in range(half) for x in (conv[i, :RIM, :], pad)]
    last = [x for i in range(half) for x in (conv[i, n_cols - RIM : n_cols, :], pad)]
    first = jnp.concatenate(first, axis=0)
    last = jnp.concatenate(last, axis=0)
    odd = lon_ref[0] == 1
    send_ref[rows.shape[0] :] = jnp.where(odd, first, last).astype(bf16)
    later_ref[...] = jnp.where(odd, last, first).astype(bf16)


def tap_sums(ext32, grad_ref):
    half, columns, lanes = grad_ref.shape

    def trip(t, carry):
        start = pl.multiple_of(t * 8, 8)
        total = list(carry)
        grads = [grad_ref[i, pl.ds(start, 8), :] for i in range(half)]
        for row in range(half + 2 * RIM):
            for b in range(TAPS):
                piece = ext32[row, pl.ds(start + b, 8), :]
                for i in range(half):
                    a = row - i
                    if 0 <= a < TAPS:
                        total[a * TAPS + b] = total[a * TAPS + b] + grads[i] * piece
        return tuple(total)

    zero = jnp.zeros((8, lanes), f32)
    total = lax.fori_loop(0, columns // 8, trip, (zero,) * (TAPS * TAPS))
    rows = []
    for a in range(TAPS):
        rows += [jnp.sum(total[a * TAPS + b], axis=0, keepdims=True) for b in range(TAPS)]
        rows.append(jnp.zeros((1, lanes), f32))
    return rows


def add_kernel(total, mine_ref, other_ref, later_ref, send_ref):
    send_ref[:total] = added(mine_ref, other_ref, total).astype(bf16)
    send_ref[total:] = later_ref[...]


def rows_kernel(
    n_total, n_cols, lon_ref, lat_ref, mine_ref, other_ref, early_ref, dconv_ref,
    keep_ref, send_ref, later_ref, full_ref,
):
    half, wide, lanes = dconv_ref.shape
    odd_lon, odd_lat = lon_ref[0] == 1, lat_ref[0] == 1
    total = added(mine_ref, other_ref, n_total)
    part = n_total // 2
    keep_ref[...] = jnp.where(odd_lat, total[part:], total[:part])
    high, low = split(jnp.where(odd_lat, total[:part], total[part:]))
    send_ref[:part] = high
    send_ref[part : 2 * part] = low
    early = early_ref[n_total:].astype(f32)
    late = other_ref[n_total:].astype(f32)
    right = jnp.where(odd_lon, late, early)
    left = jnp.where(odd_lon, early, late)
    step = early.shape[0] // half
    for i in range(half):
        full_ref[i] = dconv_ref[i]
        full_ref[i, :RIM, :] = left[i * step : i * step + RIM]
        full_ref[i, RIM + n_cols : 2 * RIM + n_cols, :] = right[i * step : i * step + RIM]
    mid = wide // 2
    first = lax.broadcasted_iota(jnp.int32, (mid, lanes), 1) < lanes // 2
    at = 2 * part
    for k in range(RIM):
        upper = full_ref[k]
        lower = full_ref[half - RIM + k]
        upper = jnp.where(first, upper[:mid], swap(upper[mid:]))
        lower = jnp.where(first, swap(lower[:mid]), lower[mid:])
        send_ref[at + k * mid : at + (k + 1) * mid, :] = jnp.where(odd_lat, upper, lower).astype(bf16)
        later_ref[k * mid : (k + 1) * mid, :] = jnp.where(odd_lat, lower, upper).astype(bf16)


def rim_rows(lat_ref, early_ref, late_ref, at):
    mid = late_ref.shape[0] // RIM
    odd = lat_ref[0] == 1

    def rows(k):
        early = early_ref[at + k * mid : at + (k + 1) * mid, :].astype(f32)
        return early, late_ref[k * mid : (k + 1) * mid, :].astype(f32)

    def top(k):
        early, late = rows(k)
        return jnp.where(odd, early, late)

    def bottom(k):
        early, late = rows(k)
        return jnp.where(odd, late, early)

    return top, bottom


def back_kernel(at, lat_ref, early_ref, late_ref, mid_ref, taps_ref, out_ref, ext32, wide):
    half, columns, lanes = out_ref.shape
    assemble(ext32, mid_ref, *rim_rows(lat_ref, early_ref, late_ref, at))
    fill_taps(taps_ref, wide, True)

    def put(i, start, value):
        out_ref[i, pl.ds(start, STEP), :] = value

    convolve(ext32, wide, put, half, columns, 1)


def finish_kernel(
    scale, lat_ref, mine_ref, other_ref,
    taps_ref, conv_ref, gain_ref, bias_ref, expand_ref, hidden_ref, project_ref, wet_ref,
):
    lanes = mine_ref.shape[1]
    chan, wide_e = expand_ref.shape
    odd = lat_ref[0] == 1
    mine, other = mine_ref[...] * scale, other_ref[...] * scale
    total = jnp.concatenate([jnp.where(odd, other, mine), jnp.where(odd, mine, other)], axis=0)
    blocks = wide_e // lanes
    small = total[2 * blocks * chan :]
    for k in range(blocks):
        expand_ref[:, k * lanes : (k + 1) * lanes] = total[k * chan : (k + 1) * chan]
        at = (blocks + k) * chan
        project_ref[:, k * lanes : (k + 1) * lanes] = total[at : at + chan]
        hidden_ref[:, k * lanes : (k + 1) * lanes] = small[k : k + 1]
    narrow = small[:, :chan] + small[:, chan:]
    for k, ref in enumerate((wet_ref, gain_ref, bias_ref, conv_ref)):
        ref[...] = narrow[blocks + k : blocks + k + 1]
    at = small.shape[0] - 8 * TAPS
    for a in range(TAPS):
        taps_ref[a] = narrow[at + 8 * a : at + 8 * a + TAPS]


def call(kernel, out_shape, scratch, flops, *args, aliases={}):
    vmem = pl.BlockSpec(memory_space=pltpu.VMEM)
    smem = pl.BlockSpec(memory_space=pltpu.SMEM)
    many = isinstance(out_shape, (list, tuple))
    return pl.pallas_call(
        kernel,
        out_shape=out_shape,
        in_specs=[smem if arg.dtype == jnp.int32 else vmem for arg in args],
        out_specs=[vmem] * len(out_shape) if many else vmem,
        scratch_shapes=scratch,
        input_output_aliases=aliases,
        cost_estimate=pl.CostEstimate(flops=flops, bytes_accessed=1 << 20, transcendentals=0),
        compiler_params=pltpu.CompilerParams(vmem_limit_bytes=40 << 20),
    )(*args)


def body(
    state, land_sea, cotangent, kernel, conv_bias, ln_gain, ln_bias, w_expand, b_expand, w_project
):
    n_chan, n_rows, n_cols = state.shape
    n_wide = w_expand.shape[1]
    half = n_rows // 2
    lanes = 2 * n_chan
    columns = -(-n_cols // STEP) * STEP
    padded = -(-(columns + 2 * RIM) // 32) * 32
    total = 2 * n_chan * n_wide // lanes + -(-(n_wide // lanes + 4) // 8) * 8 + 8 * TAPS
    part = total // 2
    rim = half * 4
    rows = RIM * padded // 2
    cells = n_rows * n_cols
    conv_flops = cells * n_chan * TAPS * TAPS * 2
    shaped = jax.ShapeDtypeStruct
    taps = kernel.transpose(1, 2, 0).reshape(TAPS * TAPS, n_chan)
    twice = lambda v: jnp.concatenate([v, v])
    vectors = jnp.stack([twice(conv_bias), twice(ln_gain), twice(ln_bias)])
    odd_lon, odd_lat = lax.axis_index("lon") % 2, lax.axis_index("lat") % 2
    scalars = (odd_lon.reshape(1), odd_lat.reshape(1))

    field = pack(state.transpose(1, 2, 0))
    field = jnp.pad(field, ((0, 0), (RIM, padded - n_cols - RIM), (0, 0)))
    first, last = dense(field[:RIM, :, :n_chan]), dense(field[-RIM:, :, n_chan:])
    flat = (rows, lanes)
    early = lax.ppermute(
        jnp.where(odd_lat == 1, first, last).reshape(flat), "lat", pairs("lat", 1)
    )
    late = lax.ppermute(
        jnp.where(odd_lat == 1, last, first).reshape(flat), "lat", ring_pairs("lat", False)
    )
    side = shaped((4 * (half + 2 * RIM), lanes), bf16)
    first, last = call(
        functools.partial(edge_kernel, n_cols), [side, side], [], cells, *scalars, field, early, late
    )
    before = lax.ppermute(first, "lon", pairs("lon", 1))
    after = lax.ppermute(last, "lon", ring_pairs("lon", True))
    ext, conv, wide_taps = call(
        inner_kernel,
        [
            shaped((half + 2 * RIM, padded, lanes), f32),
            shaped((half, columns, lanes), f32),
            shaped((TAPS * TAPS, 8, lanes), f32),
        ],
        [],
        conv_flops,
        scalars[1], field, early, late, taps,
    )

    wet = cotangent * land_sea[None].astype(bf16)
    wet = jnp.pad(wet.transpose(1, 2, 0), ((0, 0), (0, columns - n_cols), (0, 0)))

    _, _, dconv, mine, later = call(
        functools.partial(block_kernel, n_cols),
        [
            shaped(ext.shape, f32),
            shaped(conv.shape, f32),
            shaped((half, padded, lanes), f32),
            shaped((total + rim, lanes), bf16),
            shaped((rim, lanes), bf16),
        ],
        [
            pltpu.VMEM((lanes, 2 * n_wide), bf16),
            pltpu.VMEM((lanes, 2 * n_wide), bf16),
        ],
        cells * n_chan * n_wide * 10 + conv_flops,
        *scalars, before, after, pack(wet), wide_taps, vectors, w_expand,
        twice(b_expand).reshape(1, -1), w_project.T, ext, conv,
        aliases={10: 0, 11: 1},
    )

    early = lax.ppermute(mine, "lon", pairs("lon", 1))
    other = early
    for bit in bits("lon", 2) + [0]:
        add = functools.partial(add_kernel, total)
        sent = shaped((total + rim, lanes), bf16)
        mine = call(add, sent, [], total * lanes, mine, other, later)
        if bit:
            other = lax.ppermute(mine, "lon", pairs("lon", bit))
    other = lax.ppermute(mine, "lon", ring_pairs("lon", True))
    mine, send, later, full = call(
        functools.partial(rows_kernel, total, n_cols),
        [
            shaped((part, lanes), f32),
            shaped((2 * part + rows, lanes), bf16),
            shaped((rows, lanes), bf16),
            shaped(dconv.shape, f32),
        ],
        [],
        total * lanes,
        *scalars, mine, other, early, dconv,
    )
    early = lax.ppermute(send, "lat", pairs("lat", 1))
    late = lax.ppermute(later, "lat", ring_pairs("lat", False))
    mine = mine + early[:part].astype(f32) + early[part : 2 * part].astype(f32)
    for k, swaps in enumerate(split_rounds()):
        other = lax.ppermute(mine, "lat", swaps)
        if k == 0:
            other, late = lax.optimization_barrier((other, late))
        mine = mine + other
    other = lax.ppermute(mine, "lat", pairs("lat", 1))

    grad = call(
        functools.partial(back_kernel, 2 * part),
        shaped((half, columns, lanes), f32),
        [
            pltpu.VMEM((half + 2 * RIM, padded, lanes), f32),
            pltpu.VMEM((TAPS * TAPS, 8, lanes), f32),
        ],
        conv_flops,
        scalars[1], early, late, full, taps,
    )
    grad = unpack(grad)[:, :n_cols].transpose(2, 0, 1)
    state_grad = (cotangent.astype(f32) + grad).astype(bf16)

    scale = 1.0 / math.sqrt(cells * lax.axis_size("lat") * lax.axis_size("lon"))
    narrow = shaped((1, n_chan), f32)
    out = call(
        functools.partial(finish_kernel, scale),
        [
            shaped((TAPS, TAPS, n_chan), f32),
            narrow,
            narrow,
            narrow,
            shaped((n_chan, n_wide), f32),
            shaped((1, n_wide), f32),
            shaped((n_chan, n_wide), f32),
            narrow,
        ],
        [],
        total * lanes,
        scalars[1], mine, other,
    )
    return (
        state_grad,
        out[0].transpose(2, 0, 1),
        out[1].reshape(-1),
        out[2].reshape(-1),
        out[3].reshape(-1),
        out[4],
        out[5].reshape(-1),
        out[6].T,
        out[7].reshape(-1),
    )


def solution(mesh):
    in_specs = (
        P(None, "lat", "lon"),
        P("lat", "lon"),
        P(None, "lat", "lon"),
        P(),
        P(),
        P(),
        P(),
        P(),
        P(),
        P(),
    )
    out_specs = (P(None, "lat", "lon"), P(), P(), P(), P(), P(), P(), P(), P())
    return jax.shard_map(body, mesh=mesh, in_specs=in_specs, out_specs=out_specs, check_vma=False)
```

```python
import functools
import math

import jax
import jax.numpy as jnp
from jax import lax
from jax.experimental import pallas as pl
from jax.experimental.pallas import tpu as pltpu
from jax.sharding import PartitionSpec as P

TAPS = 7
RIM = 3
STEP = 16

ln_eps = 1e-06
root_half = 0.7071067811865476
inv_root_tau = 0.3989422804014327
f32 = jnp.float32
bf16 = jnp.bfloat16


def pairs(axis, bit):
    return [(i, i ^ bit) for i in range(lax.axis_size(axis))]


def ring_pairs(axis):
    size = lax.axis_size(axis)
    return [(i, (i + 1 if i % 2 else i - 1) % size) for i in range(size)]


def bits(axis, first):
    size = lax.axis_size(axis)
    if size < 4 or size & (size - 1):
        raise ValueError("axis size")
    return [1 << k for k in range(first, size.bit_length() - 1)]


def kept_half():
    place = lax.axis_index("lat")
    return sum(place // bit for bit in [1] + bits("lat", 1)) % 2


def half_rounds():
    steps = bits("lat", 1)
    turned = steps[1:] + steps[:1]
    size = lax.axis_size("lat")
    order = [turned if bin(i).count("1") % 2 else steps for i in range(size)]
    return [[(i, i ^ order[i][k] ^ 1) for i in range(size)] for k in range(len(steps))]


def pack(field):
    half = field.shape[0] // 2
    return jnp.concatenate([field[:half], field[half:]], axis=2)


def unpack(field):
    chan = field.shape[2] // 2
    return jnp.concatenate([field[:, :, :chan], field[:, :, chan:]], axis=0)


def dense(rows):
    half = rows.shape[1] // 2
    return jnp.concatenate([rows[:, :half], rows[:, half:]], axis=2)


def swap(value):
    return pltpu.roll(value, value.shape[-1] // 2, value.ndim - 1)


def assemble(ext_ref, mid_ref, top, bottom):
    half, columns, lanes = mid_ref.shape
    first = lax.broadcasted_iota(jnp.int32, (columns, lanes), 1) < lanes // 2
    for k in range(RIM):
        above, below = top(k), bottom(k)
        above = jnp.concatenate([above, swap(above)], axis=0)
        below = jnp.concatenate([swap(below), below], axis=0)
        upper = swap(mid_ref[half - RIM + k].astype(f32))
        lower = swap(mid_ref[k].astype(f32))
        ext_ref[k] = jnp.where(first, above, upper)
        ext_ref[half + RIM + k] = jnp.where(first, lower, below)
    for i in range(half):
        ext_ref[RIM + i] = mid_ref[i].astype(f32)


def split(value):
    high = value.astype(bf16)
    return high, (value - high.astype(f32)).astype(bf16)


def added(mine_ref, other_ref, total):
    return mine_ref[:total].astype(f32) + other_ref[:total].astype(f32)


def fill_taps(taps_ref, wide_ref, flip):
    count, chan = taps_ref.shape
    for tap in range(count):
        row = taps_ref[count - 1 - tap if flip else tap, :].reshape(1, chan)
        wide_ref[tap] = jnp.broadcast_to(jnp.concatenate([row, row], axis=1), (8, 2 * chan))


def convolve_tile(ext_ref, wide_ref, store, half, start):
    tiles = STEP // 8
    total = [[None] * tiles for _ in range(half)]
    for row in range(half + 2 * RIM):
        for b in range(TAPS):
            piece = [ext_ref[row, pl.ds(start + b + 8 * s, 8), :] for s in range(tiles)]
            for i in range(half):
                a = row - i
                if 0 <= a < TAPS:
                    weight = wide_ref[a * TAPS + b]
                    for s in range(tiles):
                        term = weight * piece[s]
                        total[i][s] = term if total[i][s] is None else total[i][s] + term
    for i in range(half):
        store(i, start, jnp.concatenate(total[i], axis=0))


def convolve(ext_ref, wide_ref, store, half, columns, unroll):
    def trip(t, carry):
        convolve_tile(ext_ref, wide_ref, store, half, pl.multiple_of(t * STEP, STEP))
        return carry

    lax.fori_loop(0, columns // STEP, trip, 0, unroll=unroll)


def group_mean(values, ones):
    high = values.astype(bf16)
    low = (values - high.astype(f32)).astype(bf16)
    return jnp.dot(jnp.concatenate([high, low], axis=1), ones, preferred_element_type=f32)


def edge_kernel(n_cols, lon_ref, lat_ref, pole_ref, mid_ref, early_ref, late_ref, send_ref, later_ref):
    half, wide, lanes = mid_ref.shape
    mid = wide // 2
    odd_lat, odd_lon, pole = lat_ref[0] == 1, lon_ref[0] == 1, pole_ref[0] == 1
    base = n_cols // 16 * 16
    skip = n_cols - base
    first = lax.broadcasted_iota(jnp.int32, (8, lanes), 1) < lanes // 2
    left, right = [], []
    for i in range(half):
        left.append(mid_ref[i, :16, :].astype(f32)[:8])
        right.append(mid_ref[i, base : base + 32, :].astype(f32)[skip : skip + 8])
    ends = [([], []), ([], [])]
    for k in range(RIM):
        at = k * mid
        one, two = [], []
        for ref in (early_ref, late_ref):
            one.append(ref[at : at + 16, :].astype(f32)[:8])
            two.append(ref[at + base - mid : at + mid, :].astype(f32)[skip : skip + 8])
        one[1], two[1] = jnp.where(pole, 0.0, one[1]), jnp.where(pole, 0.0, two[1])
        above = jnp.where(odd_lat, one[0], one[1]), jnp.where(odd_lat, two[0], two[1])
        below = jnp.where(odd_lat, one[1], one[0]), jnp.where(odd_lat, two[1], two[0])
        ends[0][0].append(jnp.where(first, above[0], swap(left[half - RIM + k])))
        ends[0][1].append(jnp.where(first, swap(above[1]), swap(right[half - RIM + k])))
        ends[1][0].append(jnp.where(first, swap(left[k]), swap(below[0])))
        ends[1][1].append(jnp.where(first, swap(right[k]), below[1]))
    left = ends[0][0] + left + ends[1][0]
    right = ends[0][1] + right + ends[1][1]
    left = jnp.concatenate([x[RIM : RIM + 4] for x in left], axis=0)
    right = jnp.concatenate([x[:4] for x in right], axis=0)
    send_ref[...] = jnp.where(odd_lon, left, right).astype(bf16)
    later_ref[...] = jnp.where(odd_lon, right, left).astype(bf16)


def inner_kernel(lat_ref, pole_ref, mid_ref, early_ref, late_ref, taps_ref, ext_ref, conv_ref, wide_ref):
    half, columns, lanes = conv_ref.shape
    assemble(ext_ref, mid_ref, *rim_rows(lat_ref, pole_ref, early_ref, late_ref, 0))
    fill_taps(taps_ref, wide_ref, False)

    def put(i, start, value):
        conv_ref[i, pl.ds(start, STEP), :] = value

    convolve(ext_ref, wide_ref, put, half, columns, 1)


def block_kernel(
    n_cols, lon_ref, early_ref, late_ref, wet_ref, wide, vec_ref, w1_ref, b1_ref, w2_ref,
    ext_in, conv_in, ext32, conv, dconv_ref, send_ref, later_ref, w1, w2,
):
    half, columns, lanes = wet_ref.shape
    chan = lanes // 2
    wide_e = w1_ref.shape[1]
    cells = later_ref.shape[0] // half
    odd = lon_ref[0] == 1
    one, two = early_ref[...].astype(f32), late_ref[...].astype(f32)
    left, right = jnp.where(odd, one, two), jnp.where(odd, two, one)
    for row in range(half + 2 * RIM):
        ext32[row, :RIM, :] = left[4 * row : 4 * row + RIM]
        ext32[row, RIM + n_cols : 2 * RIM + n_cols, :] = right[4 * row : 4 * row + RIM]

    def put(i, start, value):
        conv[i, pl.ds(start, STEP), :] = value

    for start in [0, *range((n_cols - RIM) // STEP * STEP, columns, STEP)]:
        convolve_tile(ext32, wide, put, half, start)
    w1[...] = jnp.zeros_like(w1)
    w2[...] = jnp.zeros_like(w2)
    w1[:chan, :wide_e] = w1_ref[...]
    w1[chan:, wide_e:] = w1_ref[...]
    w2[:chan, :wide_e] = w2_ref[...]
    w2[chan:, wide_e:] = w2_ref[...]
    dconv_ref[...] = jnp.zeros_like(dconv_ref)

    row_half = lax.broadcasted_iota(jnp.int32, (2 * lanes, lanes), 0) % lanes >= chan
    col_half = lax.broadcasted_iota(jnp.int32, (2 * lanes, lanes), 1) >= chan
    ones = jnp.where(row_half == col_half, 1.0 / chan, 0.0).astype(bf16)
    conv_bias, gain, bias = vec_ref[0:1, :], vec_ref[1:2, :], vec_ref[2:3, :]

    cells_all = half * columns
    out = conv[...].reshape(cells_all, lanes) + conv_bias
    wet = wet_ref[...].reshape(cells_all, lanes)
    center = out - group_mean(out, ones)
    rstd = lax.rsqrt(group_mean(center * center, ones) + ln_eps)
    normed = center * rstd
    zed = (normed * gain + bias).astype(bf16)
    pre = jnp.dot(zed, w1[...], preferred_element_type=f32) + b1_ref[...]
    dact = jnp.dot(wet, w2[...], preferred_element_type=f32)
    phi = 0.5 + 0.5 * lax.erf(pre * root_half)
    act = (pre * phi).astype(bf16)
    dhid = (dact * (phi + pre * (jnp.exp(-0.5 * pre * pre) * inv_root_tau))).astype(bf16)
    dzed = lax.dot_general(dhid, w1[...], (((1,), (1,)), ((), ())), preferred_element_type=f32)
    rows_first = (((0,), (0,)), ((), ()))
    expand = lax.dot_general(zed, dhid, rows_first, preferred_element_type=f32)
    project = lax.dot_general(wet, act, rows_first, preferred_element_type=f32)
    dnorm = dzed * gain
    mean1 = group_mean(dnorm, ones)
    mean2 = group_mean(dnorm * normed, ones)
    dconv = rstd * (dnorm - mean1 - normed * mean2)
    hidden = jnp.sum(dhid.astype(f32), axis=0, keepdims=True)
    parts = (wet.astype(f32), dzed * normed, dzed, dconv)
    small = [jnp.sum(part, axis=0, keepdims=True) for part in parts]
    dconv = dconv.reshape(half, columns, lanes)
    conv[...] = dconv
    dconv_ref[:, pl.ds(RIM, columns), :] = dconv

    rows = []
    for block in (expand, project):
        total = block[:chan, :wide_e] + block[chan:, wide_e:]
        rows += [total[:, k * lanes : (k + 1) * lanes] for k in range(wide_e // lanes)]
    total = hidden[:, :wide_e] + hidden[:, wide_e:]
    fine = [total[:, k * lanes : (k + 1) * lanes] for k in range(wide_e // lanes)] + small
    fine.append(jnp.zeros((-len(fine) % 8, lanes), f32))
    rows = jnp.concatenate(rows + fine + tap_sums(ext32, conv), axis=0)
    send_ref[: rows.shape[0]] = rows.astype(bf16)

    pad = jnp.zeros((cells - RIM, lanes), f32)
    first = [x for i in range(half) for x in (conv[i, :RIM, :], pad)]
    last = [x for i in range(half) for x in (conv[i, n_cols - RIM : n_cols, :], pad)]
    first = jnp.concatenate(first, axis=0)
    last = jnp.concatenate(last, axis=0)
    odd = lon_ref[0] == 1
    send_ref[rows.shape[0] :] = jnp.where(odd, first, last).astype(bf16)
    later_ref[...] = jnp.where(odd, last, first).astype(bf16)


def tap_sums(ext32, grad_ref):
    half, columns, lanes = grad_ref.shape

    def trip(t, carry):
        start = pl.multiple_of(t * 8, 8)
        total = list(carry)
        grads = [grad_ref[i, pl.ds(start, 8), :] for i in range(half)]
        for row in range(half + 2 * RIM):
            for b in range(TAPS):
                piece = ext32[row, pl.ds(start + b, 8), :]
                for i in range(half):
                    a = row - i
                    if 0 <= a < TAPS:
                        total[a * TAPS + b] = total[a * TAPS + b] + grads[i] * piece
        return tuple(total)

    zero = jnp.zeros((8, lanes), f32)
    total = lax.fori_loop(0, columns // 8, trip, (zero,) * (TAPS * TAPS))
    rows = []
    for a in range(TAPS):
        rows += [jnp.sum(total[a * TAPS + b], axis=0, keepdims=True) for b in range(TAPS)]
        rows.append(jnp.zeros((1, lanes), f32))
    return rows


def add_kernel(total, mine_ref, other_ref, later_ref, send_ref):
    send_ref[:total] = added(mine_ref, other_ref, total).astype(bf16)
    send_ref[total:] = later_ref[...]


def rows_kernel(
    n_total, n_cols, lon_ref, lat_ref, half_ref, mine_ref, other_ref, early_ref, dconv_ref,
    keep_ref, send_ref, later_ref, full_ref,
):
    half, wide, lanes = dconv_ref.shape
    odd_lon, odd_lat, upper_half = lon_ref[0] == 1, lat_ref[0] == 1, half_ref[0] == 1
    total = added(mine_ref, other_ref, n_total)
    part = n_total // 2
    keep_ref[...] = jnp.where(upper_half, total[part:], total[:part])
    high, low = split(jnp.where(upper_half, total[:part], total[part:]))
    send_ref[:part] = high
    send_ref[part : 2 * part] = low
    early = early_ref[n_total:].astype(f32)
    late = other_ref[n_total:].astype(f32)
    right = jnp.where(odd_lon, late, early)
    left = jnp.where(odd_lon, early, late)
    step = early.shape[0] // half
    for i in range(half):
        full_ref[i] = dconv_ref[i]
        full_ref[i, :RIM, :] = left[i * step : i * step + RIM]
        full_ref[i, RIM + n_cols : 2 * RIM + n_cols, :] = right[i * step : i * step + RIM]
    mid = wide // 2
    first = lax.broadcasted_iota(jnp.int32, (mid, lanes), 1) < lanes // 2
    at = 2 * part
    for k in range(RIM):
        upper = full_ref[k]
        lower = full_ref[half - RIM + k]
        upper = jnp.where(first, upper[:mid], swap(upper[mid:]))
        lower = jnp.where(first, swap(lower[:mid]), lower[mid:])
        send_ref[at + k * mid : at + (k + 1) * mid, :] = jnp.where(odd_lat, upper, lower).astype(bf16)
        later_ref[k * mid : (k + 1) * mid, :] = jnp.where(odd_lat, lower, upper).astype(bf16)


def rim_rows(lat_ref, pole_ref, early_ref, late_ref, at):
    mid = late_ref.shape[0] // RIM
    odd, pole = lat_ref[0] == 1, pole_ref[0] == 1

    def rows(k):
        early = early_ref[at + k * mid : at + (k + 1) * mid, :].astype(f32)
        late = late_ref[k * mid : (k + 1) * mid, :].astype(f32)
        return early, jnp.where(pole, 0.0, late)

    def top(k):
        early, late = rows(k)
        return jnp.where(odd, early, late)

    def bottom(k):
        early, late = rows(k)
        return jnp.where(odd, late, early)

    return top, bottom


def back_kernel(at, lat_ref, pole_ref, early_ref, late_ref, mid_ref, taps_ref, out_ref, ext32, wide):
    half, columns, lanes = out_ref.shape
    assemble(ext32, mid_ref, *rim_rows(lat_ref, pole_ref, early_ref, late_ref, at))
    fill_taps(taps_ref, wide, True)

    def put(i, start, value):
        out_ref[i, pl.ds(start, STEP), :] = value

    convolve(ext32, wide, put, half, columns, 1)


def finish_kernel(
    scale, half_ref, mine_ref, other_ref,
    taps_ref, conv_ref, gain_ref, bias_ref, expand_ref, hidden_ref, project_ref, wet_ref,
):
    lanes = mine_ref.shape[1]
    chan, wide_e = expand_ref.shape
    odd = half_ref[0] == 1
    mine, other = mine_ref[...] * scale, other_ref[...] * scale
    total = jnp.concatenate([jnp.where(odd, other, mine), jnp.where(odd, mine, other)], axis=0)
    blocks = wide_e // lanes
    small = total[2 * blocks * chan :]
    for k in range(blocks):
        expand_ref[:, k * lanes : (k + 1) * lanes] = total[k * chan : (k + 1) * chan]
        at = (blocks + k) * chan
        project_ref[:, k * lanes : (k + 1) * lanes] = total[at : at + chan]
        hidden_ref[:, k * lanes : (k + 1) * lanes] = small[k : k + 1]
    narrow = small[:, :chan] + small[:, chan:]
    for k, ref in enumerate((wet_ref, gain_ref, bias_ref, conv_ref)):
        ref[...] = narrow[blocks + k : blocks + k + 1]
    at = small.shape[0] - 8 * TAPS
    for a in range(TAPS):
        taps_ref[a] = narrow[at + 8 * a : at + 8 * a + TAPS]


def call(kernel, out_shape, scratch, flops, *args, aliases={}):
    vmem = pl.BlockSpec(memory_space=pltpu.VMEM)
    smem = pl.BlockSpec(memory_space=pltpu.SMEM)
    many = isinstance(out_shape, (list, tuple))
    return pl.pallas_call(
        kernel,
        out_shape=out_shape,
        in_specs=[smem if arg.dtype == jnp.int32 else vmem for arg in args],
        out_specs=[vmem] * len(out_shape) if many else vmem,
        scratch_shapes=scratch,
        input_output_aliases=aliases,
        cost_estimate=pl.CostEstimate(flops=flops, bytes_accessed=1 << 20, transcendentals=0),
        compiler_params=pltpu.CompilerParams(vmem_limit_bytes=40 << 20),
    )(*args)


def body(
    state, land_sea, cotangent, kernel, conv_bias, ln_gain, ln_bias, w_expand, b_expand, w_project
):
    n_chan, n_rows, n_cols = state.shape
    n_wide = w_expand.shape[1]
    half = n_rows // 2
    lanes = 2 * n_chan
    columns = -(-n_cols // STEP) * STEP
    padded = -(-(columns + 2 * RIM) // 32) * 32
    total = 2 * n_chan * n_wide // lanes + -(-(n_wide // lanes + 4) // 8) * 8 + 8 * TAPS
    part = total // 2
    rim = half * 4
    rows = RIM * padded // 2
    cells = n_rows * n_cols
    conv_flops = cells * n_chan * TAPS * TAPS * 2
    shaped = jax.ShapeDtypeStruct
    taps = kernel.transpose(1, 2, 0).reshape(TAPS * TAPS, n_chan)
    twice = lambda v: jnp.concatenate([v, v])
    vectors = jnp.stack([twice(conv_bias), twice(ln_gain), twice(ln_bias)])
    odd_lon, odd_lat = lax.axis_index("lon") % 2, lax.axis_index("lat") % 2
    place, last_place = lax.axis_index("lat"), lax.axis_size("lat") - 1
    pole = ((place == 0) | (place == last_place)).astype(jnp.int32).reshape(1)
    on_lon, on_lat, keeps = odd_lon.reshape(1), odd_lat.reshape(1), kept_half().reshape(1)

    field = pack(state.transpose(1, 2, 0))
    field = jnp.pad(field, ((0, 0), (RIM, padded - n_cols - RIM), (0, 0)))
    first, last = dense(field[:RIM, :, :n_chan]), dense(field[-RIM:, :, n_chan:])
    flat = (rows, lanes)
    early = lax.ppermute(
        jnp.where(odd_lat == 1, first, last).reshape(flat), "lat", pairs("lat", 1)
    )
    late = lax.ppermute(
        jnp.where(odd_lat == 1, last, first).reshape(flat), "lat", ring_pairs("lat")
    )
    side = shaped((4 * (half + 2 * RIM), lanes), bf16)
    first, last = call(
        functools.partial(edge_kernel, n_cols), [side, side], [], cells,
        on_lon, on_lat, pole, field, early, late,
    )
    before = lax.ppermute(first, "lon", pairs("lon", 1))
    after = lax.ppermute(last, "lon", ring_pairs("lon"))
    ext, conv, wide_taps = call(
        inner_kernel,
        [
            shaped((half + 2 * RIM, padded, lanes), f32),
            shaped((half, columns, lanes), f32),
            shaped((TAPS * TAPS, 8, lanes), f32),
        ],
        [],
        conv_flops,
        on_lat, pole, field, early, late, taps,
    )

    wet = cotangent * land_sea[None].astype(bf16)
    wet = jnp.pad(wet.transpose(1, 2, 0), ((0, 0), (0, columns - n_cols), (0, 0)))

    _, _, dconv, mine, later = call(
        functools.partial(block_kernel, n_cols),
        [
            shaped(ext.shape, f32),
            shaped(conv.shape, f32),
            shaped((half, padded, lanes), f32),
            shaped((total + rim, lanes), bf16),
            shaped((rim, lanes), bf16),
        ],
        [
            pltpu.VMEM((lanes, 2 * n_wide), bf16),
            pltpu.VMEM((lanes, 2 * n_wide), bf16),
        ],
        cells * n_chan * n_wide * 10 + conv_flops,
        on_lon, before, after, pack(wet), wide_taps, vectors, w_expand,
        twice(b_expand).reshape(1, -1), w_project.T, ext, conv,
        aliases={9: 0, 10: 1},
    )

    early = lax.ppermute(mine, "lon", pairs("lon", 1))
    other = early
    for bit in bits("lon", 2) + [0]:
        add = functools.partial(add_kernel, total)
        sent = shaped((total + rim, lanes), bf16)
        mine = call(add, sent, [], total * lanes, mine, other, later)
        if bit:
            other = lax.ppermute(mine, "lon", pairs("lon", bit))
    other = lax.ppermute(mine, "lon", ring_pairs("lon"))
    mine, send, later, full = call(
        functools.partial(rows_kernel, total, n_cols),
        [
            shaped((part, lanes), f32),
            shaped((2 * part + rows, lanes), bf16),
            shaped((rows, lanes), bf16),
            shaped(dconv.shape, f32),
        ],
        [],
        total * lanes,
        on_lon, on_lat, keeps, mine, other, early, dconv,
    )
    early = lax.ppermute(send, "lat", pairs("lat", 1))
    late = lax.ppermute(later, "lat", ring_pairs("lat"))
    mine = mine + early[:part].astype(f32) + early[part : 2 * part].astype(f32)
    for k, swaps in enumerate(half_rounds()):
        other = lax.ppermute(mine, "lat", swaps)
        if k == 0:
            other, late = lax.optimization_barrier((other, late))
        mine = mine + other
    other = lax.ppermute(mine, "lat", pairs("lat", 1))

    grad = call(
        functools.partial(back_kernel, 2 * part),
        shaped((half, columns, lanes), f32),
        [
            pltpu.VMEM((half + 2 * RIM, padded, lanes), f32),
            pltpu.VMEM((TAPS * TAPS, 8, lanes), f32),
        ],
        conv_flops,
        on_lat, pole, early, late, full, taps,
    )
    grad = unpack(grad)[:, :n_cols].transpose(2, 0, 1)
    state_grad = (cotangent.astype(f32) + grad).astype(bf16)

    scale = 1.0 / math.sqrt(cells * lax.axis_size("lat") * lax.axis_size("lon"))
    narrow = shaped((1, n_chan), f32)
    out = call(
        functools.partial(finish_kernel, scale),
        [
            shaped((TAPS, TAPS, n_chan), f32),
            narrow,
            narrow,
            narrow,
            shaped((n_chan, n_wide), f32),
            shaped((1, n_wide), f32),
            shaped((n_chan, n_wide), f32),
            narrow,
        ],
        [],
        total * lanes,
        keeps, mine, other,
    )
    return (
        state_grad,
        out[0].transpose(2, 0, 1),
        out[1].reshape(-1),
        out[2].reshape(-1),
        out[3].reshape(-1),
        out[4],
        out[5].reshape(-1),
        out[6].T,
        out[7].reshape(-1),
    )


def solution(mesh):
    in_specs = (
        P(None, "lat", "lon"),
        P("lat", "lon"),
        P(None, "lat", "lon"),
        P(),
        P(),
        P(),
        P(),
        P(),
        P(),
        P(),
    )
    out_specs = (P(None, "lat", "lon"), P(), P(), P(), P(), P(), P(), P(), P())
    return jax.shard_map(body, mesh=mesh, in_specs=in_specs, out_specs=out_specs, check_vma=False)
```

```python
import functools
import math

import jax
import jax.numpy as jnp
from jax import lax
from jax.experimental import pallas as pl
from jax.experimental.pallas import tpu as pltpu
from jax.sharding import PartitionSpec as P

TAPS = 7
RIM = 3
STEP = 16

ln_eps = 1e-06
root_half = 0.7071067811865476
inv_root_tau = 0.3989422804014327
f32 = jnp.float32
bf16 = jnp.bfloat16


def pairs(axis, bit):
    return [(i, i ^ bit) for i in range(lax.axis_size(axis))]


def ring_pairs(axis):
    size = lax.axis_size(axis)
    return [(i, (i + 1 if i % 2 else i - 1) % size) for i in range(size)]


def bits(axis, first):
    size = lax.axis_size(axis)
    if size < 4 or size & (size - 1):
        raise ValueError("axis size")
    return [1 << k for k in range(first, size.bit_length() - 1)]


def kept_half():
    place = lax.axis_index("lat")
    return sum(place // bit for bit in [1] + bits("lat", 1)) % 2


def half_rounds():
    steps = bits("lat", 1)
    turned = steps[1:] + steps[:1]
    size = lax.axis_size("lat")
    order = [turned if bin(i).count("1") % 2 else steps for i in range(size)]
    return [[(i, i ^ order[i][k] ^ 1) for i in range(size)] for k in range(len(steps))]


def unpack(field):
    chan = field.shape[2] // 2
    return jnp.concatenate([field[:, :, :chan], field[:, :, chan:]], axis=0)


def swap(value):
    return pltpu.roll(value, value.shape[-1] // 2, value.ndim - 1)


def assemble(ext_ref, mid_ref, top, bottom):
    half, columns, lanes = mid_ref.shape
    first = lax.broadcasted_iota(jnp.int32, (columns, lanes), 1) < lanes // 2
    for k in range(RIM):
        above, below = top(k), bottom(k)
        above = jnp.concatenate([above, swap(above)], axis=0)
        below = jnp.concatenate([swap(below), below], axis=0)
        upper = swap(mid_ref[half - RIM + k].astype(f32))
        lower = swap(mid_ref[k].astype(f32))
        ext_ref[k] = jnp.where(first, above, upper)
        ext_ref[half + RIM + k] = jnp.where(first, lower, below)
    for i in range(half):
        ext_ref[RIM + i] = mid_ref[i].astype(f32)


def added(mine_ref, other_ref, total):
    return mine_ref[:total].astype(f32) + other_ref[:total].astype(f32)


def fill_taps(taps_ref, wide_ref, flip):
    chan = taps_ref.shape[2]
    for a in range(TAPS):
        for b in range(TAPS):
            row = taps_ref[TAPS - 1 - a, TAPS - 1 - b, :] if flip else taps_ref[a, b, :]
            row = row.reshape(1, chan)
            row = jnp.concatenate([row, row], axis=1)
            wide_ref[a * TAPS + b] = jnp.broadcast_to(row, (8, 2 * chan))


def convolve_tile(ext_ref, wide_ref, store, half, start):
    tiles = STEP // 8
    total = [[None] * tiles for _ in range(half)]
    for row in range(half + 2 * RIM):
        for b in range(TAPS):
            piece = [ext_ref[row, pl.ds(start + b + 8 * s, 8), :] for s in range(tiles)]
            for i in range(half):
                a = row - i
                if 0 <= a < TAPS:
                    weight = wide_ref[a * TAPS + b]
                    for s in range(tiles):
                        term = weight * piece[s]
                        total[i][s] = term if total[i][s] is None else total[i][s] + term
    for i in range(half):
        store(i, start, jnp.concatenate(total[i], axis=0))


def convolve(ext_ref, wide_ref, store, half, columns, unroll):
    def trip(t, carry):
        convolve_tile(ext_ref, wide_ref, store, half, pl.multiple_of(t * STEP, STEP))
        return carry

    lax.fori_loop(0, columns // STEP, trip, 0, unroll=unroll)


def group_mean(values, ones):
    high = values.astype(bf16)
    low = (values - high.astype(f32)).astype(bf16)
    return jnp.dot(jnp.concatenate([high, low], axis=1), ones, preferred_element_type=f32)


def put_rows(packed, half, odd, send_ref, at, later_ref):
    wide, lanes = packed(0).shape
    mid = wide // 2
    first = lax.broadcasted_iota(jnp.int32, (mid, lanes), 1) < lanes // 2
    for k in range(RIM):
        upper, lower = packed(k), packed(half - RIM + k)
        upper = jnp.where(first, upper[:mid], swap(upper[mid:]))
        lower = jnp.where(first, swap(lower[:mid]), lower[mid:])
        send_ref[at + k * mid : at + (k + 1) * mid, :] = jnp.where(odd, upper, lower).astype(bf16)
        later_ref[k * mid : (k + 1) * mid, :] = jnp.where(odd, lower, upper).astype(bf16)


def packed_rows(field, half, lanes):
    count = field.shape[0]
    shape = (count // (2 * half), 2 * half, lanes)
    chan = lax.broadcasted_iota(jnp.int32, shape, 0)
    row = lax.broadcasted_iota(jnp.int32, shape, 1)
    lane = lax.broadcasted_iota(jnp.int32, shape, 2)
    lower = row >= half
    row = jnp.where(lower, row - half, row)
    here = lane == jnp.where(lower, chan + lanes // 2, chan)
    packed = []
    for i in range(half):
        pick = jnp.where(here & (row == i), 1.0, 0.0).reshape(count, lanes).astype(bf16)
        packed.append(
            lax.dot_general(field, pick, (((0,), (0,)), ((), ())), preferred_element_type=f32)
        )
    return packed


def pack_kernel(lat_ref, state_ref, mid_ref, send_ref, later_ref):
    half, wide, lanes = mid_ref.shape
    n_cols = state_ref.shape[1]
    fields = []
    for i, field in enumerate(packed_rows(state_ref[...], half, lanes)):
        before = jnp.zeros((RIM, lanes), f32)
        after = jnp.zeros((wide - RIM - n_cols, lanes), f32)
        fields.append(jnp.concatenate([before, field, after], axis=0))
        mid_ref[i] = fields[i].astype(bf16)
    put_rows(lambda i: fields[i], half, lat_ref[0] == 1, send_ref, 0, later_ref)


def wet_kernel(cot_ref, sea_ref, wet_ref):
    half, columns, lanes = wet_ref.shape
    n_rows, n_cols = sea_ref.shape
    cot = cot_ref[...].astype(f32).reshape(-1, n_rows, n_cols) * sea_ref[...].astype(f32)
    cot = cot.reshape(-1, n_cols).astype(bf16)
    for i, field in enumerate(packed_rows(cot, half, lanes)):
        after = jnp.zeros((columns - n_cols, lanes), f32)
        wet_ref[i] = jnp.concatenate([field, after], axis=0).astype(bf16)


def edge_kernel(n_cols, lon_ref, lat_ref, pole_ref, mid_ref, early_ref, late_ref, send_ref, later_ref):
    half, wide, lanes = mid_ref.shape
    mid = wide // 2
    odd_lat, odd_lon, pole = lat_ref[0] == 1, lon_ref[0] == 1, pole_ref[0] == 1
    base = n_cols // 16 * 16
    skip = n_cols - base
    first = lax.broadcasted_iota(jnp.int32, (8, lanes), 1) < lanes // 2
    left, right = [], []
    for i in range(half):
        left.append(mid_ref[i, :16, :].astype(f32)[:8])
        right.append(mid_ref[i, base : base + 32, :].astype(f32)[skip : skip + 8])
    ends = [([], []), ([], [])]
    for k in range(RIM):
        at = k * mid
        one, two = [], []
        for ref in (early_ref, late_ref):
            one.append(ref[at : at + 16, :].astype(f32)[:8])
            two.append(ref[at + base - mid : at + mid, :].astype(f32)[skip : skip + 8])
        one[1], two[1] = jnp.where(pole, 0.0, one[1]), jnp.where(pole, 0.0, two[1])
        above = jnp.where(odd_lat, one[0], one[1]), jnp.where(odd_lat, two[0], two[1])
        below = jnp.where(odd_lat, one[1], one[0]), jnp.where(odd_lat, two[1], two[0])
        ends[0][0].append(jnp.where(first, above[0], swap(left[half - RIM + k])))
        ends[0][1].append(jnp.where(first, swap(above[1]), swap(right[half - RIM + k])))
        ends[1][0].append(jnp.where(first, swap(left[k]), swap(below[0])))
        ends[1][1].append(jnp.where(first, swap(right[k]), below[1]))
    left = ends[0][0] + left + ends[1][0]
    right = ends[0][1] + right + ends[1][1]
    left = jnp.concatenate([x[RIM : RIM + 4] for x in left], axis=0)
    right = jnp.concatenate([x[:4] for x in right], axis=0)
    send_ref[...] = jnp.where(odd_lon, left, right).astype(bf16)
    later_ref[...] = jnp.where(odd_lon, right, left).astype(bf16)


def inner_kernel(lat_ref, pole_ref, mid_ref, early_ref, late_ref, taps_ref, ext_ref, conv_ref, wide_ref):
    half, columns, lanes = conv_ref.shape
    assemble(ext_ref, mid_ref, *rim_rows(lat_ref, pole_ref, early_ref, late_ref, 0))
    fill_taps(taps_ref, wide_ref, False)

    def put(i, start, value):
        conv_ref[i, pl.ds(start, STEP), :] = value

    convolve(ext_ref, wide_ref, put, half, columns, 1)


def block_kernel(
    n_cols, lon_ref, half_ref, early_ref, late_ref, wet_ref, wide, conv_bias_ref, gain_ref, bias_ref, w1_ref, b1_ref, w2_ref,
    ext_in, conv_in, ext32, conv, dconv_ref, keep_ref, send_ref, edge_ref, w1, w2,
):
    half, columns, lanes = wet_ref.shape
    chan = lanes // 2
    wide_e = w1_ref.shape[1]
    odd = lon_ref[0] == 1
    one, two = early_ref[...].astype(f32), late_ref[...].astype(f32)
    left, right = jnp.where(odd, one, two), jnp.where(odd, two, one)
    for row in range(half + 2 * RIM):
        ext32[row, :RIM, :] = left[4 * row : 4 * row + RIM]
        ext32[row, RIM + n_cols : 2 * RIM + n_cols, :] = right[4 * row : 4 * row + RIM]

    def put(i, start, value):
        conv[i, pl.ds(start, STEP), :] = value

    for start in [0, *range((n_cols - RIM) // STEP * STEP, columns, STEP)]:
        convolve_tile(ext32, wide, put, half, start)
    w1[...] = jnp.zeros_like(w1)
    w2[...] = jnp.zeros_like(w2)
    w1[:chan, :wide_e] = w1_ref[...]
    w1[chan:, wide_e:] = w1_ref[...]
    w2[:chan, :wide_e] = w2_ref[...]
    w2[chan:, wide_e:] = w2_ref[...]
    dconv_ref[...] = jnp.zeros_like(dconv_ref)

    row_half = lax.broadcasted_iota(jnp.int32, (2 * lanes, lanes), 0) % lanes >= chan
    col_half = lax.broadcasted_iota(jnp.int32, (2 * lanes, lanes), 1) >= chan
    ones = jnp.where(row_half == col_half, 1.0 / chan, 0.0).astype(bf16)
    conv_bias, gain, bias, hidden_bias = (
        jnp.concatenate([ref[...], ref[...]], axis=1)
        for ref in (conv_bias_ref, gain_ref, bias_ref, b1_ref)
    )

    cells_all = half * columns
    out = conv[...].reshape(cells_all, lanes) + conv_bias
    wet = wet_ref[...].reshape(cells_all, lanes)
    center = out - group_mean(out, ones)
    rstd = lax.rsqrt(group_mean(center * center, ones) + ln_eps)
    normed = center * rstd
    zed = (normed * gain + bias).astype(bf16)
    pre = jnp.dot(zed, w1[...], preferred_element_type=f32) + hidden_bias
    dact = jnp.dot(wet, w2[...], preferred_element_type=f32)
    phi = 0.5 + 0.5 * lax.erf(pre * root_half)
    act = (pre * phi).astype(bf16)
    dhid = (dact * (phi + pre * (jnp.exp(-0.5 * pre * pre) * inv_root_tau))).astype(bf16)
    dzed = lax.dot_general(dhid, w1[...], (((1,), (1,)), ((), ())), preferred_element_type=f32)
    rows_first = (((0,), (0,)), ((), ()))
    expand = lax.dot_general(zed, dhid, rows_first, preferred_element_type=f32)
    project = lax.dot_general(wet, act, rows_first, preferred_element_type=f32)
    dnorm = dzed * gain
    mean1 = group_mean(dnorm, ones)
    mean2 = group_mean(dnorm * normed, ones)
    dconv = rstd * (dnorm - mean1 - normed * mean2)
    hidden = jnp.sum(dhid.astype(f32), axis=0, keepdims=True)
    parts = (wet.astype(f32), dzed * normed, dzed, dconv)
    small = [jnp.sum(part, axis=0, keepdims=True) for part in parts]
    dconv = dconv.reshape(half, columns, lanes)
    conv[...] = dconv
    dconv_ref[:, pl.ds(RIM, columns), :] = dconv

    rows = []
    for block in (expand, project):
        total = block[:chan, :wide_e] + block[chan:, wide_e:]
        rows += [total[:, k * lanes : (k + 1) * lanes] for k in range(wide_e // lanes)]
    total = hidden[:, :wide_e] + hidden[:, wide_e:]
    fine = [total[:, k * lanes : (k + 1) * lanes] for k in range(wide_e // lanes)] + small
    fine.append(jnp.zeros((-len(fine) % 8, lanes), f32))
    rows = jnp.concatenate(rows + fine + tap_sums(ext32, conv), axis=0)

    pad = jnp.zeros((edge_ref.shape[0] // (2 * half) - RIM, lanes), f32)
    first = [x for i in range(half) for x in (conv[i, :RIM, :], pad)]
    last = [x for i in range(half) for x in (conv[i, n_cols - RIM : n_cols, :], pad)]
    first = jnp.concatenate(first, axis=0)
    last = jnp.concatenate(last, axis=0)
    edges = [jnp.where(odd, first, last), jnp.where(odd, last, first)]
    edge_ref[...] = jnp.concatenate(edges, axis=0).astype(bf16)
    part = rows.shape[0] // 2
    upper_half = half_ref[0] == 1
    keep_ref[...] = jnp.where(upper_half, rows[part:], rows[:part])
    send_ref[...] = jnp.where(upper_half, rows[:part], rows[part:])


def tap_sums(ext32, grad_ref):
    half, columns, lanes = grad_ref.shape

    def trip(t, carry):
        start = pl.multiple_of(t * 8, 8)
        total = list(carry)
        grads = [grad_ref[i, pl.ds(start, 8), :] for i in range(half)]
        for row in range(half + 2 * RIM):
            for b in range(TAPS):
                piece = ext32[row, pl.ds(start + b, 8), :]
                for i in range(half):
                    a = row - i
                    if 0 <= a < TAPS:
                        total[a * TAPS + b] = total[a * TAPS + b] + grads[i] * piece
        return tuple(total)

    zero = jnp.zeros((8, lanes), f32)
    total = lax.fori_loop(0, columns // 8, trip, (zero,) * (TAPS * TAPS))
    rows = []
    for a in range(TAPS):
        rows += [jnp.sum(total[a * TAPS + b], axis=0, keepdims=True) for b in range(TAPS)]
        rows.append(jnp.zeros((1, lanes), f32))
    return rows


def first_kernel(mine_ref, other_ref, edge_ref, send_ref):
    part = mine_ref.shape[0]
    send_ref[:part] = (mine_ref[...] + other_ref[...]).astype(bf16)
    send_ref[part:] = edge_ref[...]


def add_kernel(total, mine_ref, other_ref, send_ref):
    rim = send_ref.shape[0] - total
    send_ref[:total] = added(mine_ref, other_ref, total).astype(bf16)
    send_ref[total:] = other_ref[other_ref.shape[0] - rim :]


def rows_kernel(
    part, n_cols, lon_ref, lat_ref, early_ref, late_ref, dconv_ref, full_ref, send_ref, later_ref
):
    half = dconv_ref.shape[0]
    odd = lon_ref[0] == 1
    rim = (early_ref.shape[0] - part) // 2
    early = early_ref[part : part + rim].astype(f32)
    late = late_ref[late_ref.shape[0] - rim :].astype(f32)
    right = jnp.where(odd, late, early)
    left = jnp.where(odd, early, late)
    step = rim // half
    for i in range(half):
        full_ref[i] = dconv_ref[i]
        full_ref[i, :RIM, :] = left[i * step : i * step + RIM]
        full_ref[i, RIM + n_cols : 2 * RIM + n_cols, :] = right[i * step : i * step + RIM]
    put_rows(lambda i: full_ref[i], half, lat_ref[0] == 1, send_ref, 0, later_ref)


def rim_rows(lat_ref, pole_ref, early_ref, late_ref, at):
    mid = late_ref.shape[0] // RIM
    odd, pole = lat_ref[0] == 1, pole_ref[0] == 1

    def rows(k):
        early = early_ref[at + k * mid : at + (k + 1) * mid, :].astype(f32)
        late = late_ref[k * mid : (k + 1) * mid, :].astype(f32)
        return early, jnp.where(pole, 0.0, late)

    def top(k):
        early, late = rows(k)
        return jnp.where(odd, early, late)

    def bottom(k):
        early, late = rows(k)
        return jnp.where(odd, late, early)

    return top, bottom


def back_kernel(at, lat_ref, pole_ref, early_ref, late_ref, mid_ref, taps_ref, out_ref, ext32, wide):
    half, columns, lanes = out_ref.shape
    assemble(ext32, mid_ref, *rim_rows(lat_ref, pole_ref, early_ref, late_ref, at))
    fill_taps(taps_ref, wide, True)

    def put(i, start, value):
        out_ref[i, pl.ds(start, STEP), :] = value

    convolve(ext32, wide, put, half, columns, 1)


def finish_kernel(
    scale, half_ref, mine_ref, other_ref,
    taps_ref, conv_ref, gain_ref, bias_ref, expand_ref, hidden_ref, project_ref, wet_ref,
):
    lanes = mine_ref.shape[1]
    chan, wide_e = expand_ref.shape
    odd = half_ref[0] == 1
    mine, other = mine_ref[...] * scale, other_ref[...] * scale
    total = jnp.concatenate([jnp.where(odd, other, mine), jnp.where(odd, mine, other)], axis=0)
    blocks = wide_e // lanes
    small = total[2 * blocks * chan :]
    for k in range(blocks):
        expand_ref[:, k * lanes : (k + 1) * lanes] = total[k * chan : (k + 1) * chan]
        at = (blocks + k) * chan
        project_ref[:, k * lanes : (k + 1) * lanes] = total[at : at + chan]
        hidden_ref[:, k * lanes : (k + 1) * lanes] = small[k : k + 1]
    narrow = small[:, :chan] + small[:, chan:]
    for k, ref in enumerate((wet_ref, gain_ref, bias_ref, conv_ref)):
        ref[...] = narrow[blocks + k : blocks + k + 1]
    at = small.shape[0] - 8 * TAPS
    for a in range(TAPS):
        taps_ref[a] = narrow[at + 8 * a : at + 8 * a + TAPS]


def call(kernel, out_shape, scratch, flops, *args, aliases={}):
    vmem = pl.BlockSpec(memory_space=pltpu.VMEM)
    smem = pl.BlockSpec(memory_space=pltpu.SMEM)
    many = isinstance(out_shape, (list, tuple))
    return pl.pallas_call(
        kernel,
        out_shape=out_shape,
        in_specs=[smem if arg.dtype == jnp.int32 and arg.ndim == 1 else vmem for arg in args],
        out_specs=[vmem] * len(out_shape) if many else vmem,
        scratch_shapes=scratch,
        input_output_aliases=aliases,
        cost_estimate=pl.CostEstimate(flops=flops, bytes_accessed=1 << 20, transcendentals=0),
        compiler_params=pltpu.CompilerParams(vmem_limit_bytes=40 << 20),
    )(*args)


def body(
    state, land_sea, cotangent, kernel, conv_bias, ln_gain, ln_bias, w_expand, b_expand, w_project
):
    n_chan, n_rows, n_cols = state.shape
    n_wide = w_expand.shape[1]
    half = n_rows // 2
    lanes = 2 * n_chan
    columns = -(-n_cols // STEP) * STEP
    padded = -(-(columns + 2 * RIM) // 32) * 32
    total = 2 * n_chan * n_wide // lanes + -(-(n_wide // lanes + 4) // 8) * 8 + 8 * TAPS
    part = total // 2
    rim = half * 4
    rows = RIM * padded // 2
    cells = n_rows * n_cols
    conv_flops = cells * n_chan * TAPS * TAPS * 2
    shaped = jax.ShapeDtypeStruct
    row = lambda v: v.reshape(1, -1)
    taps = kernel.transpose(1, 2, 0)
    odd_lon, odd_lat = lax.axis_index("lon") % 2, lax.axis_index("lat") % 2
    place, last_place = lax.axis_index("lat"), lax.axis_size("lat") - 1
    pole = ((place == 0) | (place == last_place)).astype(jnp.int32).reshape(1)
    on_lon, on_lat, keeps = odd_lon.reshape(1), odd_lat.reshape(1), kept_half().reshape(1)

    flat = shaped((rows, lanes), bf16)
    field, first, last = call(
        pack_kernel,
        [shaped((half, padded, lanes), bf16), flat, flat],
        [],
        cells * n_chan,
        on_lat, state.reshape(n_chan * n_rows, n_cols),
    )
    early = lax.ppermute(first, "lat", pairs("lat", 1))
    late = lax.ppermute(last, "lat", ring_pairs("lat"))
    wet = call(
        wet_kernel,
        shaped((half, columns, lanes), bf16),
        [],
        cells * n_chan,
        cotangent.reshape(n_chan * n_rows, n_cols), land_sea,
    )

    early, late, wet = lax.optimization_barrier((early, late, wet))
    side = shaped((4 * (half + 2 * RIM), lanes), bf16)
    first, last = call(
        functools.partial(edge_kernel, n_cols), [side, side], [], cells,
        on_lon, on_lat, pole, field, early, late,
    )
    before = lax.ppermute(first, "lon", pairs("lon", 1))
    after = lax.ppermute(last, "lon", ring_pairs("lon"))
    ext, conv, wide_taps = call(
        inner_kernel,
        [
            shaped((half + 2 * RIM, padded, lanes), f32),
            shaped((half, columns, lanes), f32),
            shaped((TAPS * TAPS, 8, lanes), f32),
        ],
        [],
        conv_flops,
        on_lat, pole, field, early, late, taps,
    )

    _, _, dconv, mine, send, edges = call(
        functools.partial(block_kernel, n_cols),
        [
            shaped(ext.shape, f32),
            shaped(conv.shape, f32),
            shaped((half, padded, lanes), f32),
            shaped((part, lanes), f32),
            shaped((part, lanes), f32),
            shaped((2 * rim, lanes), bf16),
        ],
        [
            pltpu.VMEM((lanes, 2 * n_wide), bf16),
            pltpu.VMEM((lanes, 2 * n_wide), bf16),
        ],
        cells * n_chan * n_wide * 10 + conv_flops,
        on_lon, keeps, before, after, wet, wide_taps, row(conv_bias), row(ln_gain), row(ln_bias),
        w_expand, row(b_expand), w_project.T, ext, conv,
        aliases={12: 0, 13: 1},
    )

    other = lax.ppermute(send, "lat", pairs("lat", 1))
    sent = shaped((part + 2 * rim, lanes), bf16)
    mine = call(first_kernel, sent, [], part * lanes, mine, other, edges)
    other = early = lax.ppermute(mine, "lon", pairs("lon", 1))
    add = functools.partial(add_kernel, part)
    place, size = lax.axis_index("lon"), lax.axis_size("lon")
    apart = place ^ ((place + 2 * odd_lon - 1) % size)
    late = None
    for bit in bits("lon", 1):
        mine = call(add, shaped((part + rim, lanes), bf16), [], part * lanes, mine, other)
        other = lax.ppermute(mine, "lon", pairs("lon", bit))
        late = other if late is None else jnp.where(apart == 2 * bit - 1, other, late)
    mine = added(mine, other, part)
    row_shape = shaped((rows, lanes), bf16)
    full, first, last = call(
        functools.partial(rows_kernel, part, n_cols),
        [shaped(dconv.shape, f32), row_shape, row_shape],
        [],
        cells * n_chan,
        on_lon, on_lat, early, late, dconv,
    )
    early = lax.ppermute(first, "lat", pairs("lat", 1))
    late = lax.ppermute(last, "lat", ring_pairs("lat"))
    for k, swaps in enumerate(half_rounds()):
        mine = mine + lax.ppermute(mine, "lat", swaps)
        if k == 0:
            late, _ = lax.optimization_barrier((late, mine))
    other = lax.ppermute(mine, "lat", pairs("lat", 1))

    grad = call(
        functools.partial(back_kernel, 0),
        shaped((half, columns, lanes), f32),
        [
            pltpu.VMEM((half + 2 * RIM, padded, lanes), f32),
            pltpu.VMEM((TAPS * TAPS, 8, lanes), f32),
        ],
        conv_flops,
        on_lat, pole, early, late, full, taps,
    )
    grad = unpack(grad)[:, :n_cols].transpose(2, 0, 1)
    state_grad = (cotangent.astype(f32) + grad).astype(bf16)

    scale = 1.0 / math.sqrt(cells * lax.axis_size("lat") * lax.axis_size("lon"))
    narrow = shaped((1, n_chan), f32)
    out = call(
        functools.partial(finish_kernel, scale),
        [
            shaped((TAPS, TAPS, n_chan), f32),
            narrow,
            narrow,
            narrow,
            shaped((n_chan, n_wide), f32),
            shaped((1, n_wide), f32),
            shaped((n_chan, n_wide), f32),
            narrow,
        ],
        [],
        total * lanes,
        keeps, mine, other,
    )
    return (
        state_grad,
        out[0].transpose(2, 0, 1),
        out[1].reshape(-1),
        out[2].reshape(-1),
        out[3].reshape(-1),
        out[4],
        out[5].reshape(-1),
        out[6].T,
        out[7].reshape(-1),
    )


def solution(mesh):
    in_specs = (
        P(None, "lat", "lon"),
        P("lat", "lon"),
        P(None, "lat", "lon"),
        P(),
        P(),
        P(),
        P(),
        P(),
        P(),
        P(),
    )
    out_specs = (P(None, "lat", "lon"), P(), P(), P(), P(), P(), P(), P(), P())
    return jax.shard_map(body, mesh=mesh, in_specs=in_specs, out_specs=out_specs, check_vma=False)
```

```python
import functools
import math

import jax
import jax.numpy as jnp
from jax import lax
from jax.experimental import pallas as pl
from jax.experimental.pallas import tpu as pltpu
from jax.sharding import PartitionSpec as P

TAPS = 7
RIM = 3
STEP = 16

ln_eps = 1e-06
root_half = 0.7071067811865476
inv_root_tau = 0.3989422804014327
f32 = jnp.float32
bf16 = jnp.bfloat16


def pairs(axis, bit):
    return [(i, i ^ bit) for i in range(lax.axis_size(axis))]


def ring_pairs(axis):
    size = lax.axis_size(axis)
    return [(i, (i + 1 if i % 2 else i - 1) % size) for i in range(size)]


def bits(axis, first):
    size = lax.axis_size(axis)
    if size < 4 or size & (size - 1):
        raise ValueError("axis size")
    return [1 << k for k in range(first, size.bit_length() - 1)]


def kept_half():
    place = lax.axis_index("lat")
    return sum(place // bit for bit in [1] + bits("lat", 1)) % 2


def half_rounds():
    steps = bits("lat", 1)
    turned = steps[1:] + steps[:1]
    size = lax.axis_size("lat")
    order = [turned if bin(i).count("1") % 2 else steps for i in range(size)]
    return [[(i, i ^ order[i][k] ^ 1) for i in range(size)] for k in range(len(steps))]


def unpack(field):
    chan = field.shape[2] // 2
    return jnp.concatenate([field[:, :, :chan], field[:, :, chan:]], axis=0)


def swap(value):
    return pltpu.roll(value, value.shape[-1] // 2, value.ndim - 1)


def assemble(ext_ref, mid_ref, top, bottom):
    half, columns, lanes = mid_ref.shape
    first = lax.broadcasted_iota(jnp.int32, (columns, lanes), 1) < lanes // 2
    for k in range(RIM):
        above, below = top(k), bottom(k)
        above = jnp.concatenate([above, swap(above)], axis=0)
        below = jnp.concatenate([swap(below), below], axis=0)
        upper = swap(mid_ref[half - RIM + k].astype(f32))
        lower = swap(mid_ref[k].astype(f32))
        ext_ref[k] = jnp.where(first, above, upper)
        ext_ref[half + RIM + k] = jnp.where(first, lower, below)
    for i in range(half):
        ext_ref[RIM + i] = mid_ref[i].astype(f32)


def added(mine_ref, other_ref, total):
    return mine_ref[:total].astype(f32) + other_ref[:total].astype(f32)


def fill_taps(taps_ref, wide_ref, flip):
    chan = taps_ref.shape[2]
    for a in range(TAPS):
        for b in range(TAPS):
            row = taps_ref[TAPS - 1 - a, TAPS - 1 - b, :] if flip else taps_ref[a, b, :]
            row = row.reshape(1, chan)
            row = jnp.concatenate([row, row], axis=1)
            wide_ref[a * TAPS + b] = jnp.broadcast_to(row, (8, 2 * chan))


def convolve_tile(ext_ref, wide_ref, store, half, start):
    tiles = STEP // 8
    total = [[None] * tiles for _ in range(half)]
    for row in range(half + 2 * RIM):
        for b in range(TAPS):
            piece = [ext_ref[row, pl.ds(start + b + 8 * s, 8), :] for s in range(tiles)]
            for i in range(half):
                a = row - i
                if 0 <= a < TAPS:
                    weight = wide_ref[a * TAPS + b]
                    for s in range(tiles):
                        term = weight * piece[s]
                        total[i][s] = term if total[i][s] is None else total[i][s] + term
    for i in range(half):
        store(i, start, jnp.concatenate(total[i], axis=0))


def convolve(ext_ref, wide_ref, store, half, columns, unroll):
    def trip(t, carry):
        convolve_tile(ext_ref, wide_ref, store, half, pl.multiple_of(t * STEP, STEP))
        return carry

    lax.fori_loop(0, columns // STEP, trip, 0, unroll=unroll)


def group_mean(values, ones):
    high = values.astype(bf16)
    low = (values - high.astype(f32)).astype(bf16)
    return jnp.dot(jnp.concatenate([high, low], axis=1), ones, preferred_element_type=f32)


def put_rows(packed, half, odd, send_ref, at, later_ref):
    wide, lanes = packed(0).shape
    mid = wide // 2
    first = lax.broadcasted_iota(jnp.int32, (mid, lanes), 1) < lanes // 2
    for k in range(RIM):
        upper, lower = packed(k), packed(half - RIM + k)
        upper = jnp.where(first, upper[:mid], swap(upper[mid:]))
        lower = jnp.where(first, swap(lower[:mid]), lower[mid:])
        send_ref[at + k * mid : at + (k + 1) * mid, :] = jnp.where(odd, upper, lower).astype(bf16)
        later_ref[k * mid : (k + 1) * mid, :] = jnp.where(odd, lower, upper).astype(bf16)


def packed_rows(field, half, lanes):
    count = field.shape[0]
    shape = (count // (2 * half), 2 * half, lanes)
    chan = lax.broadcasted_iota(jnp.int32, shape, 0)
    row = lax.broadcasted_iota(jnp.int32, shape, 1)
    lane = lax.broadcasted_iota(jnp.int32, shape, 2)
    lower = row >= half
    row = jnp.where(lower, row - half, row)
    here = lane == jnp.where(lower, chan + lanes // 2, chan)
    packed = []
    for i in range(half):
        pick = jnp.where(here & (row == i), 1.0, 0.0).reshape(count, lanes).astype(bf16)
        packed.append(
            lax.dot_general(field, pick, (((0,), (0,)), ((), ())), preferred_element_type=f32)
        )
    return packed


def pack_kernel(lat_ref, state_ref, mid_ref, send_ref, later_ref):
    half, wide, lanes = mid_ref.shape
    n_cols = state_ref.shape[1]
    fields = []
    for i, field in enumerate(packed_rows(state_ref[...], half, lanes)):
        before = jnp.zeros((RIM, lanes), f32)
        after = jnp.zeros((wide - RIM - n_cols, lanes), f32)
        fields.append(jnp.concatenate([before, field, after], axis=0))
        mid_ref[i] = fields[i].astype(bf16)
    put_rows(lambda i: fields[i], half, lat_ref[0] == 1, send_ref, 0, later_ref)


def wet_kernel(cot_ref, sea_ref, wet_ref):
    half, columns, lanes = wet_ref.shape
    n_rows, n_cols = sea_ref.shape
    cot = cot_ref[...].astype(f32).reshape(-1, n_rows, n_cols) * sea_ref[...].astype(f32)
    cot = cot.reshape(-1, n_cols).astype(bf16)
    for i, field in enumerate(packed_rows(cot, half, lanes)):
        after = jnp.zeros((columns - n_cols, lanes), f32)
        wet_ref[i] = jnp.concatenate([field, after], axis=0).astype(bf16)


def edge_kernel(n_cols, lon_ref, lat_ref, pole_ref, mid_ref, early_ref, late_ref, send_ref, later_ref):
    half, wide, lanes = mid_ref.shape
    mid = wide // 2
    odd_lat, odd_lon, pole = lat_ref[0] == 1, lon_ref[0] == 1, pole_ref[0] == 1
    base = n_cols // 16 * 16
    skip = n_cols - base
    first = lax.broadcasted_iota(jnp.int32, (8, lanes), 1) < lanes // 2
    left, right = [], []
    for i in range(half):
        left.append(mid_ref[i, :16, :].astype(f32)[:8])
        right.append(mid_ref[i, base : base + 32, :].astype(f32)[skip : skip + 8])
    ends = [([], []), ([], [])]
    for k in range(RIM):
        at = k * mid
        one, two = [], []
        for ref in (early_ref, late_ref):
            one.append(ref[at : at + 16, :].astype(f32)[:8])
            two.append(ref[at + base - mid : at + mid, :].astype(f32)[skip : skip + 8])
        one[1], two[1] = jnp.where(pole, 0.0, one[1]), jnp.where(pole, 0.0, two[1])
        above = jnp.where(odd_lat, one[0], one[1]), jnp.where(odd_lat, two[0], two[1])
        below = jnp.where(odd_lat, one[1], one[0]), jnp.where(odd_lat, two[1], two[0])
        ends[0][0].append(jnp.where(first, above[0], swap(left[half - RIM + k])))
        ends[0][1].append(jnp.where(first, swap(above[1]), swap(right[half - RIM + k])))
        ends[1][0].append(jnp.where(first, swap(left[k]), swap(below[0])))
        ends[1][1].append(jnp.where(first, swap(right[k]), below[1]))
    left = ends[0][0] + left + ends[1][0]
    right = ends[0][1] + right + ends[1][1]
    left = jnp.concatenate([x[RIM : RIM + 4] for x in left], axis=0)
    right = jnp.concatenate([x[:4] for x in right], axis=0)
    send_ref[...] = jnp.where(odd_lon, left, right).astype(bf16)
    later_ref[...] = jnp.where(odd_lon, right, left).astype(bf16)


def inner_kernel(lat_ref, pole_ref, mid_ref, early_ref, late_ref, taps_ref, ext_ref, conv_ref, wide_ref):
    half, columns, lanes = conv_ref.shape
    assemble(ext_ref, mid_ref, *rim_rows(lat_ref, pole_ref, early_ref, late_ref, 0))
    fill_taps(taps_ref, wide_ref, False)

    def put(i, start, value):
        conv_ref[i, pl.ds(start, STEP), :] = value

    convolve(ext_ref, wide_ref, put, half, columns, 1)


def block_kernel(
    n_cols, lon_ref, half_ref, early_ref, late_ref, wet_ref, wide,
    conv_bias_ref, gain_ref, bias_ref, w1_ref, b1_ref, w2_ref, ext_ref, conv_ref,
    dconv_ref, keep_ref, send_ref, edge_ref, w1, w2, conv, left_ext, right_ext,
):
    half, columns, lanes = wet_ref.shape
    chan = lanes // 2
    wide_e = w1_ref.shape[1]
    odd = lon_ref[0] == 1
    one, two = early_ref[...].astype(f32), late_ref[...].astype(f32)
    left, right = jnp.where(odd, one, two), jnp.where(odd, two, one)
    base = ext_ref.shape[1] - right_ext.shape[1]
    at = RIM + n_cols - base
    for row in range(half + 2 * RIM):
        left_ext[row] = ext_ref[row, : left_ext.shape[1], :]
        right_ext[row] = ext_ref[row, base:, :]
        left_ext[row, :RIM, :] = left[4 * row : 4 * row + RIM]
        right_ext[row, at : at + RIM, :] = right[4 * row : 4 * row + RIM]

    def put_left(i, start, value):
        conv[i, :STEP, :] = value

    def put_right(i, start, value):
        conv[i, base + start : base + start + STEP, :] = value

    convolve_tile(left_ext, wide, put_left, half, 0)
    for start in range(0, columns - base, STEP):
        convolve_tile(right_ext, wide, put_right, half, start)
    conv[:, STEP:base, :] = conv_ref[:, STEP:base, :]
    w1[...] = jnp.zeros_like(w1)
    w2[...] = jnp.zeros_like(w2)
    w1[:chan, :wide_e] = w1_ref[...]
    w1[chan:, wide_e:] = w1_ref[...]
    w2[:chan, :wide_e] = w2_ref[...]
    w2[chan:, wide_e:] = w2_ref[...]
    dconv_ref[...] = jnp.zeros_like(dconv_ref)

    row_half = lax.broadcasted_iota(jnp.int32, (2 * lanes, lanes), 0) % lanes >= chan
    col_half = lax.broadcasted_iota(jnp.int32, (2 * lanes, lanes), 1) >= chan
    ones = jnp.where(row_half == col_half, 1.0 / chan, 0.0).astype(bf16)
    conv_bias, gain, bias, hidden_bias = (
        jnp.concatenate([ref[...], ref[...]], axis=1)
        for ref in (conv_bias_ref, gain_ref, bias_ref, b1_ref)
    )

    cells_all = half * columns
    out = conv[...].reshape(cells_all, lanes) + conv_bias
    wet = wet_ref[...].reshape(cells_all, lanes)
    center = out - group_mean(out, ones)
    rstd = lax.rsqrt(group_mean(center * center, ones) + ln_eps)
    normed = center * rstd
    zed = (normed * gain + bias).astype(bf16)
    pre = jnp.dot(zed, w1[...], preferred_element_type=f32) + hidden_bias
    dact = jnp.dot(wet, w2[...], preferred_element_type=f32)
    phi = 0.5 + 0.5 * lax.erf(pre * root_half)
    act = (pre * phi).astype(bf16)
    dhid = (dact * (phi + pre * (jnp.exp(-0.5 * pre * pre) * inv_root_tau))).astype(bf16)
    dzed = lax.dot_general(dhid, w1[...], (((1,), (1,)), ((), ())), preferred_element_type=f32)
    rows_first = (((0,), (0,)), ((), ()))
    expand = lax.dot_general(zed, dhid, rows_first, preferred_element_type=f32)
    project = lax.dot_general(wet, act, rows_first, preferred_element_type=f32)
    dnorm = dzed * gain
    mean1 = group_mean(dnorm, ones)
    mean2 = group_mean(dnorm * normed, ones)
    dconv = rstd * (dnorm - mean1 - normed * mean2)
    count = jnp.ones((cells_all, 16), bf16)
    hidden = lax.dot_general(count, dhid, rows_first, preferred_element_type=f32)[:1]
    parts = (wet.astype(f32), dzed * normed, dzed, dconv)
    small = [jnp.sum(part, axis=0, keepdims=True) for part in parts]
    dconv = dconv.reshape(half, columns, lanes)
    conv[...] = dconv
    dconv_ref[:, pl.ds(RIM, columns), :] = dconv

    rows = []
    for block in (expand, project):
        total = block[:chan, :wide_e] + block[chan:, wide_e:]
        rows += [total[:, k * lanes : (k + 1) * lanes] for k in range(wide_e // lanes)]
    total = hidden[:, :wide_e] + hidden[:, wide_e:]
    fine = [total[:, k * lanes : (k + 1) * lanes] for k in range(wide_e // lanes)] + small
    fine.append(jnp.zeros((-len(fine) % 8, lanes), f32))
    rows = jnp.concatenate(rows + fine + tap_sums(ext_ref, left_ext, right_ext, conv), axis=0)

    pad = jnp.zeros((edge_ref.shape[0] // (2 * half) - RIM, lanes), f32)
    first = [x for i in range(half) for x in (conv[i, :RIM, :], pad)]
    last = [x for i in range(half) for x in (conv[i, n_cols - RIM : n_cols, :], pad)]
    first = jnp.concatenate(first, axis=0)
    last = jnp.concatenate(last, axis=0)
    edges = [jnp.where(odd, first, last), jnp.where(odd, last, first)]
    edge_ref[...] = jnp.concatenate(edges, axis=0).astype(bf16)
    part = rows.shape[0] // 2
    upper_half = half_ref[0] == 1
    keep_ref[...] = jnp.where(upper_half, rows[part:], rows[:part])
    send_ref[...] = jnp.where(upper_half, rows[:part], rows[part:])


def tap_sums(ext_ref, left_ext, right_ext, grad_ref):
    half, columns, lanes = grad_ref.shape
    base = ext_ref.shape[1] - right_ext.shape[1]

    def tile(total, field_ref, at, start):
        total = list(total)
        grads = [grad_ref[i, pl.ds(start, 8), :] for i in range(half)]
        for row in range(half + 2 * RIM):
            for b in range(TAPS):
                piece = field_ref[row, pl.ds(at + b, 8), :]
                for i in range(half):
                    a = row - i
                    if 0 <= a < TAPS:
                        total[a * TAPS + b] = total[a * TAPS + b] + grads[i] * piece
        return tuple(total)

    def trip(t, total):
        start = pl.multiple_of(t * 8, 8)
        return tile(total, ext_ref, start, start)

    total = tile((jnp.zeros((8, lanes), f32),) * (TAPS * TAPS), left_ext, 0, 0)
    for at in range(0, columns - base, 8):
        total = tile(total, right_ext, at, base + at)
    total = lax.fori_loop(1, base // 8, trip, total, unroll=2)
    rows = []
    for a in range(TAPS):
        rows += [jnp.sum(total[a * TAPS + b], axis=0, keepdims=True) for b in range(TAPS)]
        rows.append(jnp.zeros((1, lanes), f32))
    return rows


def first_kernel(mine_ref, other_ref, edge_ref, send_ref):
    part = mine_ref.shape[0]
    send_ref[:part] = (mine_ref[...] + other_ref[...]).astype(bf16)
    send_ref[part:] = edge_ref[...]


def add_kernel(total, mine_ref, other_ref, send_ref):
    rim = send_ref.shape[0] - total
    send_ref[:total] = added(mine_ref, other_ref, total).astype(bf16)
    send_ref[total:] = other_ref[other_ref.shape[0] - rim :]


def rows_kernel(
    part, n_cols, lon_ref, lat_ref, early_ref, late_ref, dconv_ref, full_ref, send_ref, later_ref
):
    half = dconv_ref.shape[0]
    odd = lon_ref[0] == 1
    rim = (early_ref.shape[0] - part) // 2
    early = early_ref[part : part + rim].astype(f32)
    late = late_ref[late_ref.shape[0] - rim :].astype(f32)
    right = jnp.where(odd, late, early)
    left = jnp.where(odd, early, late)
    step = rim // half
    for i in range(half):
        full_ref[i] = dconv_ref[i]
        full_ref[i, :RIM, :] = left[i * step : i * step + RIM]
        full_ref[i, RIM + n_cols : 2 * RIM + n_cols, :] = right[i * step : i * step + RIM]
    put_rows(lambda i: full_ref[i], half, lat_ref[0] == 1, send_ref, 0, later_ref)


def rim_rows(lat_ref, pole_ref, early_ref, late_ref, at):
    mid = late_ref.shape[0] // RIM
    odd, pole = lat_ref[0] == 1, pole_ref[0] == 1

    def rows(k):
        early = early_ref[at + k * mid : at + (k + 1) * mid, :].astype(f32)
        late = late_ref[k * mid : (k + 1) * mid, :].astype(f32)
        return early, jnp.where(pole, 0.0, late)

    def top(k):
        early, late = rows(k)
        return jnp.where(odd, early, late)

    def bottom(k):
        early, late = rows(k)
        return jnp.where(odd, late, early)

    return top, bottom


def back_kernel(at, lat_ref, pole_ref, early_ref, late_ref, mid_ref, taps_ref, out_ref, ext32, wide):
    half, columns, lanes = out_ref.shape
    assemble(ext32, mid_ref, *rim_rows(lat_ref, pole_ref, early_ref, late_ref, at))
    fill_taps(taps_ref, wide, True)

    def put(i, start, value):
        out_ref[i, pl.ds(start, STEP), :] = value

    convolve(ext32, wide, put, half, columns, 1)


def finish_kernel(
    scale, half_ref, mine_ref, other_ref,
    taps_ref, conv_ref, gain_ref, bias_ref, expand_ref, hidden_ref, project_ref, wet_ref,
):
    lanes = mine_ref.shape[1]
    chan, wide_e = expand_ref.shape
    odd = half_ref[0] == 1
    mine, other = mine_ref[...] * scale, other_ref[...] * scale
    total = jnp.concatenate([jnp.where(odd, other, mine), jnp.where(odd, mine, other)], axis=0)
    blocks = wide_e // lanes
    small = total[2 * blocks * chan :]
    for k in range(blocks):
        expand_ref[:, k * lanes : (k + 1) * lanes] = total[k * chan : (k + 1) * chan]
        at = (blocks + k) * chan
        project_ref[:, k * lanes : (k + 1) * lanes] = total[at : at + chan]
        hidden_ref[:, k * lanes : (k + 1) * lanes] = small[k : k + 1]
    narrow = small[:, :chan] + small[:, chan:]
    for k, ref in enumerate((wet_ref, gain_ref, bias_ref, conv_ref)):
        ref[...] = narrow[blocks + k : blocks + k + 1]
    at = small.shape[0] - 8 * TAPS
    for a in range(TAPS):
        taps_ref[a] = narrow[at + 8 * a : at + 8 * a + TAPS]


def call(kernel, out_shape, scratch, flops, *args):
    vmem = pl.BlockSpec(memory_space=pltpu.VMEM)
    smem = pl.BlockSpec(memory_space=pltpu.SMEM)
    many = isinstance(out_shape, (list, tuple))
    return pl.pallas_call(
        kernel,
        out_shape=out_shape,
        in_specs=[smem if arg.dtype == jnp.int32 and arg.ndim == 1 else vmem for arg in args],
        out_specs=[vmem] * len(out_shape) if many else vmem,
        scratch_shapes=scratch,
        cost_estimate=pl.CostEstimate(flops=flops, bytes_accessed=1 << 20, transcendentals=0),
        compiler_params=pltpu.CompilerParams(vmem_limit_bytes=40 << 20),
    )(*args)


def body(
    state, land_sea, cotangent, kernel, conv_bias, ln_gain, ln_bias, w_expand, b_expand, w_project
):
    n_chan, n_rows, n_cols = state.shape
    n_wide = w_expand.shape[1]
    half = n_rows // 2
    lanes = 2 * n_chan
    columns = -(-n_cols // STEP) * STEP
    padded = -(-(columns + 2 * RIM) // 32) * 32
    total = 2 * n_chan * n_wide // lanes + -(-(n_wide // lanes + 4) // 8) * 8 + 8 * TAPS
    part = total // 2
    rim = half * 4
    rows = RIM * padded // 2
    cells = n_rows * n_cols
    conv_flops = cells * n_chan * TAPS * TAPS * 2
    shaped = jax.ShapeDtypeStruct
    row = lambda v: v.reshape(1, -1)
    taps = kernel.transpose(1, 2, 0)
    odd_lon, odd_lat = lax.axis_index("lon") % 2, lax.axis_index("lat") % 2
    place, last_place = lax.axis_index("lat"), lax.axis_size("lat") - 1
    pole = ((place == 0) | (place == last_place)).astype(jnp.int32).reshape(1)
    on_lon, on_lat, keeps = odd_lon.reshape(1), odd_lat.reshape(1), kept_half().reshape(1)

    flat = shaped((rows, lanes), bf16)
    field, first, last = call(
        pack_kernel,
        [shaped((half, padded, lanes), bf16), flat, flat],
        [],
        cells * n_chan,
        on_lat, state.reshape(n_chan * n_rows, n_cols),
    )
    early = lax.ppermute(first, "lat", pairs("lat", 1))
    late = lax.ppermute(last, "lat", ring_pairs("lat"))
    wet = call(
        wet_kernel,
        shaped((half, columns, lanes), bf16),
        [],
        cells * n_chan,
        cotangent.reshape(n_chan * n_rows, n_cols), land_sea,
    )

    early, late, wet = lax.optimization_barrier((early, late, wet))
    side = shaped((4 * (half + 2 * RIM), lanes), bf16)
    first, last = call(
        functools.partial(edge_kernel, n_cols), [side, side], [], cells,
        on_lon, on_lat, pole, field, early, late,
    )
    before = lax.ppermute(first, "lon", pairs("lon", 1))
    after = lax.ppermute(last, "lon", ring_pairs("lon"))
    ext, conv, wide_taps = call(
        inner_kernel,
        [
            shaped((half + 2 * RIM, padded, lanes), f32),
            shaped((half, columns, lanes), f32),
            shaped((TAPS * TAPS, 8, lanes), f32),
        ],
        [],
        conv_flops,
        on_lat, pole, field, early, late, taps,
    )

    dconv, mine, send, edges = call(
        functools.partial(block_kernel, n_cols),
        [
            shaped((half, padded, lanes), f32),
            shaped((part, lanes), f32),
            shaped((part, lanes), f32),
            shaped((2 * rim, lanes), bf16),
        ],
        [
            pltpu.VMEM((lanes, 2 * n_wide), bf16),
            pltpu.VMEM((lanes, 2 * n_wide), bf16),
            pltpu.VMEM((half, columns, lanes), f32),
            pltpu.VMEM((half + 2 * RIM, STEP + 8, lanes), f32),
            pltpu.VMEM((half + 2 * RIM, padded - (n_cols - RIM) // STEP * STEP, lanes), f32),
        ],
        cells * n_chan * n_wide * 10 + conv_flops,
        on_lon, keeps, before, after, wet, wide_taps, row(conv_bias), row(ln_gain), row(ln_bias),
        w_expand, row(b_expand), w_project.T, ext, conv,
    )

    other = lax.ppermute(send, "lat", pairs("lat", 1))
    sent = shaped((part + 2 * rim, lanes), bf16)
    mine = call(first_kernel, sent, [], part * lanes, mine, other, edges)
    other = early = lax.ppermute(mine, "lon", pairs("lon", 1))
    add = functools.partial(add_kernel, part)
    place, size = lax.axis_index("lon"), lax.axis_size("lon")
    apart = place ^ ((place + 2 * odd_lon - 1) % size)
    late = None
    for bit in bits("lon", 1):
        mine = call(add, shaped((part + rim, lanes), bf16), [], part * lanes, mine, other)
        other = lax.ppermute(mine, "lon", pairs("lon", bit))
        late = other if late is None else jnp.where(apart == 2 * bit - 1, other, late)
    mine = added(mine, other, part)
    row_shape = shaped((rows, lanes), bf16)
    full, first, last = call(
        functools.partial(rows_kernel, part, n_cols),
        [shaped(dconv.shape, f32), row_shape, row_shape],
        [],
        cells * n_chan,
        on_lon, on_lat, early, late, dconv,
    )
    early = lax.ppermute(first, "lat", pairs("lat", 1))
    late = lax.ppermute(last, "lat", ring_pairs("lat"))
    for k, swaps in enumerate(half_rounds()):
        mine = mine + lax.ppermute(mine, "lat", swaps)
        if k == 0:
            late, _ = lax.optimization_barrier((late, mine))
    other = lax.ppermute(mine, "lat", pairs("lat", 1))

    grad = call(
        functools.partial(back_kernel, 0),
        shaped((half, columns, lanes), f32),
        [
            pltpu.VMEM((half + 2 * RIM, padded, lanes), f32),
            pltpu.VMEM((TAPS * TAPS, 8, lanes), f32),
        ],
        conv_flops,
        on_lat, pole, early, late, full, taps,
    )
    grad = unpack(grad)[:, :n_cols].transpose(2, 0, 1)
    state_grad = (cotangent.astype(f32) + grad).astype(bf16)

    scale = 1.0 / math.sqrt(cells * lax.axis_size("lat") * lax.axis_size("lon"))
    narrow = shaped((1, n_chan), f32)
    out = call(
        functools.partial(finish_kernel, scale),
        [
            shaped((TAPS, TAPS, n_chan), f32),
            narrow,
            narrow,
            narrow,
            shaped((n_chan, n_wide), f32),
            shaped((1, n_wide), f32),
            shaped((n_chan, n_wide), f32),
            narrow,
        ],
        [],
        total * lanes,
        keeps, mine, other,
    )
    return (
        state_grad,
        out[0].transpose(2, 0, 1),
        out[1].reshape(-1),
        out[2].reshape(-1),
        out[3].reshape(-1),
        out[4],
        out[5].reshape(-1),
        out[6].T,
        out[7].reshape(-1),
    )


def solution(mesh):
    in_specs = (
        P(None, "lat", "lon"),
        P("lat", "lon"),
        P(None, "lat", "lon"),
        P(),
        P(),
        P(),
        P(),
        P(),
        P(),
        P(),
    )
    out_specs = (P(None, "lat", "lon"), P(), P(), P(), P(), P(), P(), P(), P())
    return jax.shard_map(body, mesh=mesh, in_specs=in_specs, out_specs=out_specs, check_vma=False)
```

```python
import functools
import math

import jax
import jax.numpy as jnp
from jax import lax
from jax.experimental import pallas as pl
from jax.experimental.pallas import tpu as pltpu
from jax.sharding import PartitionSpec as P

TAPS = 7
RIM = 3
STEP = 16

ln_eps = 1e-06
root_half = 0.7071067811865476
inv_root_tau = 0.3989422804014327
f32 = jnp.float32
bf16 = jnp.bfloat16


def pairs(axis, bit):
    return [(i, i ^ bit) for i in range(lax.axis_size(axis))]


def ring_pairs(axis):
    size = lax.axis_size(axis)
    return [(i, (i + 1 if i % 2 else i - 1) % size) for i in range(size)]


def bits(axis, first):
    size = lax.axis_size(axis)
    if size < 4 or size & (size - 1):
        raise ValueError("axis size")
    return [1 << k for k in range(first, size.bit_length() - 1)]


def kept_half():
    place = lax.axis_index("lat")
    return sum(place // bit for bit in [1] + bits("lat", 1)) % 2


def half_rounds():
    steps = bits("lat", 1)
    turned = steps[1:] + steps[:1]
    size = lax.axis_size("lat")
    order = [turned if bin(i).count("1") % 2 else steps for i in range(size)]
    return [[(i, i ^ order[i][k] ^ 1) for i in range(size)] for k in range(len(steps))]


def unpack(field):
    chan = field.shape[2] // 2
    return jnp.concatenate([field[:, :, :chan], field[:, :, chan:]], axis=0)


def swap(value):
    return pltpu.roll(value, value.shape[-1] // 2, value.ndim - 1)


def assemble(ext_ref, mid_ref, top, bottom):
    half, columns, lanes = mid_ref.shape
    first = lax.broadcasted_iota(jnp.int32, (columns, lanes), 1) < lanes // 2
    for k in range(RIM):
        above, below = top(k), bottom(k)
        above = jnp.concatenate([above, swap(above)], axis=0)
        below = jnp.concatenate([swap(below), below], axis=0)
        upper = swap(mid_ref[half - RIM + k].astype(f32))
        lower = swap(mid_ref[k].astype(f32))
        ext_ref[k] = jnp.where(first, above, upper)
        ext_ref[half + RIM + k] = jnp.where(first, lower, below)
    for i in range(half):
        ext_ref[RIM + i] = mid_ref[i].astype(f32)


def added(mine_ref, other_ref, total):
    return mine_ref[:total].astype(f32) + other_ref[:total].astype(f32)


def fill_taps(taps_ref, wide_ref, flip):
    chan = taps_ref.shape[2]
    for a in range(TAPS):
        for b in range(TAPS):
            row = taps_ref[TAPS - 1 - a, TAPS - 1 - b, :] if flip else taps_ref[a, b, :]
            row = row.reshape(1, chan)
            row = jnp.concatenate([row, row], axis=1)
            wide_ref[a * TAPS + b] = jnp.broadcast_to(row, (8, 2 * chan))


def convolve_tile(ext_ref, wide_ref, store, half, start):
    tiles = STEP // 8
    total = [[None] * tiles for _ in range(half)]
    for row in range(half + 2 * RIM):
        for b in range(TAPS):
            piece = [ext_ref[row, pl.ds(start + b + 8 * s, 8), :] for s in range(tiles)]
            for i in range(half):
                a = row - i
                if 0 <= a < TAPS:
                    weight = wide_ref[a * TAPS + b]
                    for s in range(tiles):
                        term = weight * piece[s]
                        total[i][s] = term if total[i][s] is None else total[i][s] + term
    for i in range(half):
        store(i, start, jnp.concatenate(total[i], axis=0))


def convolve(ext_ref, wide_ref, store, half, columns, unroll):
    def trip(t, carry):
        convolve_tile(ext_ref, wide_ref, store, half, pl.multiple_of(t * STEP, STEP))
        return carry

    lax.fori_loop(0, columns // STEP, trip, 0, unroll=unroll)


def group_mean(values, ones):
    high = values.astype(bf16)
    low = (values - high.astype(f32)).astype(bf16)
    return jnp.dot(jnp.concatenate([high, low], axis=1), ones, preferred_element_type=f32)


def put_rows(packed, half, odd, send_ref, at, later_ref):
    wide, lanes = packed(0).shape
    mid = wide // 2
    first = lax.broadcasted_iota(jnp.int32, (mid, lanes), 1) < lanes // 2
    for k in range(RIM):
        upper, lower = packed(k), packed(half - RIM + k)
        upper = jnp.where(first, upper[:mid], swap(upper[mid:]))
        lower = jnp.where(first, swap(lower[:mid]), lower[mid:])
        send_ref[at + k * mid : at + (k + 1) * mid, :] = jnp.where(odd, upper, lower).astype(bf16)
        later_ref[k * mid : (k + 1) * mid, :] = jnp.where(odd, lower, upper).astype(bf16)


def packed_rows(field, half, lanes):
    count = field.shape[0]
    shape = (count // (2 * half), 2 * half, lanes)
    chan = lax.broadcasted_iota(jnp.int32, shape, 0)
    row = lax.broadcasted_iota(jnp.int32, shape, 1)
    lane = lax.broadcasted_iota(jnp.int32, shape, 2)
    lower = row >= half
    row = jnp.where(lower, row - half, row)
    here = lane == jnp.where(lower, chan + lanes // 2, chan)
    packed = []
    for i in range(half):
        pick = jnp.where(here & (row == i), 1.0, 0.0).reshape(count, lanes).astype(bf16)
        packed.append(
            lax.dot_general(field, pick, (((0,), (0,)), ((), ())), preferred_element_type=f32)
        )
    return packed


def pack_kernel(lat_ref, state_ref, mid_ref, send_ref, later_ref):
    half, wide, lanes = mid_ref.shape
    n_cols = state_ref.shape[1]
    fields = []
    for i, field in enumerate(packed_rows(state_ref[...], half, lanes)):
        before = jnp.zeros((RIM, lanes), f32)
        after = jnp.zeros((wide - RIM - n_cols, lanes), f32)
        fields.append(jnp.concatenate([before, field, after], axis=0))
        mid_ref[i] = fields[i].astype(bf16)
    put_rows(lambda i: fields[i], half, lat_ref[0] == 1, send_ref, 0, later_ref)


def wet_kernel(cot_ref, sea_ref, wet_ref):
    half, columns, lanes = wet_ref.shape
    n_rows, n_cols = sea_ref.shape
    cot = cot_ref[...].astype(f32).reshape(-1, n_rows, n_cols) * sea_ref[...].astype(f32)
    cot = cot.reshape(-1, n_cols).astype(bf16)
    for i, field in enumerate(packed_rows(cot, half, lanes)):
        after = jnp.zeros((columns - n_cols, lanes), f32)
        wet_ref[i] = jnp.concatenate([field, after], axis=0).astype(bf16)


def edge_kernel(n_cols, lon_ref, lat_ref, pole_ref, mid_ref, early_ref, late_ref, send_ref, later_ref):
    half, wide, lanes = mid_ref.shape
    mid = wide // 2
    odd_lat, odd_lon, pole = lat_ref[0] == 1, lon_ref[0] == 1, pole_ref[0] == 1
    base = n_cols // 16 * 16
    skip = n_cols - base
    first = lax.broadcasted_iota(jnp.int32, (8, lanes), 1) < lanes // 2
    left, right = [], []
    for i in range(half):
        left.append(mid_ref[i, :16, :].astype(f32)[:8])
        right.append(mid_ref[i, base : base + 32, :].astype(f32)[skip : skip + 8])
    ends = [([], []), ([], [])]
    for k in range(RIM):
        at = k * mid
        one, two = [], []
        for ref in (early_ref, late_ref):
            one.append(ref[at : at + 16, :].astype(f32)[:8])
            two.append(ref[at + base - mid : at + mid, :].astype(f32)[skip : skip + 8])
        one[1], two[1] = jnp.where(pole, 0.0, one[1]), jnp.where(pole, 0.0, two[1])
        above = jnp.where(odd_lat, one[0], one[1]), jnp.where(odd_lat, two[0], two[1])
        below = jnp.where(odd_lat, one[1], one[0]), jnp.where(odd_lat, two[1], two[0])
        ends[0][0].append(jnp.where(first, above[0], swap(left[half - RIM + k])))
        ends[0][1].append(jnp.where(first, swap(above[1]), swap(right[half - RIM + k])))
        ends[1][0].append(jnp.where(first, swap(left[k]), swap(below[0])))
        ends[1][1].append(jnp.where(first, swap(right[k]), below[1]))
    left = ends[0][0] + left + ends[1][0]
    right = ends[0][1] + right + ends[1][1]
    left = jnp.concatenate([x[RIM : RIM + 4] for x in left], axis=0)
    right = jnp.concatenate([x[:4] for x in right], axis=0)
    send_ref[...] = jnp.where(odd_lon, left, right).astype(bf16)
    later_ref[...] = jnp.where(odd_lon, right, left).astype(bf16)


def inner_kernel(lat_ref, pole_ref, mid_ref, early_ref, late_ref, taps_ref, ext_ref, conv_ref, wide_ref):
    half, columns, lanes = conv_ref.shape
    assemble(ext_ref, mid_ref, *rim_rows(lat_ref, pole_ref, early_ref, late_ref, 0))
    fill_taps(taps_ref, wide_ref, False)

    def put(i, start, value):
        conv_ref[i, pl.ds(start, STEP), :] = value

    convolve(ext_ref, wide_ref, put, half, columns, 1)


def block_kernel(
    n_cols, lon_ref, half_ref, early_ref, late_ref, wet_ref, wide,
    conv_bias_ref, gain_ref, bias_ref, w1_ref, b1_ref, w2_ref, ext_ref, conv_ref,
    dconv_ref, keep_ref, send_ref, edge_ref, left_ext, right_ext, w1, w2, conv,
):
    half, columns, lanes = wet_ref.shape
    chan = lanes // 2
    wide_e = w1_ref.shape[1]
    odd = lon_ref[0] == 1
    one, two = early_ref[...].astype(f32), late_ref[...].astype(f32)
    left, right = jnp.where(odd, one, two), jnp.where(odd, two, one)
    base = ext_ref.shape[1] - right_ext.shape[1]
    at = RIM + n_cols - base
    for row in range(half + 2 * RIM):
        left_ext[row] = ext_ref[row, : left_ext.shape[1], :]
        right_ext[row] = ext_ref[row, base:, :]
        left_ext[row, :RIM, :] = left[4 * row : 4 * row + RIM]
        right_ext[row, at : at + RIM, :] = right[4 * row : 4 * row + RIM]

    def put_left(i, start, value):
        conv[i, :STEP, :] = value

    def put_right(i, start, value):
        conv[i, base + start : base + start + STEP, :] = value

    convolve_tile(left_ext, wide, put_left, half, 0)
    for start in range(0, columns - base, STEP):
        convolve_tile(right_ext, wide, put_right, half, start)
    conv[:, STEP:base, :] = conv_ref[:, STEP:base, :]
    w1[...] = jnp.zeros_like(w1)
    w2[...] = jnp.zeros_like(w2)
    w1[:chan, :wide_e] = w1_ref[...]
    w1[chan:, wide_e:] = w1_ref[...]
    w2[:chan, :wide_e] = w2_ref[...]
    w2[chan:, wide_e:] = w2_ref[...]
    dconv_ref[...] = jnp.zeros_like(dconv_ref)

    row_half = lax.broadcasted_iota(jnp.int32, (2 * lanes, lanes), 0) % lanes >= chan
    col_half = lax.broadcasted_iota(jnp.int32, (2 * lanes, lanes), 1) >= chan
    ones = jnp.where(row_half == col_half, 1.0 / chan, 0.0).astype(bf16)
    conv_bias, gain, bias, hidden_bias = (
        jnp.concatenate([ref[...], ref[...]], axis=1)
        for ref in (conv_bias_ref, gain_ref, bias_ref, b1_ref)
    )

    cells_all = half * columns
    out = conv[...].reshape(cells_all, lanes) + conv_bias
    wet = wet_ref[...].reshape(cells_all, lanes)
    center = out - group_mean(out, ones)
    rstd = lax.rsqrt(group_mean(center * center, ones) + ln_eps)
    normed = center * rstd
    zed = (normed * gain + bias).astype(bf16)
    pre = jnp.dot(zed, w1[...], preferred_element_type=f32) + hidden_bias
    dact = jnp.dot(wet, w2[...], preferred_element_type=f32)
    phi = 0.5 + 0.5 * lax.erf(pre * root_half)
    act = (pre * phi).astype(bf16)
    dhid = (dact * (phi + pre * (jnp.exp(-0.5 * pre * pre) * inv_root_tau))).astype(bf16)
    dzed = lax.dot_general(dhid, w1[...], (((1,), (1,)), ((), ())), preferred_element_type=f32)
    rows_first = (((0,), (0,)), ((), ()))
    expand = lax.dot_general(zed, dhid, rows_first, preferred_element_type=f32)
    project = lax.dot_general(wet, act, rows_first, preferred_element_type=f32)
    dnorm = dzed * gain
    mean1 = group_mean(dnorm, ones)
    mean2 = group_mean(dnorm * normed, ones)
    dconv = rstd * (dnorm - mean1 - normed * mean2)
    count = jnp.ones((cells_all, 16), bf16)
    hidden = lax.dot_general(count, dhid, rows_first, preferred_element_type=f32)[:1]
    parts = (wet.astype(f32), dzed * normed, dzed, dconv)
    small = [jnp.sum(part, axis=0, keepdims=True) for part in parts]
    dconv = dconv.reshape(half, columns, lanes)
    conv[...] = dconv
    dconv_ref[:, pl.ds(RIM, columns), :] = dconv

    rows = []
    for block in (expand, project):
        total = block[:chan, :wide_e] + block[chan:, wide_e:]
        rows += [total[:, k * lanes : (k + 1) * lanes] for k in range(wide_e // lanes)]
    total = hidden[:, :wide_e] + hidden[:, wide_e:]
    fine = [total[:, k * lanes : (k + 1) * lanes] for k in range(wide_e // lanes)] + small
    fine.append(jnp.zeros((-len(fine) % 16, lanes), f32))
    rows = jnp.concatenate(rows + fine, axis=0)

    pad = jnp.zeros((edge_ref.shape[0] // (2 * half) - RIM, lanes), f32)
    first = [x for i in range(half) for x in (conv[i, :RIM, :], pad)]
    last = [x for i in range(half) for x in (conv[i, n_cols - RIM : n_cols, :], pad)]
    first = jnp.concatenate(first, axis=0)
    last = jnp.concatenate(last, axis=0)
    edges = [jnp.where(odd, first, last), jnp.where(odd, last, first)]
    edge_ref[...] = jnp.concatenate(edges, axis=0).astype(bf16)
    part = rows.shape[0] // 2
    upper_half = half_ref[0] == 1
    keep_ref[...] = jnp.where(upper_half, rows[part:], rows[:part])
    send_ref[...] = jnp.where(upper_half, rows[:part], rows[part:])


def tap_kernel(columns, ext_ref, left_ext, right_ext, grad_ref, sums_ref):
    half, lanes = grad_ref.shape[0], grad_ref.shape[2]
    base = ext_ref.shape[1] - right_ext.shape[1]

    def tile(total, field_ref, at, start):
        total = list(total)
        grads = [grad_ref[i, pl.ds(start + RIM, 8), :] for i in range(half)]
        for row in range(half + 2 * RIM):
            for b in range(TAPS):
                piece = field_ref[row, pl.ds(at + b, 8), :]
                for i in range(half):
                    a = row - i
                    if 0 <= a < TAPS:
                        total[a * TAPS + b] = total[a * TAPS + b] + grads[i] * piece
        return tuple(total)

    def trip(t, total):
        start = pl.multiple_of(t * 8, 8)
        return tile(total, ext_ref, start, start)

    total = tile((jnp.zeros((8, lanes), f32),) * (TAPS * TAPS), left_ext, 0, 0)
    for at in range(0, columns - base, 8):
        total = tile(total, right_ext, at, base + at)
    total = lax.fori_loop(1, base // 8, trip, total, unroll=2)
    rows = []
    for a in range(TAPS):
        rows += [jnp.sum(total[a * TAPS + b], axis=0, keepdims=True) for b in range(TAPS)]
        rows.append(jnp.zeros((1, lanes), f32))
    sums_ref[...] = jnp.concatenate(rows, axis=0)


def first_kernel(mine_ref, other_ref, taps_ref, edge_ref, send_ref):
    sums = jnp.concatenate([mine_ref[...] + other_ref[...], taps_ref[...]], axis=0)
    send_ref[: sums.shape[0]] = sums.astype(bf16)
    send_ref[sums.shape[0] :] = edge_ref[...]


def add_kernel(total, mine_ref, other_ref, send_ref):
    rim = send_ref.shape[0] - total
    send_ref[:total] = added(mine_ref, other_ref, total).astype(bf16)
    send_ref[total:] = other_ref[other_ref.shape[0] - rim :]


def rows_kernel(
    part, n_cols, lon_ref, lat_ref, early_ref, late_ref, dconv_ref, full_ref, send_ref, later_ref
):
    half = dconv_ref.shape[0]
    odd = lon_ref[0] == 1
    rim = (early_ref.shape[0] - part) // 2
    early = early_ref[part : part + rim].astype(f32)
    late = late_ref[late_ref.shape[0] - rim :].astype(f32)
    right = jnp.where(odd, late, early)
    left = jnp.where(odd, early, late)
    step = rim // half
    for i in range(half):
        full_ref[i] = dconv_ref[i]
        full_ref[i, :RIM, :] = left[i * step : i * step + RIM]
        full_ref[i, RIM + n_cols : 2 * RIM + n_cols, :] = right[i * step : i * step + RIM]
    put_rows(lambda i: full_ref[i], half, lat_ref[0] == 1, send_ref, 0, later_ref)


def rim_rows(lat_ref, pole_ref, early_ref, late_ref, at):
    mid = late_ref.shape[0] // RIM
    odd, pole = lat_ref[0] == 1, pole_ref[0] == 1

    def rows(k):
        early = early_ref[at + k * mid : at + (k + 1) * mid, :].astype(f32)
        late = late_ref[k * mid : (k + 1) * mid, :].astype(f32)
        return early, jnp.where(pole, 0.0, late)

    def top(k):
        early, late = rows(k)
        return jnp.where(odd, early, late)

    def bottom(k):
        early, late = rows(k)
        return jnp.where(odd, late, early)

    return top, bottom


def back_kernel(at, lat_ref, pole_ref, early_ref, late_ref, mid_ref, taps_ref, out_ref, ext32, wide):
    half, columns, lanes = out_ref.shape
    assemble(ext32, mid_ref, *rim_rows(lat_ref, pole_ref, early_ref, late_ref, at))
    fill_taps(taps_ref, wide, True)

    def put(i, start, value):
        out_ref[i, pl.ds(start, STEP), :] = value

    convolve(ext32, wide, put, half, columns, 2)


def finish_kernel(
    scale, half_ref, mine_ref, other_ref,
    taps_ref, conv_ref, gain_ref, bias_ref, expand_ref, hidden_ref, project_ref, wet_ref,
):
    lanes = mine_ref.shape[1]
    chan, wide_e = expand_ref.shape
    odd = half_ref[0] == 1
    mine, other = mine_ref[...] * scale, other_ref[...] * scale
    part = mine.shape[0] - 8 * TAPS
    taps = mine[part:] + other[part:]
    taps = taps[:, :chan] + taps[:, chan:]
    mine, other = mine[:part], other[:part]
    total = jnp.concatenate([jnp.where(odd, other, mine), jnp.where(odd, mine, other)], axis=0)
    blocks = wide_e // lanes
    small = total[2 * blocks * chan :]
    for k in range(blocks):
        expand_ref[:, k * lanes : (k + 1) * lanes] = total[k * chan : (k + 1) * chan]
        at = (blocks + k) * chan
        project_ref[:, k * lanes : (k + 1) * lanes] = total[at : at + chan]
        hidden_ref[:, k * lanes : (k + 1) * lanes] = small[k : k + 1]
    narrow = small[:, :chan] + small[:, chan:]
    for k, ref in enumerate((wet_ref, gain_ref, bias_ref, conv_ref)):
        ref[...] = narrow[blocks + k : blocks + k + 1]
    for a in range(TAPS):
        taps_ref[a] = taps[8 * a : 8 * a + TAPS]


def call(kernel, out_shape, scratch, flops, *args):
    vmem = pl.BlockSpec(memory_space=pltpu.VMEM)
    smem = pl.BlockSpec(memory_space=pltpu.SMEM)
    many = isinstance(out_shape, (list, tuple))
    return pl.pallas_call(
        kernel,
        out_shape=out_shape,
        in_specs=[smem if arg.dtype == jnp.int32 and arg.ndim == 1 else vmem for arg in args],
        out_specs=[vmem] * len(out_shape) if many else vmem,
        scratch_shapes=scratch,
        cost_estimate=pl.CostEstimate(flops=flops, bytes_accessed=1 << 20, transcendentals=0),
        compiler_params=pltpu.CompilerParams(vmem_limit_bytes=40 << 20),
    )(*args)


def body(
    state, land_sea, cotangent, kernel, conv_bias, ln_gain, ln_bias, w_expand, b_expand, w_project
):
    n_chan, n_rows, n_cols = state.shape
    n_wide = w_expand.shape[1]
    half = n_rows // 2
    lanes = 2 * n_chan
    columns = -(-n_cols // STEP) * STEP
    padded = -(-(columns + 2 * RIM) // 32) * 32
    total = 2 * n_chan * n_wide // lanes + -(-(n_wide // lanes + 4) // 16) * 16
    part = total // 2
    sums = part + 8 * TAPS
    rim = half * 4
    rows = RIM * padded // 2
    cells = n_rows * n_cols
    conv_flops = cells * n_chan * TAPS * TAPS * 2
    shaped = jax.ShapeDtypeStruct
    row = lambda v: v.reshape(1, -1)
    taps = kernel.transpose(1, 2, 0)
    odd_lon, odd_lat = lax.axis_index("lon") % 2, lax.axis_index("lat") % 2
    place, last_place = lax.axis_index("lat"), lax.axis_size("lat") - 1
    pole = ((place == 0) | (place == last_place)).astype(jnp.int32).reshape(1)
    on_lon, on_lat, keeps = odd_lon.reshape(1), odd_lat.reshape(1), kept_half().reshape(1)

    flat = shaped((rows, lanes), bf16)
    field, first, last = call(
        pack_kernel,
        [shaped((half, padded, lanes), bf16), flat, flat],
        [],
        cells * n_chan,
        on_lat, state.reshape(n_chan * n_rows, n_cols),
    )
    early = lax.ppermute(first, "lat", pairs("lat", 1))
    late = lax.ppermute(last, "lat", ring_pairs("lat"))
    wet = call(
        wet_kernel,
        shaped((half, columns, lanes), bf16),
        [],
        cells * n_chan,
        cotangent.reshape(n_chan * n_rows, n_cols), land_sea,
    )

    early, late, wet = lax.optimization_barrier((early, late, wet))
    side = shaped((4 * (half + 2 * RIM), lanes), bf16)
    first, last = call(
        functools.partial(edge_kernel, n_cols), [side, side], [], cells,
        on_lon, on_lat, pole, field, early, late,
    )
    before = lax.ppermute(first, "lon", pairs("lon", 1))
    after = lax.ppermute(last, "lon", ring_pairs("lon"))
    ext, conv, wide_taps = call(
        inner_kernel,
        [
            shaped((half + 2 * RIM, padded, lanes), f32),
            shaped((half, columns, lanes), f32),
            shaped((TAPS * TAPS, 8, lanes), f32),
        ],
        [],
        conv_flops,
        on_lat, pole, field, early, late, taps,
    )

    dconv, mine, send, edges, left_ext, right_ext = call(
        functools.partial(block_kernel, n_cols),
        [
            shaped((half, padded, lanes), f32),
            shaped((part, lanes), f32),
            shaped((part, lanes), f32),
            shaped((2 * rim, lanes), bf16),
            shaped((half + 2 * RIM, STEP + 8, lanes), f32),
            shaped((half + 2 * RIM, padded - (n_cols - RIM) // STEP * STEP, lanes), f32),
        ],
        [
            pltpu.VMEM((lanes, 2 * n_wide), bf16),
            pltpu.VMEM((lanes, 2 * n_wide), bf16),
            pltpu.VMEM((half, columns, lanes), f32),
        ],
        cells * n_chan * n_wide * 10 + conv_flops,
        on_lon, keeps, before, after, wet, wide_taps, row(conv_bias), row(ln_gain), row(ln_bias),
        w_expand, row(b_expand), w_project.T, ext, conv,
    )

    other = lax.ppermute(send, "lat", pairs("lat", 1))
    tap_total = call(
        functools.partial(tap_kernel, columns),
        shaped((8 * TAPS, lanes), f32),
        [],
        conv_flops,
        ext, left_ext, right_ext, dconv,
    )
    sent = shaped((sums + 2 * rim, lanes), bf16)
    mine = call(first_kernel, sent, [], part * lanes, mine, other, tap_total, edges)
    other = early = lax.ppermute(mine, "lon", pairs("lon", 1))
    add = functools.partial(add_kernel, sums)
    place, size = lax.axis_index("lon"), lax.axis_size("lon")
    apart = place ^ ((place + 2 * odd_lon - 1) % size)
    late = None
    for bit in bits("lon", 1):
        mine = call(add, shaped((sums + rim, lanes), bf16), [], part * lanes, mine, other)
        other = lax.ppermute(mine, "lon", pairs("lon", bit))
        late = other if late is None else jnp.where(apart == 2 * bit - 1, other, late)
    mine = added(mine, other, sums)
    row_shape = shaped((rows, lanes), bf16)
    full, first, last = call(
        functools.partial(rows_kernel, sums, n_cols),
        [shaped(dconv.shape, f32), row_shape, row_shape],
        [],
        cells * n_chan,
        on_lon, on_lat, early, late, dconv,
    )
    early = lax.ppermute(first, "lat", pairs("lat", 1))
    late = lax.ppermute(last, "lat", ring_pairs("lat"))
    for k, swaps in enumerate(half_rounds()):
        mine = mine + lax.ppermute(mine, "lat", swaps)
        if k == 0:
            late, _ = lax.optimization_barrier((late, mine))
    other = lax.ppermute(mine, "lat", pairs("lat", 1))

    grad = call(
        functools.partial(back_kernel, 0),
        shaped((half, columns, lanes), f32),
        [
            pltpu.VMEM((half + 2 * RIM, padded, lanes), f32),
            pltpu.VMEM((TAPS * TAPS, 8, lanes), f32),
        ],
        conv_flops,
        on_lat, pole, early, late, full, taps,
    )
    grad = unpack(grad)[:, :n_cols].transpose(2, 0, 1)
    state_grad = (cotangent.astype(f32) + grad).astype(bf16)

    scale = 1.0 / math.sqrt(cells * lax.axis_size("lat") * lax.axis_size("lon"))
    narrow = shaped((1, n_chan), f32)
    out = call(
        functools.partial(finish_kernel, scale),
        [
            shaped((TAPS, TAPS, n_chan), f32),
            narrow,
            narrow,
            narrow,
            shaped((n_chan, n_wide), f32),
            shaped((1, n_wide), f32),
            shaped((n_chan, n_wide), f32),
            narrow,
        ],
        [],
        total * lanes,
        keeps, mine, other,
    )
    return (
        state_grad,
        out[0].transpose(2, 0, 1),
        out[1].reshape(-1),
        out[2].reshape(-1),
        out[3].reshape(-1),
        out[4],
        out[5].reshape(-1),
        out[6].T,
        out[7].reshape(-1),
    )


def solution(mesh):
    in_specs = (
        P(None, "lat", "lon"),
        P("lat", "lon"),
        P(None, "lat", "lon"),
        P(),
        P(),
        P(),
        P(),
        P(),
        P(),
        P(),
    )
    out_specs = (P(None, "lat", "lon"), P(), P(), P(), P(), P(), P(), P(), P())
    return jax.shard_map(body, mesh=mesh, in_specs=in_specs, out_specs=out_specs, check_vma=False)
```

```python
import functools
import math

import jax
import jax.numpy as jnp
from jax import lax
from jax.experimental import pallas as pl
from jax.experimental.pallas import tpu as pltpu
from jax.sharding import PartitionSpec as P

TAPS = 7
RIM = 3
STEP = 16

ln_eps = 1e-06
root_half = 0.7071067811865476
inv_root_tau = 0.3989422804014327
f32 = jnp.float32
bf16 = jnp.bfloat16


def pairs(axis, bit):
    return [(i, i ^ bit) for i in range(lax.axis_size(axis))]


def ring_pairs(axis):
    size = lax.axis_size(axis)
    return [(i, (i + 1 if i % 2 else i - 1) % size) for i in range(size)]


def bits(axis, first):
    size = lax.axis_size(axis)
    if size < 4 or size & (size - 1):
        raise ValueError("axis size")
    return [1 << k for k in range(first, size.bit_length() - 1)]


def kept_half():
    place = lax.axis_index("lat")
    return sum(place // bit for bit in [1] + bits("lat", 1)) % 2


def half_rounds():
    steps = bits("lat", 1)
    turned = steps[1:] + steps[:1]
    size = lax.axis_size("lat")
    order = [turned if bin(i).count("1") % 2 else steps for i in range(size)]
    return [[(i, i ^ order[i][k] ^ 1) for i in range(size)] for k in range(len(steps))]


def unpack(field):
    chan = field.shape[2] // 2
    return jnp.concatenate([field[:, :, :chan], field[:, :, chan:]], axis=0)


def swap(value):
    return pltpu.roll(value, value.shape[-1] // 2, value.ndim - 1)


def assemble(ext_ref, mid_ref, top, bottom):
    half, columns, lanes = mid_ref.shape
    first = lax.broadcasted_iota(jnp.int32, (columns, lanes), 1) < lanes // 2
    for k in range(RIM):
        above, below = top(k), bottom(k)
        above = jnp.concatenate([above, swap(above)], axis=0)
        below = jnp.concatenate([swap(below), below], axis=0)
        upper = swap(mid_ref[half - RIM + k].astype(f32))
        lower = swap(mid_ref[k].astype(f32))
        ext_ref[k] = jnp.where(first, above, upper)
        ext_ref[half + RIM + k] = jnp.where(first, lower, below)
    for i in range(half):
        ext_ref[RIM + i] = mid_ref[i].astype(f32)


def added(mine_ref, other_ref, total):
    return mine_ref[:total].astype(f32) + other_ref[:total].astype(f32)


def fill_taps(taps_ref, wide_ref, flip):
    chan = taps_ref.shape[2]
    for a in range(TAPS):
        for b in range(TAPS):
            row = taps_ref[TAPS - 1 - a, TAPS - 1 - b, :] if flip else taps_ref[a, b, :]
            row = row.reshape(1, chan)
            row = jnp.concatenate([row, row], axis=1)
            wide_ref[a * TAPS + b] = jnp.broadcast_to(row, (8, 2 * chan))


def convolve_tile(ext_ref, wide_ref, store, half, start):
    tiles = STEP // 8
    total = [[None] * tiles for _ in range(half)]
    for row in range(half + 2 * RIM):
        for b in range(TAPS):
            piece = [ext_ref[row, pl.ds(start + b + 8 * s, 8), :] for s in range(tiles)]
            for i in range(half):
                a = row - i
                if 0 <= a < TAPS:
                    weight = wide_ref[a * TAPS + b]
                    for s in range(tiles):
                        term = weight * piece[s]
                        total[i][s] = term if total[i][s] is None else total[i][s] + term
    for i in range(half):
        store(i, start, jnp.concatenate(total[i], axis=0))


def convolve(ext_ref, wide_ref, store, half, columns, unroll):
    def trip(t, carry):
        convolve_tile(ext_ref, wide_ref, store, half, pl.multiple_of(t * STEP, STEP))
        return carry

    lax.fori_loop(0, columns // STEP, trip, 0, unroll=unroll)


def group_mean(values, ones):
    high = values.astype(bf16)
    low = (values - high.astype(f32)).astype(bf16)
    return jnp.dot(jnp.concatenate([high, low], axis=1), ones, preferred_element_type=f32)


def put_rows(packed, half, odd, send_ref, at, later_ref):
    wide, lanes = packed(0).shape
    mid = wide // 2
    first = lax.broadcasted_iota(jnp.int32, (mid, lanes), 1) < lanes // 2
    for k in range(RIM):
        upper, lower = packed(k), packed(half - RIM + k)
        upper = jnp.where(first, upper[:mid], swap(upper[mid:]))
        lower = jnp.where(first, swap(lower[:mid]), lower[mid:])
        send_ref[at + k * mid : at + (k + 1) * mid, :] = jnp.where(odd, upper, lower).astype(bf16)
        later_ref[k * mid : (k + 1) * mid, :] = jnp.where(odd, lower, upper).astype(bf16)


def packed_rows(field, half, lanes):
    count = field.shape[0]
    shape = (count // (2 * half), 2 * half, lanes)
    chan = lax.broadcasted_iota(jnp.int32, shape, 0)
    row = lax.broadcasted_iota(jnp.int32, shape, 1)
    lane = lax.broadcasted_iota(jnp.int32, shape, 2)
    lower = row >= half
    row = jnp.where(lower, row - half, row)
    here = lane == jnp.where(lower, chan + lanes // 2, chan)
    packed = []
    for i in range(half):
        pick = jnp.where(here & (row == i), 1.0, 0.0).reshape(count, lanes).astype(bf16)
        packed.append(
            lax.dot_general(field, pick, (((0,), (0,)), ((), ())), preferred_element_type=f32)
        )
    return packed


def pack_kernel(lat_ref, state_ref, mid_ref, send_ref, later_ref):
    half, wide, lanes = mid_ref.shape
    n_cols = state_ref.shape[1]
    fields = []
    for i, field in enumerate(packed_rows(state_ref[...], half, lanes)):
        before = jnp.zeros((RIM, lanes), f32)
        after = jnp.zeros((wide - RIM - n_cols, lanes), f32)
        fields.append(jnp.concatenate([before, field, after], axis=0))
        mid_ref[i] = fields[i].astype(bf16)
    put_rows(lambda i: fields[i], half, lat_ref[0] == 1, send_ref, 0, later_ref)


def wet_kernel(cot_ref, sea_ref, wet_ref):
    half, columns, lanes = wet_ref.shape
    n_rows, n_cols = sea_ref.shape
    cot = cot_ref[...].astype(f32).reshape(-1, n_rows, n_cols) * sea_ref[...].astype(f32)
    cot = cot.reshape(-1, n_cols).astype(bf16)
    for i, field in enumerate(packed_rows(cot, half, lanes)):
        after = jnp.zeros((columns - n_cols, lanes), f32)
        wet_ref[i] = jnp.concatenate([field, after], axis=0).astype(bf16)


def edge_kernel(n_cols, lon_ref, lat_ref, pole_ref, mid_ref, late_ref, early_ref, later_ref, send_ref):
    half, wide, lanes = mid_ref.shape
    mid = wide // 2
    odd_lat, odd_lon, pole = lat_ref[0] == 1, lon_ref[0] == 1, pole_ref[0] == 1
    base = n_cols // 16 * 16
    skip = n_cols - base
    first = lax.broadcasted_iota(jnp.int32, (8, lanes), 1) < lanes // 2
    left, right = [], []
    for i in range(half):
        left.append(mid_ref[i, :16, :].astype(f32)[:8])
        right.append(mid_ref[i, base : base + 32, :].astype(f32)[skip : skip + 8])
    ends = [([], []), ([], [])]
    for k in range(RIM):
        at = k * mid
        one, two = [], []
        for ref in (early_ref, late_ref):
            one.append(ref[at : at + 16, :].astype(f32)[:8])
            two.append(ref[at + base - mid : at + mid, :].astype(f32)[skip : skip + 8])
        one[1], two[1] = jnp.where(pole, 0.0, one[1]), jnp.where(pole, 0.0, two[1])
        above = jnp.where(odd_lat, one[0], one[1]), jnp.where(odd_lat, two[0], two[1])
        below = jnp.where(odd_lat, one[1], one[0]), jnp.where(odd_lat, two[1], two[0])
        ends[0][0].append(jnp.where(first, above[0], swap(left[half - RIM + k])))
        ends[0][1].append(jnp.where(first, swap(above[1]), swap(right[half - RIM + k])))
        ends[1][0].append(jnp.where(first, swap(left[k]), swap(below[0])))
        ends[1][1].append(jnp.where(first, swap(right[k]), below[1]))
    left = ends[0][0] + left + ends[1][0]
    right = ends[0][1] + right + ends[1][1]
    left = jnp.concatenate([x[RIM : RIM + 4] for x in left], axis=0)
    right = jnp.concatenate([x[:4] for x in right], axis=0)
    send_ref[...] = jnp.where(odd_lon, left, right).astype(bf16)
    later_ref[...] = jnp.where(odd_lon, right, left).astype(bf16)


def inner_kernel(lat_ref, pole_ref, mid_ref, early_ref, late_ref, taps_ref, ext_ref, conv_ref, wide_ref):
    half, columns, lanes = conv_ref.shape
    assemble(ext_ref, mid_ref, *rim_rows(lat_ref, pole_ref, early_ref, late_ref, 0))
    fill_taps(taps_ref, wide_ref, False)

    def put(i, start, value):
        conv_ref[i, pl.ds(start, STEP), :] = value

    convolve(ext_ref, wide_ref, put, half, columns, 1)


def block_kernel(
    n_cols, lon_ref, half_ref, late_ref, early_ref, wet_ref, wide,
    conv_bias_ref, gain_ref, bias_ref, w1_ref, b1_ref, w2_ref, ext_ref, conv_ref,
    dconv_ref, keep_ref, send_ref, edge_ref, left_ext, right_ext, w1, w2, conv,
):
    half, columns, lanes = wet_ref.shape
    chan = lanes // 2
    wide_e = w1_ref.shape[1]
    odd = lon_ref[0] == 1
    one, two = early_ref[...].astype(f32), late_ref[...].astype(f32)
    left, right = jnp.where(odd, one, two), jnp.where(odd, two, one)
    base = ext_ref.shape[1] - right_ext.shape[1]
    at = RIM + n_cols - base
    for row in range(half + 2 * RIM):
        left_ext[row] = ext_ref[row, : left_ext.shape[1], :]
        right_ext[row] = ext_ref[row, base:, :]
        left_ext[row, :RIM, :] = left[4 * row : 4 * row + RIM]
        right_ext[row, at : at + RIM, :] = right[4 * row : 4 * row + RIM]

    def put_left(i, start, value):
        conv[i, :STEP, :] = value

    def put_right(i, start, value):
        conv[i, base + start : base + start + STEP, :] = value

    convolve_tile(left_ext, wide, put_left, half, 0)
    for start in range(0, columns - base, STEP):
        convolve_tile(right_ext, wide, put_right, half, start)
    conv[:, STEP:base, :] = conv_ref[:, STEP:base, :]
    w1[...] = jnp.zeros_like(w1)
    w2[...] = jnp.zeros_like(w2)
    w1[:chan, :wide_e] = w1_ref[...]
    w1[chan:, wide_e:] = w1_ref[...]
    w2[:chan, :wide_e] = w2_ref[...]
    w2[chan:, wide_e:] = w2_ref[...]
    dconv_ref[...] = jnp.zeros_like(dconv_ref)

    row_half = lax.broadcasted_iota(jnp.int32, (2 * lanes, lanes), 0) % lanes >= chan
    col_half = lax.broadcasted_iota(jnp.int32, (2 * lanes, lanes), 1) >= chan
    ones = jnp.where(row_half == col_half, 1.0 / chan, 0.0).astype(bf16)
    conv_bias, gain, bias, hidden_bias = (
        jnp.concatenate([ref[...], ref[...]], axis=1)
        for ref in (conv_bias_ref, gain_ref, bias_ref, b1_ref)
    )

    cells_all = half * columns
    out = conv[...].reshape(cells_all, lanes) + conv_bias
    wet = wet_ref[...].reshape(cells_all, lanes)
    center = out - group_mean(out, ones)
    rstd = lax.rsqrt(group_mean(center * center, ones) + ln_eps)
    normed = center * rstd
    zed = (normed * gain + bias).astype(bf16)
    pre = jnp.dot(zed, w1[...], preferred_element_type=f32) + hidden_bias
    dact = jnp.dot(wet, w2[...], preferred_element_type=f32)
    phi = 0.5 + 0.5 * lax.erf(pre * root_half)
    act = (pre * phi).astype(bf16)
    dhid = (dact * (phi + pre * (jnp.exp(-0.5 * pre * pre) * inv_root_tau))).astype(bf16)
    dzed = lax.dot_general(dhid, w1[...], (((1,), (1,)), ((), ())), preferred_element_type=f32)
    rows_first = (((0,), (0,)), ((), ()))
    expand = lax.dot_general(zed, dhid, rows_first, preferred_element_type=f32)
    project = lax.dot_general(wet, act, rows_first, preferred_element_type=f32)
    dnorm = dzed * gain
    mean1 = group_mean(dnorm, ones)
    mean2 = group_mean(dnorm * normed, ones)
    dconv = rstd * (dnorm - mean1 - normed * mean2)
    count = jnp.ones((cells_all, 16), bf16)
    hidden = lax.dot_general(count, dhid, rows_first, preferred_element_type=f32)[:1]
    parts = (wet.astype(f32), dzed * normed, dzed, dconv)
    small = [jnp.sum(part, axis=0, keepdims=True) for part in parts]
    dconv = dconv.reshape(half, columns, lanes)
    conv[...] = dconv
    dconv_ref[:, pl.ds(RIM, columns), :] = dconv

    rows = []
    for block in (expand, project):
        total = block[:chan, :wide_e] + block[chan:, wide_e:]
        rows += [total[:, k * lanes : (k + 1) * lanes] for k in range(wide_e // lanes)]
    total = hidden[:, :wide_e] + hidden[:, wide_e:]
    fine = [total[:, k * lanes : (k + 1) * lanes] for k in range(wide_e // lanes)] + small
    fine.append(jnp.zeros((-len(fine) % 16, lanes), f32))
    rows = jnp.concatenate(rows + fine, axis=0)

    pad = jnp.zeros((edge_ref.shape[0] // (2 * half) - RIM, lanes), f32)
    first = [x for i in range(half) for x in (conv[i, :RIM, :], pad)]
    last = [x for i in range(half) for x in (conv[i, n_cols - RIM : n_cols, :], pad)]
    first = jnp.concatenate(first, axis=0)
    last = jnp.concatenate(last, axis=0)
    edges = [jnp.where(odd, first, last), jnp.where(odd, last, first)]
    edge_ref[...] = jnp.concatenate(edges, axis=0).astype(bf16)
    part = rows.shape[0] // 2
    upper_half = half_ref[0] == 1
    keep_ref[...] = jnp.where(upper_half, rows[part:], rows[:part])
    send_ref[...] = jnp.where(upper_half, rows[:part], rows[part:])


def tap_kernel(columns, ext_ref, left_ext, right_ext, grad_ref, sums_ref):
    half, lanes = grad_ref.shape[0], grad_ref.shape[2]
    base = ext_ref.shape[1] - right_ext.shape[1]

    def tile(total, field_ref, at, start):
        total = list(total)
        grads = [grad_ref[i, pl.ds(start + RIM, 8), :] for i in range(half)]
        for row in range(half + 2 * RIM):
            for b in range(TAPS):
                piece = field_ref[row, pl.ds(at + b, 8), :]
                for i in range(half):
                    a = row - i
                    if 0 <= a < TAPS:
                        total[a * TAPS + b] = total[a * TAPS + b] + grads[i] * piece
        return tuple(total)

    def trip(t, total):
        start = pl.multiple_of(t * 8, 8)
        return tile(total, ext_ref, start, start)

    total = tile((jnp.zeros((8, lanes), f32),) * (TAPS * TAPS), left_ext, 0, 0)
    for at in range(0, columns - base, 8):
        total = tile(total, right_ext, at, base + at)
    total = lax.fori_loop(1, base // 8, trip, total, unroll=2)
    rows = []
    for a in range(TAPS):
        rows += [jnp.sum(total[a * TAPS + b], axis=0, keepdims=True) for b in range(TAPS)]
        rows.append(jnp.zeros((1, lanes), f32))
    sums_ref[...] = jnp.concatenate(rows, axis=0)


def first_kernel(mine_ref, other_ref, taps_ref, edge_ref, send_ref):
    sums = jnp.concatenate([mine_ref[...] + other_ref[...], taps_ref[...]], axis=0)
    send_ref[: sums.shape[0]] = sums.astype(bf16)
    send_ref[sums.shape[0] :] = edge_ref[...]


def add_kernel(total, mine_ref, other_ref, send_ref):
    rim = send_ref.shape[0] - total
    send_ref[:total] = added(mine_ref, other_ref, total).astype(bf16)
    send_ref[total:] = other_ref[other_ref.shape[0] - rim :]


def rows_kernel(
    part, n_cols, lon_ref, lat_ref, early_ref, late_ref, dconv_ref, full_ref, send_ref, later_ref
):
    half = dconv_ref.shape[0]
    odd = lon_ref[0] == 1
    rim = (early_ref.shape[0] - part) // 2
    early = early_ref[part : part + rim].astype(f32)
    late = late_ref[late_ref.shape[0] - rim :].astype(f32)
    right = jnp.where(odd, late, early)
    left = jnp.where(odd, early, late)
    step = rim // half
    for i in range(half):
        full_ref[i] = dconv_ref[i]
        full_ref[i, :RIM, :] = left[i * step : i * step + RIM]
        full_ref[i, RIM + n_cols : 2 * RIM + n_cols, :] = right[i * step : i * step + RIM]
    put_rows(lambda i: full_ref[i], half, lat_ref[0] == 1, send_ref, 0, later_ref)


def rim_rows(lat_ref, pole_ref, early_ref, late_ref, at):
    mid = late_ref.shape[0] // RIM
    odd, pole = lat_ref[0] == 1, pole_ref[0] == 1

    def rows(k):
        early = early_ref[at + k * mid : at + (k + 1) * mid, :].astype(f32)
        late = late_ref[k * mid : (k + 1) * mid, :].astype(f32)
        return early, jnp.where(pole, 0.0, late)

    def top(k):
        early, late = rows(k)
        return jnp.where(odd, early, late)

    def bottom(k):
        early, late = rows(k)
        return jnp.where(odd, late, early)

    return top, bottom


def back_kernel(at, lat_ref, pole_ref, early_ref, late_ref, mid_ref, taps_ref, out_ref, ext32, wide):
    half, columns, lanes = out_ref.shape
    assemble(ext32, mid_ref, *rim_rows(lat_ref, pole_ref, early_ref, late_ref, at))
    fill_taps(taps_ref, wide, True)

    def put(i, start, value):
        out_ref[i, pl.ds(start, STEP), :] = value

    convolve(ext32, wide, put, half, columns, 2)


def finish_kernel(
    scale, half_ref, mine_ref, other_ref,
    taps_ref, conv_ref, gain_ref, bias_ref, expand_ref, hidden_ref, project_ref, wet_ref,
):
    lanes = mine_ref.shape[1]
    chan, wide_e = expand_ref.shape
    odd = half_ref[0] == 1
    mine, other = mine_ref[...] * scale, other_ref[...] * scale
    part = mine.shape[0] - 8 * TAPS
    taps = mine[part:] + other[part:]
    taps = taps[:, :chan] + taps[:, chan:]
    mine, other = mine[:part], other[:part]
    total = jnp.concatenate([jnp.where(odd, other, mine), jnp.where(odd, mine, other)], axis=0)
    blocks = wide_e // lanes
    small = total[2 * blocks * chan :]
    for k in range(blocks):
        expand_ref[:, k * lanes : (k + 1) * lanes] = total[k * chan : (k + 1) * chan]
        at = (blocks + k) * chan
        project_ref[:, k * lanes : (k + 1) * lanes] = total[at : at + chan]
        hidden_ref[:, k * lanes : (k + 1) * lanes] = small[k : k + 1]
    narrow = small[:, :chan] + small[:, chan:]
    for k, ref in enumerate((wet_ref, gain_ref, bias_ref, conv_ref)):
        ref[...] = narrow[blocks + k : blocks + k + 1]
    for a in range(TAPS):
        taps_ref[a] = taps[8 * a : 8 * a + TAPS]


def call(kernel, out_shape, scratch, flops, *args):
    vmem = pl.BlockSpec(memory_space=pltpu.VMEM)
    smem = pl.BlockSpec(memory_space=pltpu.SMEM)
    many = isinstance(out_shape, (list, tuple))
    return pl.pallas_call(
        kernel,
        out_shape=out_shape,
        in_specs=[smem if arg.dtype == jnp.int32 and arg.ndim == 1 else vmem for arg in args],
        out_specs=[vmem] * len(out_shape) if many else vmem,
        scratch_shapes=scratch,
        cost_estimate=pl.CostEstimate(flops=flops, bytes_accessed=1 << 20, transcendentals=0),
        compiler_params=pltpu.CompilerParams(vmem_limit_bytes=40 << 20),
    )(*args)


def body(
    state, land_sea, cotangent, kernel, conv_bias, ln_gain, ln_bias, w_expand, b_expand, w_project
):
    n_chan, n_rows, n_cols = state.shape
    n_wide = w_expand.shape[1]
    half = n_rows // 2
    lanes = 2 * n_chan
    columns = -(-n_cols // STEP) * STEP
    padded = -(-(columns + 2 * RIM) // 32) * 32
    total = 2 * n_chan * n_wide // lanes + -(-(n_wide // lanes + 4) // 16) * 16
    part = total // 2
    sums = part + 8 * TAPS
    rim = half * 4
    rows = RIM * padded // 2
    cells = n_rows * n_cols
    conv_flops = cells * n_chan * TAPS * TAPS * 2
    shaped = jax.ShapeDtypeStruct
    row = lambda v: v.reshape(1, -1)
    taps = kernel.transpose(1, 2, 0)
    odd_lon, odd_lat = lax.axis_index("lon") % 2, lax.axis_index("lat") % 2
    place, last_place = lax.axis_index("lat"), lax.axis_size("lat") - 1
    pole = ((place == 0) | (place == last_place)).astype(jnp.int32).reshape(1)
    on_lon, on_lat, keeps = odd_lon.reshape(1), odd_lat.reshape(1), kept_half().reshape(1)

    flat = shaped((rows, lanes), bf16)
    field, first, last = call(
        pack_kernel,
        [shaped((half, padded, lanes), bf16), flat, flat],
        [],
        cells * n_chan,
        on_lat, state.reshape(n_chan * n_rows, n_cols),
    )
    late = lax.ppermute(last, "lat", ring_pairs("lat"))
    early = lax.ppermute(first, "lat", pairs("lat", 1))
    wet = call(
        wet_kernel,
        shaped((half, columns, lanes), bf16),
        [],
        cells * n_chan,
        cotangent.reshape(n_chan * n_rows, n_cols), land_sea,
    )

    late, early, wet = lax.optimization_barrier((late, early, wet))
    side = shaped((4 * (half + 2 * RIM), lanes), bf16)
    last, first = call(
        functools.partial(edge_kernel, n_cols), [side, side], [], cells,
        on_lon, on_lat, pole, field, late, early,
    )
    after = lax.ppermute(last, "lon", ring_pairs("lon"))
    before = lax.ppermute(first, "lon", pairs("lon", 1))
    ext, conv, wide_taps = call(
        inner_kernel,
        [
            shaped((half + 2 * RIM, padded, lanes), f32),
            shaped((half, columns, lanes), f32),
            shaped((TAPS * TAPS, 8, lanes), f32),
        ],
        [],
        conv_flops,
        on_lat, pole, field, early, late, taps,
    )

    dconv, mine, send, edges, left_ext, right_ext = call(
        functools.partial(block_kernel, n_cols),
        [
            shaped((half, padded, lanes), f32),
            shaped((part, lanes), f32),
            shaped((part, lanes), f32),
            shaped((2 * rim, lanes), bf16),
            shaped((half + 2 * RIM, STEP + 8, lanes), f32),
            shaped((half + 2 * RIM, padded - (n_cols - RIM) // STEP * STEP, lanes), f32),
        ],
        [
            pltpu.VMEM((lanes, 2 * n_wide), bf16),
            pltpu.VMEM((lanes, 2 * n_wide), bf16),
            pltpu.VMEM((half, columns, lanes), f32),
        ],
        cells * n_chan * n_wide * 10 + conv_flops,
        on_lon, keeps, after, before, wet, wide_taps, row(conv_bias), row(ln_gain), row(ln_bias),
        w_expand, row(b_expand), w_project.T, ext, conv,
    )

    other = lax.ppermute(send, "lat", pairs("lat", 1))
    tap_total = call(
        functools.partial(tap_kernel, columns),
        shaped((8 * TAPS, lanes), f32),
        [],
        conv_flops,
        ext, left_ext, right_ext, dconv,
    )
    sent = shaped((sums + 2 * rim, lanes), bf16)
    mine = call(first_kernel, sent, [], part * lanes, mine, other, tap_total, edges)
    other = early = lax.ppermute(mine, "lon", pairs("lon", 1))
    add = functools.partial(add_kernel, sums)
    place, size = lax.axis_index("lon"), lax.axis_size("lon")
    apart = place ^ ((place + 2 * odd_lon - 1) % size)
    late = None
    for bit in bits("lon", 1):
        mine = call(add, shaped((sums + rim, lanes), bf16), [], part * lanes, mine, other)
        other = lax.ppermute(mine, "lon", pairs("lon", bit))
        late = other if late is None else jnp.where(apart == 2 * bit - 1, other, late)
    mine = added(mine, other, sums)
    row_shape = shaped((rows, lanes), bf16)
    full, first, last = call(
        functools.partial(rows_kernel, sums, n_cols),
        [shaped(dconv.shape, f32), row_shape, row_shape],
        [],
        cells * n_chan,
        on_lon, on_lat, early, late, dconv,
    )
    early = lax.ppermute(first, "lat", pairs("lat", 1))
    late = lax.ppermute(last, "lat", ring_pairs("lat"))
    for k, swaps in enumerate(half_rounds()):
        mine = mine + lax.ppermute(mine, "lat", swaps)
        if k == 0:
            late, _ = lax.optimization_barrier((late, mine))
    other = lax.ppermute(mine, "lat", pairs("lat", 1))

    grad = call(
        functools.partial(back_kernel, 0),
        shaped((half, columns, lanes), f32),
        [
            pltpu.VMEM((half + 2 * RIM, padded, lanes), f32),
            pltpu.VMEM((TAPS * TAPS, 8, lanes), f32),
        ],
        conv_flops,
        on_lat, pole, early, late, full, taps,
    )
    grad = unpack(grad)[:, :n_cols].transpose(2, 0, 1)
    state_grad = (cotangent.astype(f32) + grad).astype(bf16)

    scale = 1.0 / math.sqrt(cells * lax.axis_size("lat") * lax.axis_size("lon"))
    narrow = shaped((1, n_chan), f32)
    out = call(
        functools.partial(finish_kernel, scale),
        [
            shaped((TAPS, TAPS, n_chan), f32),
            narrow,
            narrow,
            narrow,
            shaped((n_chan, n_wide), f32),
            shaped((1, n_wide), f32),
            shaped((n_chan, n_wide), f32),
            narrow,
        ],
        [],
        total * lanes,
        keeps, mine, other,
    )
    return (
        state_grad,
        out[0].transpose(2, 0, 1),
        out[1].reshape(-1),
        out[2].reshape(-1),
        out[3].reshape(-1),
        out[4],
        out[5].reshape(-1),
        out[6].T,
        out[7].reshape(-1),
    )


def solution(mesh):
    in_specs = (
        P(None, "lat", "lon"),
        P("lat", "lon"),
        P(None, "lat", "lon"),
        P(),
        P(),
        P(),
        P(),
        P(),
        P(),
        P(),
    )
    out_specs = (P(None, "lat", "lon"), P(), P(), P(), P(), P(), P(), P(), P())
    return jax.shard_map(body, mesh=mesh, in_specs=in_specs, out_specs=out_specs, check_vma=False)
```

```python
import functools
import math

import jax
import jax.numpy as jnp
from jax import lax
from jax.experimental import pallas as pl
from jax.experimental.pallas import tpu as pltpu
from jax.sharding import PartitionSpec as P

TAPS = 7
RIM = 3
STEP = 16

ln_eps = 1e-06
root_half = 0.7071067811865476
inv_root_tau = 0.3989422804014327
f32 = jnp.float32
bf16 = jnp.bfloat16


def pairs(axis, bit):
    return [(i, i ^ bit) for i in range(lax.axis_size(axis))]


def ring_pairs(axis):
    size = lax.axis_size(axis)
    return [(i, (i + 1 if i % 2 else i - 1) % size) for i in range(size)]


def bits(axis, first):
    size = lax.axis_size(axis)
    if size < 4 or size & (size - 1):
        raise ValueError("axis size")
    return [1 << k for k in range(first, size.bit_length() - 1)]


def kept_half():
    place = lax.axis_index("lat")
    return sum(place // bit for bit in [1] + bits("lat", 1)) % 2


def half_rounds():
    steps = bits("lat", 1)
    turned = steps[1:] + steps[:1]
    size = lax.axis_size("lat")
    order = [turned if bin(i).count("1") % 2 else steps for i in range(size)]
    return [[(i, i ^ order[i][k] ^ 1) for i in range(size)] for k in range(len(steps))]


def swap(value):
    return pltpu.roll(value, value.shape[-1] // 2, value.ndim - 1)


def assemble(ext_ref, mid_ref, top, bottom):
    half, columns, lanes = mid_ref.shape
    first = lax.broadcasted_iota(jnp.int32, (columns, lanes), 1) < lanes // 2
    for k in range(RIM):
        above, below = top(k), bottom(k)
        above = jnp.concatenate([above, swap(above)], axis=0)
        below = jnp.concatenate([swap(below), below], axis=0)
        upper = swap(mid_ref[half - RIM + k].astype(f32))
        lower = swap(mid_ref[k].astype(f32))
        ext_ref[k] = jnp.where(first, above, upper)
        ext_ref[half + RIM + k] = jnp.where(first, lower, below)
    for i in range(half):
        ext_ref[RIM + i] = mid_ref[i].astype(f32)


def added(mine_ref, other_ref, total):
    return mine_ref[:total].astype(f32) + other_ref[:total].astype(f32)


def fill_taps(taps_ref, wide_ref, flip):
    chan = taps_ref.shape[2]
    for a in range(TAPS):
        for b in range(TAPS):
            row = taps_ref[TAPS - 1 - a, TAPS - 1 - b, :] if flip else taps_ref[a, b, :]
            row = row.reshape(1, chan)
            row = jnp.concatenate([row, row], axis=1)
            wide_ref[a * TAPS + b] = jnp.broadcast_to(row, (8, 2 * chan))


def convolve_tile(ext_ref, wide_ref, store, half, start):
    tiles = STEP // 8
    total = [[None] * tiles for _ in range(half)]
    for row in range(half + 2 * RIM):
        for b in range(TAPS):
            piece = [ext_ref[row, pl.ds(start + b + 8 * s, 8), :] for s in range(tiles)]
            for i in range(half):
                a = row - i
                if 0 <= a < TAPS:
                    weight = wide_ref[a * TAPS + b]
                    for s in range(tiles):
                        term = weight * piece[s]
                        total[i][s] = term if total[i][s] is None else total[i][s] + term
    for i in range(half):
        store(i, start, jnp.concatenate(total[i], axis=0))


def convolve(ext_ref, wide_ref, store, half, columns, unroll):
    def trip(t, carry):
        convolve_tile(ext_ref, wide_ref, store, half, pl.multiple_of(t * STEP, STEP))
        return carry

    lax.fori_loop(0, columns // STEP, trip, 0, unroll=unroll)


def group_mean(values, ones):
    high = values.astype(bf16)
    low = (values - high.astype(f32)).astype(bf16)
    return jnp.dot(jnp.concatenate([high, low], axis=1), ones, preferred_element_type=f32)


def put_rows(packed, half, odd, send_ref, at, later_ref):
    wide, lanes = packed(0).shape
    mid = wide // 2
    first = lax.broadcasted_iota(jnp.int32, (mid, lanes), 1) < lanes // 2
    for k in range(RIM):
        upper, lower = packed(k), packed(half - RIM + k)
        upper = jnp.where(first, upper[:mid], swap(upper[mid:]))
        lower = jnp.where(first, swap(lower[:mid]), lower[mid:])
        send_ref[at + k * mid : at + (k + 1) * mid, :] = jnp.where(odd, upper, lower).astype(bf16)
        later_ref[k * mid : (k + 1) * mid, :] = jnp.where(odd, lower, upper).astype(bf16)


def packed_rows(field, half, lanes):
    count = field.shape[0]
    shape = (count // (2 * half), 2 * half, lanes)
    chan = lax.broadcasted_iota(jnp.int32, shape, 0)
    row = lax.broadcasted_iota(jnp.int32, shape, 1)
    lane = lax.broadcasted_iota(jnp.int32, shape, 2)
    lower = row >= half
    row = jnp.where(lower, row - half, row)
    here = lane == jnp.where(lower, chan + lanes // 2, chan)
    packed = []
    for i in range(half):
        pick = jnp.where(here & (row == i), 1.0, 0.0).reshape(count, lanes).astype(bf16)
        packed.append(
            lax.dot_general(field, pick, (((0,), (0,)), ((), ())), preferred_element_type=f32)
        )
    return packed


def pack_kernel(lat_ref, state_ref, mid_ref, send_ref, later_ref):
    half, wide, lanes = mid_ref.shape
    n_cols = state_ref.shape[1]
    fields = []
    for i, field in enumerate(packed_rows(state_ref[...], half, lanes)):
        before = jnp.zeros((RIM, lanes), f32)
        after = jnp.zeros((wide - RIM - n_cols, lanes), f32)
        fields.append(jnp.concatenate([before, field, after], axis=0))
        mid_ref[i] = fields[i].astype(bf16)
    put_rows(lambda i: fields[i], half, lat_ref[0] == 1, send_ref, 0, later_ref)


def wet_kernel(cot_ref, sea_ref, wet_ref):
    half, columns, lanes = wet_ref.shape
    n_rows, n_cols = sea_ref.shape
    cot = cot_ref[...].astype(f32).reshape(-1, n_rows, n_cols) * sea_ref[...].astype(f32)
    cot = cot.reshape(-1, n_cols).astype(bf16)
    for i, field in enumerate(packed_rows(cot, half, lanes)):
        after = jnp.zeros((columns - n_cols, lanes), f32)
        wet_ref[i] = jnp.concatenate([field, after], axis=0).astype(bf16)


def edge_kernel(n_cols, lon_ref, lat_ref, pole_ref, mid_ref, late_ref, early_ref, later_ref, send_ref):
    half, wide, lanes = mid_ref.shape
    mid = wide // 2
    odd_lat, odd_lon, pole = lat_ref[0] == 1, lon_ref[0] == 1, pole_ref[0] == 1
    base = n_cols // 16 * 16
    skip = n_cols - base
    first = lax.broadcasted_iota(jnp.int32, (8, lanes), 1) < lanes // 2
    left, right = [], []
    for i in range(half):
        left.append(mid_ref[i, :16, :].astype(f32)[:8])
        right.append(mid_ref[i, base : base + 32, :].astype(f32)[skip : skip + 8])
    ends = [([], []), ([], [])]
    for k in range(RIM):
        at = k * mid
        one, two = [], []
        for ref in (early_ref, late_ref):
            one.append(ref[at : at + 16, :].astype(f32)[:8])
            two.append(ref[at + base - mid : at + mid, :].astype(f32)[skip : skip + 8])
        one[1], two[1] = jnp.where(pole, 0.0, one[1]), jnp.where(pole, 0.0, two[1])
        above = jnp.where(odd_lat, one[0], one[1]), jnp.where(odd_lat, two[0], two[1])
        below = jnp.where(odd_lat, one[1], one[0]), jnp.where(odd_lat, two[1], two[0])
        ends[0][0].append(jnp.where(first, above[0], swap(left[half - RIM + k])))
        ends[0][1].append(jnp.where(first, swap(above[1]), swap(right[half - RIM + k])))
        ends[1][0].append(jnp.where(first, swap(left[k]), swap(below[0])))
        ends[1][1].append(jnp.where(first, swap(right[k]), below[1]))
    left = ends[0][0] + left + ends[1][0]
    right = ends[0][1] + right + ends[1][1]
    left = jnp.concatenate([x[RIM : RIM + 4] for x in left], axis=0)
    right = jnp.concatenate([x[:4] for x in right], axis=0)
    send_ref[...] = jnp.where(odd_lon, left, right).astype(bf16)
    later_ref[...] = jnp.where(odd_lon, right, left).astype(bf16)


def inner_kernel(lat_ref, pole_ref, mid_ref, early_ref, late_ref, taps_ref, ext_ref, conv_ref, wide_ref):
    half, columns, lanes = conv_ref.shape
    assemble(ext_ref, mid_ref, *rim_rows(lat_ref, pole_ref, early_ref, late_ref, 0))
    fill_taps(taps_ref, wide_ref, False)

    def put(i, start, value):
        conv_ref[i, pl.ds(start, STEP), :] = value

    convolve(ext_ref, wide_ref, put, half, columns, 1)


def block_kernel(
    n_cols, lon_ref, half_ref, late_ref, early_ref, wet_ref, wide,
    conv_bias_ref, gain_ref, bias_ref, w1_ref, b1_ref, w2_ref, ext_ref, conv_ref,
    dconv_ref, keep_ref, send_ref, edge_ref, left_ext, right_ext, w1, w2, conv,
):
    half, columns, lanes = wet_ref.shape
    chan = lanes // 2
    wide_e = w1_ref.shape[1]
    odd = lon_ref[0] == 1
    one, two = early_ref[...].astype(f32), late_ref[...].astype(f32)
    left, right = jnp.where(odd, one, two), jnp.where(odd, two, one)
    base = ext_ref.shape[1] - right_ext.shape[1]
    at = RIM + n_cols - base
    for row in range(half + 2 * RIM):
        left_ext[row] = ext_ref[row, : left_ext.shape[1], :]
        right_ext[row] = ext_ref[row, base:, :]
        left_ext[row, :RIM, :] = left[4 * row : 4 * row + RIM]
        right_ext[row, at : at + RIM, :] = right[4 * row : 4 * row + RIM]

    def put_left(i, start, value):
        conv[i, :STEP, :] = value

    def put_right(i, start, value):
        conv[i, base + start : base + start + STEP, :] = value

    convolve_tile(left_ext, wide, put_left, half, 0)
    for start in range(0, columns - base, STEP):
        convolve_tile(right_ext, wide, put_right, half, start)
    conv[:, STEP:base, :] = conv_ref[:, STEP:base, :]
    w1[...] = jnp.zeros_like(w1)
    w2[...] = jnp.zeros_like(w2)
    w1[:chan, :wide_e] = w1_ref[...]
    w1[chan:, wide_e:] = w1_ref[...]
    w2[:chan, :wide_e] = w2_ref[...]
    w2[chan:, wide_e:] = w2_ref[...]
    dconv_ref[...] = jnp.zeros_like(dconv_ref)

    row_half = lax.broadcasted_iota(jnp.int32, (2 * lanes, lanes), 0) % lanes >= chan
    col_half = lax.broadcasted_iota(jnp.int32, (2 * lanes, lanes), 1) >= chan
    ones = jnp.where(row_half == col_half, 1.0 / chan, 0.0).astype(bf16)
    conv_bias, gain, bias, hidden_bias = (
        jnp.concatenate([ref[...], ref[...]], axis=1)
        for ref in (conv_bias_ref, gain_ref, bias_ref, b1_ref)
    )

    cells_all = half * columns
    out = conv[...].reshape(cells_all, lanes) + conv_bias
    wet = wet_ref[...].reshape(cells_all, lanes)
    center = out - group_mean(out, ones)
    rstd = lax.rsqrt(group_mean(center * center, ones) + ln_eps)
    normed = center * rstd
    zed = (normed * gain + bias).astype(bf16)
    pre = jnp.dot(zed, w1[...], preferred_element_type=f32) + hidden_bias
    dact = jnp.dot(wet, w2[...], preferred_element_type=f32)
    phi = 0.5 + 0.5 * lax.erf(pre * root_half)
    act = (pre * phi).astype(bf16)
    dhid = (dact * (phi + pre * (jnp.exp(-0.5 * pre * pre) * inv_root_tau))).astype(bf16)
    dzed = lax.dot_general(dhid, w1[...], (((1,), (1,)), ((), ())), preferred_element_type=f32)
    rows_first = (((0,), (0,)), ((), ()))
    expand = lax.dot_general(zed, dhid, rows_first, preferred_element_type=f32)
    project = lax.dot_general(wet, act, rows_first, preferred_element_type=f32)
    dnorm = dzed * gain
    mean1 = group_mean(dnorm, ones)
    mean2 = group_mean(dnorm * normed, ones)
    dconv = rstd * (dnorm - mean1 - normed * mean2)
    count = jnp.ones((cells_all, 16), bf16)
    hidden = lax.dot_general(count, dhid, rows_first, preferred_element_type=f32)[:1]
    parts = (wet.astype(f32), dzed * normed, dzed, dconv)
    small = [jnp.sum(part, axis=0, keepdims=True) for part in parts]
    dconv = dconv.reshape(half, columns, lanes)
    conv[...] = dconv
    dconv_ref[:, pl.ds(RIM, columns), :] = dconv

    rows = []
    for block in (expand, project):
        total = block[:chan, :wide_e] + block[chan:, wide_e:]
        rows += [total[:, k * lanes : (k + 1) * lanes] for k in range(wide_e // lanes)]
    total = hidden[:, :wide_e] + hidden[:, wide_e:]
    fine = [total[:, k * lanes : (k + 1) * lanes] for k in range(wide_e // lanes)] + small
    fine.append(jnp.zeros((-len(fine) % 16, lanes), f32))
    rows = jnp.concatenate(rows + fine, axis=0)

    pad = jnp.zeros((edge_ref.shape[0] // (2 * half) - RIM, lanes), f32)
    first = [x for i in range(half) for x in (conv[i, :RIM, :], pad)]
    last = [x for i in range(half) for x in (conv[i, n_cols - RIM : n_cols, :], pad)]
    first = jnp.concatenate(first, axis=0)
    last = jnp.concatenate(last, axis=0)
    edges = [jnp.where(odd, first, last), jnp.where(odd, last, first)]
    edge_ref[...] = jnp.concatenate(edges, axis=0).astype(bf16)
    part = rows.shape[0] // 2
    upper_half = half_ref[0] == 1
    keep_ref[...] = jnp.where(upper_half, rows[part:], rows[:part])
    send_ref[...] = jnp.where(upper_half, rows[:part], rows[part:])


def tap_kernel(columns, ext_ref, left_ext, right_ext, grad_ref, sums_ref):
    half, lanes = grad_ref.shape[0], grad_ref.shape[2]
    base = ext_ref.shape[1] - right_ext.shape[1]

    def tile(total, field_ref, at, start):
        total = list(total)
        grads = [grad_ref[i, pl.ds(start + RIM, 8), :] for i in range(half)]
        for row in range(half + 2 * RIM):
            for b in range(TAPS):
                piece = field_ref[row, pl.ds(at + b, 8), :]
                for i in range(half):
                    a = row - i
                    if 0 <= a < TAPS:
                        total[a * TAPS + b] = total[a * TAPS + b] + grads[i] * piece
        return tuple(total)

    def trip(t, total):
        start = pl.multiple_of(t * 8, 8)
        return tile(total, ext_ref, start, start)

    total = tile((jnp.zeros((8, lanes), f32),) * (TAPS * TAPS), left_ext, 0, 0)
    for at in range(0, columns - base, 8):
        total = tile(total, right_ext, at, base + at)
    total = lax.fori_loop(1, base // 8, trip, total, unroll=2)
    rows = []
    for a in range(TAPS):
        rows += [jnp.sum(total[a * TAPS + b], axis=0, keepdims=True) for b in range(TAPS)]
        rows.append(jnp.zeros((1, lanes), f32))
    sums_ref[...] = jnp.concatenate(rows, axis=0)


def first_kernel(mine_ref, other_ref, taps_ref, edge_ref, send_ref):
    sums = jnp.concatenate([mine_ref[...] + other_ref[...], taps_ref[...]], axis=0)
    send_ref[: sums.shape[0]] = sums.astype(bf16)
    send_ref[sums.shape[0] :] = edge_ref[...]


def add_kernel(total, mine_ref, other_ref, send_ref):
    rim = send_ref.shape[0] - total
    send_ref[:total] = added(mine_ref, other_ref, total).astype(bf16)
    send_ref[total:] = other_ref[other_ref.shape[0] - rim :]


def rows_kernel(
    part, n_cols, lon_ref, lat_ref, early_ref, late_ref, dconv_ref, full_ref, send_ref, later_ref
):
    half = dconv_ref.shape[0]
    odd = lon_ref[0] == 1
    rim = (early_ref.shape[0] - part) // 2
    early = early_ref[part : part + rim].astype(f32)
    late = late_ref[late_ref.shape[0] - rim :].astype(f32)
    right = jnp.where(odd, late, early)
    left = jnp.where(odd, early, late)
    step = rim // half
    for i in range(half):
        full_ref[i] = dconv_ref[i]
        full_ref[i, :RIM, :] = left[i * step : i * step + RIM]
        full_ref[i, RIM + n_cols : 2 * RIM + n_cols, :] = right[i * step : i * step + RIM]
    put_rows(lambda i: full_ref[i], half, lat_ref[0] == 1, send_ref, 0, later_ref)


def rim_rows(lat_ref, pole_ref, early_ref, late_ref, at):
    mid = late_ref.shape[0] // RIM
    odd, pole = lat_ref[0] == 1, pole_ref[0] == 1

    def rows(k):
        early = early_ref[at + k * mid : at + (k + 1) * mid, :].astype(f32)
        late = late_ref[k * mid : (k + 1) * mid, :].astype(f32)
        return early, jnp.where(pole, 0.0, late)

    def top(k):
        early, late = rows(k)
        return jnp.where(odd, early, late)

    def bottom(k):
        early, late = rows(k)
        return jnp.where(odd, late, early)

    return top, bottom


def back_kernel(at, lat_ref, pole_ref, early_ref, late_ref, mid_ref, taps_ref, out_ref, ext32, wide):
    half, columns, chan = out_ref.shape[0] // 2, out_ref.shape[1], out_ref.shape[2]
    assemble(ext32, mid_ref, *rim_rows(lat_ref, pole_ref, early_ref, late_ref, at))
    fill_taps(taps_ref, wide, True)

    def put(i, start, value):
        out_ref[i, pl.ds(start, STEP), :] = value[:, :chan]
        out_ref[half + i, pl.ds(start, STEP), :] = swap(value)[:, :chan]

    convolve(ext32, wide, put, half, columns, 2)


def finish_kernel(
    scale, half_ref, mine_ref, other_ref,
    taps_ref, conv_ref, gain_ref, bias_ref, expand_ref, hidden_ref, project_ref, wet_ref,
):
    lanes = mine_ref.shape[1]
    chan, wide_e = expand_ref.shape
    odd = half_ref[0] == 1
    mine, other = mine_ref[...] * scale, other_ref[...] * scale
    part = mine.shape[0] - 8 * TAPS
    taps = mine[part:] + other[part:]
    taps = taps[:, :chan] + taps[:, chan:]
    mine, other = mine[:part], other[:part]
    total = jnp.concatenate([jnp.where(odd, other, mine), jnp.where(odd, mine, other)], axis=0)
    blocks = wide_e // lanes
    small = total[2 * blocks * chan :]
    for k in range(blocks):
        expand_ref[:, k * lanes : (k + 1) * lanes] = total[k * chan : (k + 1) * chan]
        at = (blocks + k) * chan
        project_ref[:, k * lanes : (k + 1) * lanes] = total[at : at + chan]
        hidden_ref[:, k * lanes : (k + 1) * lanes] = small[k : k + 1]
    narrow = small[:, :chan] + small[:, chan:]
    for k, ref in enumerate((wet_ref, gain_ref, bias_ref, conv_ref)):
        ref[...] = narrow[blocks + k : blocks + k + 1]
    for a in range(TAPS):
        taps_ref[a] = taps[8 * a : 8 * a + TAPS]


def call(kernel, out_shape, scratch, flops, *args):
    vmem = pl.BlockSpec(memory_space=pltpu.VMEM)
    smem = pl.BlockSpec(memory_space=pltpu.SMEM)
    many = isinstance(out_shape, (list, tuple))
    return pl.pallas_call(
        kernel,
        out_shape=out_shape,
        in_specs=[smem if arg.dtype == jnp.int32 and arg.ndim == 1 else vmem for arg in args],
        out_specs=[vmem] * len(out_shape) if many else vmem,
        scratch_shapes=scratch,
        cost_estimate=pl.CostEstimate(flops=flops, bytes_accessed=1 << 20, transcendentals=0),
        compiler_params=pltpu.CompilerParams(vmem_limit_bytes=40 << 20),
    )(*args)


def body(
    state, land_sea, cotangent, kernel, conv_bias, ln_gain, ln_bias, w_expand, b_expand, w_project
):
    n_chan, n_rows, n_cols = state.shape
    n_wide = w_expand.shape[1]
    half = n_rows // 2
    lanes = 2 * n_chan
    columns = -(-n_cols // STEP) * STEP
    padded = -(-(columns + 2 * RIM) // 32) * 32
    total = 2 * n_chan * n_wide // lanes + -(-(n_wide // lanes + 4) // 16) * 16
    part = total // 2
    sums = part + 8 * TAPS
    rim = half * 4
    rows = RIM * padded // 2
    cells = n_rows * n_cols
    conv_flops = cells * n_chan * TAPS * TAPS * 2
    shaped = jax.ShapeDtypeStruct
    row = lambda v: v.reshape(1, -1)
    taps = kernel.transpose(1, 2, 0)
    odd_lon, odd_lat = lax.axis_index("lon") % 2, lax.axis_index("lat") % 2
    place, last_place = lax.axis_index("lat"), lax.axis_size("lat") - 1
    pole = ((place == 0) | (place == last_place)).astype(jnp.int32).reshape(1)
    on_lon, on_lat, keeps = odd_lon.reshape(1), odd_lat.reshape(1), kept_half().reshape(1)

    flat = shaped((rows, lanes), bf16)
    field, first, last = call(
        pack_kernel,
        [shaped((half, padded, lanes), bf16), flat, flat],
        [],
        cells * n_chan,
        on_lat, state.reshape(n_chan * n_rows, n_cols),
    )
    late = lax.ppermute(last, "lat", ring_pairs("lat"))
    early = lax.ppermute(first, "lat", pairs("lat", 1))
    wet = call(
        wet_kernel,
        shaped((half, columns, lanes), bf16),
        [],
        cells * n_chan,
        cotangent.reshape(n_chan * n_rows, n_cols), land_sea,
    )

    late, early, wet = lax.optimization_barrier((late, early, wet))
    side = shaped((4 * (half + 2 * RIM), lanes), bf16)
    last, first = call(
        functools.partial(edge_kernel, n_cols), [side, side], [], cells,
        on_lon, on_lat, pole, field, late, early,
    )
    after = lax.ppermute(last, "lon", ring_pairs("lon"))
    before = lax.ppermute(first, "lon", pairs("lon", 1))
    ext, conv, wide_taps = call(
        inner_kernel,
        [
            shaped((half + 2 * RIM, padded, lanes), f32),
            shaped((half, columns, lanes), f32),
            shaped((TAPS * TAPS, 8, lanes), f32),
        ],
        [],
        conv_flops,
        on_lat, pole, field, early, late, taps,
    )

    dconv, mine, send, edges, left_ext, right_ext = call(
        functools.partial(block_kernel, n_cols),
        [
            shaped((half, padded, lanes), f32),
            shaped((part, lanes), f32),
            shaped((part, lanes), f32),
            shaped((2 * rim, lanes), bf16),
            shaped((half + 2 * RIM, STEP + 8, lanes), f32),
            shaped((half + 2 * RIM, padded - (n_cols - RIM) // STEP * STEP, lanes), f32),
        ],
        [
            pltpu.VMEM((lanes, 2 * n_wide), bf16),
            pltpu.VMEM((lanes, 2 * n_wide), bf16),
            pltpu.VMEM((half, columns, lanes), f32),
        ],
        cells * n_chan * n_wide * 10 + conv_flops,
        on_lon, keeps, after, before, wet, wide_taps, row(conv_bias), row(ln_gain), row(ln_bias),
        w_expand, row(b_expand), w_project.T, ext, conv,
    )

    other = lax.ppermute(send, "lat", pairs("lat", 1))
    tap_total = call(
        functools.partial(tap_kernel, columns),
        shaped((8 * TAPS, lanes), f32),
        [],
        conv_flops,
        ext, left_ext, right_ext, dconv,
    )
    sent = shaped((sums + 2 * rim, lanes), bf16)
    mine = call(first_kernel, sent, [], part * lanes, mine, other, tap_total, edges)
    other = early = lax.ppermute(mine, "lon", pairs("lon", 1))
    add = functools.partial(add_kernel, sums)
    place, size = lax.axis_index("lon"), lax.axis_size("lon")
    apart = place ^ ((place + 2 * odd_lon - 1) % size)
    late = None
    for bit in bits("lon", 1):
        mine = call(add, shaped((sums + rim, lanes), bf16), [], part * lanes, mine, other)
        other = lax.ppermute(mine, "lon", pairs("lon", bit))
        late = other if late is None else jnp.where(apart == 2 * bit - 1, other, late)
    mine = added(mine, other, sums)
    row_shape = shaped((rows, lanes), bf16)
    full, first, last = call(
        functools.partial(rows_kernel, sums, n_cols),
        [shaped(dconv.shape, f32), row_shape, row_shape],
        [],
        cells * n_chan,
        on_lon, on_lat, early, late, dconv,
    )
    early = lax.ppermute(first, "lat", pairs("lat", 1))
    late = lax.ppermute(last, "lat", ring_pairs("lat"))
    for k, swaps in enumerate(half_rounds()):
        mine = mine + lax.ppermute(mine, "lat", swaps)
        if k == 0:
            late, _ = lax.optimization_barrier((late, mine))
    other = lax.ppermute(mine, "lat", pairs("lat", 1))

    grad = call(
        functools.partial(back_kernel, 0),
        shaped((n_rows, columns, n_chan), f32),
        [
            pltpu.VMEM((half + 2 * RIM, padded, lanes), f32),
            pltpu.VMEM((TAPS * TAPS, 8, lanes), f32),
        ],
        conv_flops,
        on_lat, pole, early, late, full, taps,
    )
    grad = grad[:, :n_cols].transpose(2, 0, 1)
    state_grad = (cotangent.astype(f32) + grad).astype(bf16)

    scale = 1.0 / math.sqrt(cells * lax.axis_size("lat") * lax.axis_size("lon"))
    narrow = shaped((1, n_chan), f32)
    out = call(
        functools.partial(finish_kernel, scale),
        [
            shaped((TAPS, TAPS, n_chan), f32),
            narrow,
            narrow,
            narrow,
            shaped((n_chan, n_wide), f32),
            shaped((1, n_wide), f32),
            shaped((n_chan, n_wide), f32),
            narrow,
        ],
        [],
        total * lanes,
        keeps, mine, other,
    )
    return (
        state_grad,
        out[0].transpose(2, 0, 1),
        out[1].reshape(-1),
        out[2].reshape(-1),
        out[3].reshape(-1),
        out[4],
        out[5].reshape(-1),
        out[6].T,
        out[7].reshape(-1),
    )


def solution(mesh):
    in_specs = (
        P(None, "lat", "lon"),
        P("lat", "lon"),
        P(None, "lat", "lon"),
        P(),
        P(),
        P(),
        P(),
        P(),
        P(),
        P(),
    )
    out_specs = (P(None, "lat", "lon"), P(), P(), P(), P(), P(), P(), P(), P())
    return jax.shard_map(body, mesh=mesh, in_specs=in_specs, out_specs=out_specs, check_vma=False)
```

```python
import functools
import math

import jax
import jax.numpy as jnp
from jax import lax
from jax.experimental import pallas as pl
from jax.experimental.pallas import tpu as pltpu
from jax.sharding import PartitionSpec as P

TAPS = 7
RIM = 3
STEP = 16

ln_eps = 1e-06
root_half = 0.7071067811865476
inv_root_tau = 0.3989422804014327
f32 = jnp.float32
bf16 = jnp.bfloat16


def pairs(axis, bit):
    return [(i, i ^ bit) for i in range(lax.axis_size(axis))]


def ring_pairs(axis):
    size = lax.axis_size(axis)
    return [(i, (i + 1 if i % 2 else i - 1) % size) for i in range(size)]


def bits(axis, first):
    size = lax.axis_size(axis)
    if size < 4 or size & (size - 1):
        raise ValueError("axis size")
    return [1 << k for k in range(first, size.bit_length() - 1)]


def kept_half():
    place = lax.axis_index("lat")
    return sum(place // bit for bit in [1] + bits("lat", 1)) % 2


def half_rounds():
    steps = bits("lat", 1)
    turned = steps[1:] + steps[:1]
    size = lax.axis_size("lat")
    order = [turned if bin(i).count("1") % 2 else steps for i in range(size)]
    return [[(i, i ^ order[i][k] ^ 1) for i in range(size)] for k in range(len(steps))]


def unpack(field):
    chan = field.shape[2] // 2
    return jnp.concatenate([field[:, :, :chan], field[:, :, chan:]], axis=0)


def swap(value):
    return pltpu.roll(value, value.shape[-1] // 2, value.ndim - 1)


def assemble(ext_ref, mid_ref, top, bottom):
    half, columns, lanes = mid_ref.shape
    first = lax.broadcasted_iota(jnp.int32, (columns, lanes), 1) < lanes // 2
    for k in range(RIM):
        above, below = top(k), bottom(k)
        above = jnp.concatenate([above, swap(above)], axis=0)
        below = jnp.concatenate([swap(below), below], axis=0)
        upper = swap(mid_ref[half - RIM + k].astype(f32))
        lower = swap(mid_ref[k].astype(f32))
        ext_ref[k] = jnp.where(first, above, upper)
        ext_ref[half + RIM + k] = jnp.where(first, lower, below)
    for i in range(half):
        ext_ref[RIM + i] = mid_ref[i].astype(f32)


def added(mine_ref, other_ref, total):
    return mine_ref[:total].astype(f32) + other_ref[:total].astype(f32)


def fill_taps(taps_ref, wide_ref, flip):
    chan = taps_ref.shape[2]
    for a in range(TAPS):
        for b in range(TAPS):
            row = taps_ref[TAPS - 1 - a, TAPS - 1 - b, :] if flip else taps_ref[a, b, :]
            row = row.reshape(1, chan)
            row = jnp.concatenate([row, row], axis=1)
            wide_ref[a * TAPS + b] = jnp.broadcast_to(row, (8, 2 * chan))


def convolve_tile(ext_ref, wide_ref, store, half, start):
    tiles = STEP // 8
    total = [[None] * tiles for _ in range(half)]
    for row in range(half + 2 * RIM):
        for b in range(TAPS):
            piece = [ext_ref[row, pl.ds(start + b + 8 * s, 8), :] for s in range(tiles)]
            for i in range(half):
                a = row - i
                if 0 <= a < TAPS:
                    weight = wide_ref[a * TAPS + b]
                    for s in range(tiles):
                        term = weight * piece[s]
                        total[i][s] = term if total[i][s] is None else total[i][s] + term
    for i in range(half):
        store(i, start, jnp.concatenate(total[i], axis=0))


def convolve(ext_ref, wide_ref, store, half, columns, unroll):
    def trip(t, carry):
        convolve_tile(ext_ref, wide_ref, store, half, pl.multiple_of(t * STEP, STEP))
        return carry

    lax.fori_loop(0, columns // STEP, trip, 0, unroll=unroll)


def group_mean(values, ones):
    high = values.astype(bf16)
    low = (values - high.astype(f32)).astype(bf16)
    return jnp.dot(jnp.concatenate([high, low], axis=1), ones, preferred_element_type=f32)


def put_rows(packed, half, odd, send_ref, at, later_ref):
    wide, lanes = packed(0).shape
    mid = wide // 2
    first = lax.broadcasted_iota(jnp.int32, (mid, lanes), 1) < lanes // 2
    for k in range(RIM):
        upper, lower = packed(k), packed(half - RIM + k)
        upper = jnp.where(first, upper[:mid], swap(upper[mid:]))
        lower = jnp.where(first, swap(lower[:mid]), lower[mid:])
        send_ref[at + k * mid : at + (k + 1) * mid, :] = jnp.where(odd, upper, lower).astype(bf16)
        later_ref[k * mid : (k + 1) * mid, :] = jnp.where(odd, lower, upper).astype(bf16)


def packed_rows(field, half, lanes):
    count = field.shape[0]
    shape = (count // (2 * half), 2 * half, lanes)
    chan = lax.broadcasted_iota(jnp.int32, shape, 0)
    row = lax.broadcasted_iota(jnp.int32, shape, 1)
    lane = lax.broadcasted_iota(jnp.int32, shape, 2)
    lower = row >= half
    row = jnp.where(lower, row - half, row)
    here = lane == jnp.where(lower, chan + lanes // 2, chan)
    packed = []
    for i in range(half):
        pick = jnp.where(here & (row == i), 1.0, 0.0).reshape(count, lanes).astype(bf16)
        packed.append(
            lax.dot_general(field, pick, (((0,), (0,)), ((), ())), preferred_element_type=f32)
        )
    return packed


def pack_kernel(lat_ref, state_ref, mid_ref, send_ref, later_ref):
    half, wide, lanes = mid_ref.shape
    n_cols = state_ref.shape[1]
    fields = []
    for i, field in enumerate(packed_rows(state_ref[...], half, lanes)):
        before = jnp.zeros((RIM, lanes), f32)
        after = jnp.zeros((wide - RIM - n_cols, lanes), f32)
        fields.append(jnp.concatenate([before, field, after], axis=0))
        mid_ref[i] = fields[i].astype(bf16)
    put_rows(lambda i: fields[i], half, lat_ref[0] == 1, send_ref, 0, later_ref)


def wet_kernel(cot_ref, sea_ref, wet_ref):
    half, columns, lanes = wet_ref.shape
    n_rows, n_cols = sea_ref.shape
    cot = cot_ref[...].astype(f32).reshape(-1, n_rows, n_cols) * sea_ref[...].astype(f32)
    cot = cot.reshape(-1, n_cols).astype(bf16)
    for i, field in enumerate(packed_rows(cot, half, lanes)):
        after = jnp.zeros((columns - n_cols, lanes), f32)
        wet_ref[i] = jnp.concatenate([field, after], axis=0).astype(bf16)


def edge_kernel(n_cols, lon_ref, lat_ref, pole_ref, mid_ref, late_ref, early_ref, later_ref, send_ref):
    half, wide, lanes = mid_ref.shape
    mid = wide // 2
    odd_lat, odd_lon, pole = lat_ref[0] == 1, lon_ref[0] == 1, pole_ref[0] == 1
    base = n_cols // 16 * 16
    skip = n_cols - base
    first = lax.broadcasted_iota(jnp.int32, (8, lanes), 1) < lanes // 2
    left, right = [], []
    for i in range(half):
        left.append(mid_ref[i, :16, :].astype(f32)[:8])
        right.append(mid_ref[i, base : base + 32, :].astype(f32)[skip : skip + 8])
    ends = [([], []), ([], [])]
    for k in range(RIM):
        at = k * mid
        one, two = [], []
        for ref in (early_ref, late_ref):
            one.append(ref[at : at + 16, :].astype(f32)[:8])
            two.append(ref[at + base - mid : at + mid, :].astype(f32)[skip : skip + 8])
        one[1], two[1] = jnp.where(pole, 0.0, one[1]), jnp.where(pole, 0.0, two[1])
        above = jnp.where(odd_lat, one[0], one[1]), jnp.where(odd_lat, two[0], two[1])
        below = jnp.where(odd_lat, one[1], one[0]), jnp.where(odd_lat, two[1], two[0])
        ends[0][0].append(jnp.where(first, above[0], swap(left[half - RIM + k])))
        ends[0][1].append(jnp.where(first, swap(above[1]), swap(right[half - RIM + k])))
        ends[1][0].append(jnp.where(first, swap(left[k]), swap(below[0])))
        ends[1][1].append(jnp.where(first, swap(right[k]), below[1]))
    left = ends[0][0] + left + ends[1][0]
    right = ends[0][1] + right + ends[1][1]
    left = jnp.concatenate([x[RIM : RIM + 4] for x in left], axis=0)
    right = jnp.concatenate([x[:4] for x in right], axis=0)
    send_ref[...] = jnp.where(odd_lon, left, right).astype(bf16)
    later_ref[...] = jnp.where(odd_lon, right, left).astype(bf16)


def inner_kernel(lat_ref, pole_ref, mid_ref, early_ref, late_ref, taps_ref, ext_ref, conv_ref, wide_ref):
    half, columns, lanes = conv_ref.shape
    assemble(ext_ref, mid_ref, *rim_rows(lat_ref, pole_ref, early_ref, late_ref, 0))
    fill_taps(taps_ref, wide_ref, False)

    def put(i, start, value):
        conv_ref[i, pl.ds(start, STEP), :] = value

    convolve(ext_ref, wide_ref, put, half, columns, 2)


def block_kernel(
    n_cols, lon_ref, half_ref, late_ref, early_ref, wet_ref, wide,
    conv_bias_ref, gain_ref, bias_ref, w1_ref, b1_ref, w2_ref, ext_ref, conv_ref,
    dconv_ref, keep_ref, send_ref, edge_ref, left_ext, right_ext, w1, w2, conv,
):
    half, columns, lanes = wet_ref.shape
    chan = lanes // 2
    wide_e = w1_ref.shape[1]
    odd = lon_ref[0] == 1
    one, two = early_ref[...].astype(f32), late_ref[...].astype(f32)
    left, right = jnp.where(odd, one, two), jnp.where(odd, two, one)
    base = ext_ref.shape[1] - right_ext.shape[1]
    at = RIM + n_cols - base
    for row in range(half + 2 * RIM):
        left_ext[row] = ext_ref[row, : left_ext.shape[1], :]
        right_ext[row] = ext_ref[row, base:, :]
        left_ext[row, :RIM, :] = left[4 * row : 4 * row + RIM]
        right_ext[row, at : at + RIM, :] = right[4 * row : 4 * row + RIM]

    def put_left(i, start, value):
        conv[i, :STEP, :] = value

    def put_right(i, start, value):
        conv[i, base + start : base + start + STEP, :] = value

    convolve_tile(left_ext, wide, put_left, half, 0)
    for start in range(0, columns - base, STEP):
        convolve_tile(right_ext, wide, put_right, half, start)
    conv[:, STEP:base, :] = conv_ref[:, STEP:base, :]
    w1[...] = jnp.zeros_like(w1)
    w2[...] = jnp.zeros_like(w2)
    w1[:chan, :wide_e] = w1_ref[...]
    w1[chan:, wide_e:] = w1_ref[...]
    w2[:chan, :wide_e] = w2_ref[...]
    w2[chan:, wide_e:] = w2_ref[...]
    dconv_ref[...] = jnp.zeros_like(dconv_ref)

    row_half = lax.broadcasted_iota(jnp.int32, (2 * lanes, lanes), 0) % lanes >= chan
    col_half = lax.broadcasted_iota(jnp.int32, (2 * lanes, lanes), 1) >= chan
    ones = jnp.where(row_half == col_half, 1.0 / chan, 0.0).astype(bf16)
    conv_bias, gain, bias, hidden_bias = (
        jnp.concatenate([ref[...], ref[...]], axis=1)
        for ref in (conv_bias_ref, gain_ref, bias_ref, b1_ref)
    )

    cells_all = half * columns
    out = conv[...].reshape(cells_all, lanes) + conv_bias
    wet = wet_ref[...].reshape(cells_all, lanes)
    center = out - group_mean(out, ones)
    rstd = lax.rsqrt(group_mean(center * center, ones) + ln_eps)
    normed = center * rstd
    zed = (normed * gain + bias).astype(bf16)
    pre = jnp.dot(zed, w1[...], preferred_element_type=f32) + hidden_bias
    dact = jnp.dot(wet, w2[...], preferred_element_type=f32)
    phi = 0.5 + 0.5 * lax.erf(pre * root_half)
    act = (pre * phi).astype(bf16)
    dhid = (dact * (phi + pre * (jnp.exp(-0.5 * pre * pre) * inv_root_tau))).astype(bf16)
    dzed = lax.dot_general(dhid, w1[...], (((1,), (1,)), ((), ())), preferred_element_type=f32)
    rows_first = (((0,), (0,)), ((), ()))
    expand = lax.dot_general(zed, dhid, rows_first, preferred_element_type=f32)
    project = lax.dot_general(wet, act, rows_first, preferred_element_type=f32)
    dnorm = dzed * gain
    mean1 = group_mean(dnorm, ones)
    mean2 = group_mean(dnorm * normed, ones)
    dconv = rstd * (dnorm - mean1 - normed * mean2)
    count = jnp.ones((cells_all, 16), bf16)
    hidden = lax.dot_general(count, dhid, rows_first, preferred_element_type=f32)[:1]
    parts = (wet.astype(f32), dzed * normed, dzed, dconv)
    small = [jnp.sum(part, axis=0, keepdims=True) for part in parts]
    dconv = dconv.reshape(half, columns, lanes)
    conv[...] = dconv
    dconv_ref[:, pl.ds(RIM, columns), :] = dconv

    rows = []
    for block in (expand, project):
        total = block[:chan, :wide_e] + block[chan:, wide_e:]
        rows += [total[:, k * lanes : (k + 1) * lanes] for k in range(wide_e // lanes)]
    total = hidden[:, :wide_e] + hidden[:, wide_e:]
    fine = [total[:, k * lanes : (k + 1) * lanes] for k in range(wide_e // lanes)] + small
    fine.append(jnp.zeros((-len(fine) % 16, lanes), f32))
    rows = jnp.concatenate(rows + fine, axis=0)

    pad = jnp.zeros((edge_ref.shape[0] // (2 * half) - RIM, lanes), f32)
    first = [x for i in range(half) for x in (conv[i, :RIM, :], pad)]
    last = [x for i in range(half) for x in (conv[i, n_cols - RIM : n_cols, :], pad)]
    first = jnp.concatenate(first, axis=0)
    last = jnp.concatenate(last, axis=0)
    edges = [jnp.where(odd, first, last), jnp.where(odd, last, first)]
    edge_ref[...] = jnp.concatenate(edges, axis=0).astype(bf16)
    part = rows.shape[0] // 2
    upper_half = half_ref[0] == 1
    keep_ref[...] = jnp.where(upper_half, rows[part:], rows[:part])
    send_ref[...] = jnp.where(upper_half, rows[:part], rows[part:])


def tap_kernel(columns, ext_ref, left_ext, right_ext, grad_ref, sums_ref):
    half, lanes = grad_ref.shape[0], grad_ref.shape[2]
    base = ext_ref.shape[1] - right_ext.shape[1]

    def tile(total, field_ref, at, start):
        total = list(total)
        grads = [grad_ref[i, pl.ds(start + RIM, 8), :] for i in range(half)]
        for row in range(half + 2 * RIM):
            for b in range(TAPS):
                piece = field_ref[row, pl.ds(at + b, 8), :]
                for i in range(half):
                    a = row - i
                    if 0 <= a < TAPS:
                        total[a * TAPS + b] = total[a * TAPS + b] + grads[i] * piece
        return tuple(total)

    def trip(t, total):
        start = pl.multiple_of(t * 8, 8)
        return tile(total, ext_ref, start, start)

    total = tile((jnp.zeros((8, lanes), f32),) * (TAPS * TAPS), left_ext, 0, 0)
    for at in range(0, columns - base, 8):
        total = tile(total, right_ext, at, base + at)
    total = lax.fori_loop(1, base // 8, trip, total, unroll=2)
    rows = []
    for a in range(TAPS):
        rows += [jnp.sum(total[a * TAPS + b], axis=0, keepdims=True) for b in range(TAPS)]
        rows.append(jnp.zeros((1, lanes), f32))
    sums_ref[...] = jnp.concatenate(rows, axis=0)


def first_kernel(mine_ref, other_ref, taps_ref, edge_ref, send_ref):
    sums = jnp.concatenate([mine_ref[...] + other_ref[...], taps_ref[...]], axis=0)
    send_ref[: sums.shape[0]] = sums.astype(bf16)
    send_ref[sums.shape[0] :] = edge_ref[...]


def add_kernel(total, mine_ref, other_ref, send_ref):
    rim = send_ref.shape[0] - total
    send_ref[:total] = added(mine_ref, other_ref, total).astype(bf16)
    send_ref[total:] = other_ref[other_ref.shape[0] - rim :]


def rows_kernel(
    part, n_cols, lon_ref, lat_ref, early_ref, late_ref, dconv_ref, full_ref, send_ref, later_ref
):
    half = dconv_ref.shape[0]
    odd = lon_ref[0] == 1
    rim = (early_ref.shape[0] - part) // 2
    early = early_ref[part : part + rim].astype(f32)
    late = late_ref[late_ref.shape[0] - rim :].astype(f32)
    right = jnp.where(odd, late, early)
    left = jnp.where(odd, early, late)
    step = rim // half
    for i in range(half):
        full_ref[i] = dconv_ref[i]
        full_ref[i, :RIM, :] = left[i * step : i * step + RIM]
        full_ref[i, RIM + n_cols : 2 * RIM + n_cols, :] = right[i * step : i * step + RIM]
    put_rows(lambda i: full_ref[i], half, lat_ref[0] == 1, send_ref, 0, later_ref)


def rim_rows(lat_ref, pole_ref, early_ref, late_ref, at):
    mid = late_ref.shape[0] // RIM
    odd, pole = lat_ref[0] == 1, pole_ref[0] == 1

    def rows(k):
        early = early_ref[at + k * mid : at + (k + 1) * mid, :].astype(f32)
        late = late_ref[k * mid : (k + 1) * mid, :].astype(f32)
        return early, jnp.where(pole, 0.0, late)

    def top(k):
        early, late = rows(k)
        return jnp.where(odd, early, late)

    def bottom(k):
        early, late = rows(k)
        return jnp.where(odd, late, early)

    return top, bottom


def back_kernel(at, lat_ref, pole_ref, early_ref, late_ref, mid_ref, taps_ref, out_ref, ext32, wide):
    half, columns, lanes = out_ref.shape
    assemble(ext32, mid_ref, *rim_rows(lat_ref, pole_ref, early_ref, late_ref, at))
    fill_taps(taps_ref, wide, True)

    def put(i, start, value):
        out_ref[i, pl.ds(start, STEP), :] = value

    convolve(ext32, wide, put, half, columns, 2)


def finish_kernel(
    scale, half_ref, mine_ref, other_ref,
    taps_ref, conv_ref, gain_ref, bias_ref, expand_ref, hidden_ref, project_ref, wet_ref,
):
    lanes = mine_ref.shape[1]
    chan, wide_e = expand_ref.shape
    odd = half_ref[0] == 1
    mine, other = mine_ref[...] * scale, other_ref[...] * scale
    part = mine.shape[0] - 8 * TAPS
    taps = mine[part:] + other[part:]
    taps = taps[:, :chan] + taps[:, chan:]
    mine, other = mine[:part], other[:part]
    total = jnp.concatenate([jnp.where(odd, other, mine), jnp.where(odd, mine, other)], axis=0)
    blocks = wide_e // lanes
    small = total[2 * blocks * chan :]
    for k in range(blocks):
        expand_ref[:, k * lanes : (k + 1) * lanes] = total[k * chan : (k + 1) * chan]
        at = (blocks + k) * chan
        project_ref[:, k * lanes : (k + 1) * lanes] = total[at : at + chan]
        hidden_ref[:, k * lanes : (k + 1) * lanes] = small[k : k + 1]
    narrow = small[:, :chan] + small[:, chan:]
    for k, ref in enumerate((wet_ref, gain_ref, bias_ref, conv_ref)):
        ref[...] = narrow[blocks + k : blocks + k + 1]
    for a in range(TAPS):
        taps_ref[a] = taps[8 * a : 8 * a + TAPS]


def call(kernel, out_shape, scratch, flops, *args):
    vmem = pl.BlockSpec(memory_space=pltpu.VMEM)
    smem = pl.BlockSpec(memory_space=pltpu.SMEM)
    many = isinstance(out_shape, (list, tuple))
    return pl.pallas_call(
        kernel,
        out_shape=out_shape,
        in_specs=[smem if arg.dtype == jnp.int32 and arg.ndim == 1 else vmem for arg in args],
        out_specs=[vmem] * len(out_shape) if many else vmem,
        scratch_shapes=scratch,
        cost_estimate=pl.CostEstimate(flops=flops, bytes_accessed=1 << 20, transcendentals=0),
        compiler_params=pltpu.CompilerParams(vmem_limit_bytes=40 << 20),
    )(*args)


def body(
    state, land_sea, cotangent, kernel, conv_bias, ln_gain, ln_bias, w_expand, b_expand, w_project
):
    n_chan, n_rows, n_cols = state.shape
    n_wide = w_expand.shape[1]
    half = n_rows // 2
    lanes = 2 * n_chan
    columns = -(-n_cols // STEP) * STEP
    padded = -(-(columns + 2 * RIM) // 32) * 32
    total = 2 * n_chan * n_wide // lanes + -(-(n_wide // lanes + 4) // 16) * 16
    part = total // 2
    sums = part + 8 * TAPS
    rim = half * 4
    rows = RIM * padded // 2
    cells = n_rows * n_cols
    conv_flops = cells * n_chan * TAPS * TAPS * 2
    shaped = jax.ShapeDtypeStruct
    row = lambda v: v.reshape(1, -1)
    taps = kernel.transpose(1, 2, 0)
    odd_lon, odd_lat = lax.axis_index("lon") % 2, lax.axis_index("lat") % 2
    place, last_place = lax.axis_index("lat"), lax.axis_size("lat") - 1
    pole = ((place == 0) | (place == last_place)).astype(jnp.int32).reshape(1)
    on_lon, on_lat, keeps = odd_lon.reshape(1), odd_lat.reshape(1), kept_half().reshape(1)

    flat = shaped((rows, lanes), bf16)
    field, first, last = call(
        pack_kernel,
        [shaped((half, padded, lanes), bf16), flat, flat],
        [],
        cells * n_chan,
        on_lat, state.reshape(n_chan * n_rows, n_cols),
    )
    late = lax.ppermute(last, "lat", ring_pairs("lat"))
    early = lax.ppermute(first, "lat", pairs("lat", 1))
    wet = call(
        wet_kernel,
        shaped((half, columns, lanes), bf16),
        [],
        cells * n_chan,
        cotangent.reshape(n_chan * n_rows, n_cols), land_sea,
    )

    late, early, wet = lax.optimization_barrier((late, early, wet))
    side = shaped((4 * (half + 2 * RIM), lanes), bf16)
    last, first = call(
        functools.partial(edge_kernel, n_cols), [side, side], [], cells,
        on_lon, on_lat, pole, field, late, early,
    )
    after = lax.ppermute(last, "lon", ring_pairs("lon"))
    before = lax.ppermute(first, "lon", pairs("lon", 1))
    ext, conv, wide_taps = call(
        inner_kernel,
        [
            shaped((half + 2 * RIM, padded, lanes), f32),
            shaped((half, columns, lanes), f32),
            shaped((TAPS * TAPS, 8, lanes), f32),
        ],
        [],
        conv_flops,
        on_lat, pole, field, early, late, taps,
    )

    dconv, mine, send, edges, left_ext, right_ext = call(
        functools.partial(block_kernel, n_cols),
        [
            shaped((half, padded, lanes), f32),
            shaped((part, lanes), f32),
            shaped((part, lanes), f32),
            shaped((2 * rim, lanes), bf16),
            shaped((half + 2 * RIM, STEP + 8, lanes), f32),
            shaped((half + 2 * RIM, padded - (n_cols - RIM) // STEP * STEP, lanes), f32),
        ],
        [
            pltpu.VMEM((lanes, 2 * n_wide), bf16),
            pltpu.VMEM((lanes, 2 * n_wide), bf16),
            pltpu.VMEM((half, columns, lanes), f32),
        ],
        cells * n_chan * n_wide * 10 + conv_flops,
        on_lon, keeps, after, before, wet, wide_taps, row(conv_bias), row(ln_gain), row(ln_bias),
        w_expand, row(b_expand), w_project.T, ext, conv,
    )

    other = lax.ppermute(send, "lat", pairs("lat", 1))
    tap_total = call(
        functools.partial(tap_kernel, columns),
        shaped((8 * TAPS, lanes), f32),
        [],
        conv_flops,
        ext, left_ext, right_ext, dconv,
    )
    sent = shaped((sums + 2 * rim, lanes), bf16)
    mine = call(first_kernel, sent, [], part * lanes, mine, other, tap_total, edges)
    other = early = lax.ppermute(mine, "lon", pairs("lon", 1))
    add = functools.partial(add_kernel, sums)
    place, size = lax.axis_index("lon"), lax.axis_size("lon")
    apart = place ^ ((place + 2 * odd_lon - 1) % size)
    late = None
    for bit in bits("lon", 1):
        mine = call(add, shaped((sums + rim, lanes), bf16), [], part * lanes, mine, other)
        other = lax.ppermute(mine, "lon", pairs("lon", bit))
        late = other if late is None else jnp.where(apart == 2 * bit - 1, other, late)
    mine = added(mine, other, sums)
    row_shape = shaped((rows, lanes), bf16)
    full, first, last = call(
        functools.partial(rows_kernel, sums, n_cols),
        [shaped(dconv.shape, f32), row_shape, row_shape],
        [],
        cells * n_chan,
        on_lon, on_lat, early, late, dconv,
    )
    early = lax.ppermute(first, "lat", pairs("lat", 1))
    late = lax.ppermute(last, "lat", ring_pairs("lat"))
    for k, swaps in enumerate(half_rounds()):
        mine = mine + lax.ppermute(mine, "lat", swaps)
        if k == 0:
            late, _ = lax.optimization_barrier((late, mine))
    other = lax.ppermute(mine, "lat", pairs("lat", 1))

    grad = call(
        functools.partial(back_kernel, 0),
        shaped((half, columns, lanes), f32),
        [
            pltpu.VMEM((half + 2 * RIM, padded, lanes), f32),
            pltpu.VMEM((TAPS * TAPS, 8, lanes), f32),
        ],
        conv_flops,
        on_lat, pole, early, late, full, taps,
    )
    grad = unpack(grad)[:, :n_cols].transpose(2, 0, 1)
    state_grad = (cotangent.astype(f32) + grad).astype(bf16)

    scale = 1.0 / math.sqrt(cells * lax.axis_size("lat") * lax.axis_size("lon"))
    narrow = shaped((1, n_chan), f32)
    out = call(
        functools.partial(finish_kernel, scale),
        [
            shaped((TAPS, TAPS, n_chan), f32),
            narrow,
            narrow,
            narrow,
            shaped((n_chan, n_wide), f32),
            shaped((1, n_wide), f32),
            shaped((n_chan, n_wide), f32),
            narrow,
        ],
        [],
        total * lanes,
        keeps, mine, other,
    )
    return (
        state_grad,
        out[0].transpose(2, 0, 1),
        out[1].reshape(-1),
        out[2].reshape(-1),
        out[3].reshape(-1),
        out[4],
        out[5].reshape(-1),
        out[6].T,
        out[7].reshape(-1),
    )


def solution(mesh):
    in_specs = (
        P(None, "lat", "lon"),
        P("lat", "lon"),
        P(None, "lat", "lon"),
        P(),
        P(),
        P(),
        P(),
        P(),
        P(),
        P(),
    )
    out_specs = (P(None, "lat", "lon"), P(), P(), P(), P(), P(), P(), P(), P())
    return jax.shard_map(body, mesh=mesh, in_specs=in_specs, out_specs=out_specs, check_vma=False)
```
